32 devices in a mesh: dp: 4 (over x, core), mp: 8 (over z, y).
Axes of the slice: x: 2, y: 2, z: 4, core: 2. Of those that a mesh axis runs over, the one named last changes fastest.
Arguments:
- hidden: bfloat16 [2048, 5120], P('dp', 'mp'), may hold values from -6 to 6
- mod_table: bfloat16 [50, 2, 5120], P(None, None, 'mp'), may hold values from -3 to 3
- timestep: int32 [4], P('dp'), may hold values from 0 to 49
- head_weight: bfloat16 [5120, 64], P('mp'), may hold values from -0.078125 to 0.078125
- conv_in: bfloat16 [16, 27, 384], replicated, may hold values from -0.3125 to 0.3125
- conv_mid: bfloat16 [384, 27, 384], P('dp'), may hold values from -0.0625 to 0.0625
- patch_weight: bfloat16 [384, 1024], replicated, may hold values from -0.3125 to 0.3125
- text_emb: float32 [4, 1024], P('dp'), may hold values from -6 to 6
Outputs:
- reward: float32 [4], P('dp')
- head_grad: float32 [5120, 64], P('mp')
- hidden_grad: bfloat16 [2048, 5120], P('dp', 'mp')
The draws below stay inside these ranges and needn't reach their ends.
Inputs may be any that keep to these rules, and one draw needn't show every extreme that they name: One timestep index a video.
All inputs are finite; a program needn't handle non-finite values.
Results may differ from the reference program's by a relative error of at most 0.029.
Values may be sent and summed in bfloat16 or wider, within the bound.
No kernel may reach another device: no remote copies, remote signals or barrier semaphores. Data moves between devices by JAX's collectives and lax.ppermute only.
A program may use at most 64 MiB of HBM per device.

```python
import jax
import jax.numpy as jnp
from jax import lax

D = 5120
C = 16
CH = 384
EMB = 1024
NSTEPS = 50
LW = 64
LT = 2
LH = 16
VIDEOS = 4
S = 512
TOKENS = 2048


def with_ends(array, rng, smallest, largest):
    longest = array.shape.index(max(array.shape))
    spots = []
    for shift in (0, 1):
        where = [jax.random.randint(jax.random.fold_in(rng, axis), (), 0, length) for axis, length in enumerate(array.shape)]
        where[longest] = (where[longest] + shift) % array.shape[longest]
        spots.append(tuple(where))
    return array.at[spots[0]].set(smallest).at[spots[1]].set(largest)


def steps_of(rng, shape, split, smallest, high):
    def one(position, blocks):
        steps = jax.random.uniform(jax.random.fold_in(jax.random.fold_in(rng, 6), position), (blocks,), jnp.float32, smallest / len(split), high / len(split))
        return jnp.repeat(jnp.exp(steps), shape[position] // blocks).reshape((-1,) + (1,) * (len(shape) - position - 1))

    level = one(*split[0])
    for cut in split[1:]:
        level = level * one(*cut)
    return level


def bell_draw(rng, dims, spread, most, split=(), kind=jnp.bfloat16):
    level = steps_of(rng, dims, split, -0.22, 0.18) if split else 1.0
    array = jax.random.normal(rng, dims, jnp.float32) * spread * level
    return jnp.minimum(jnp.maximum(array, -most), most).astype(kind)


def setup_inputs(seed: int = 0) -> dict:
    arg_keys = jax.random.split(jax.random.key(seed), 9)
    return {
        "hidden": bell_draw(arg_keys[0], (TOKENS, D), 1.0, 6.0, ((0, 4), (1, 8))),
        "mod_table": bell_draw(arg_keys[1], (NSTEPS, 2, D), 0.5, 3.0, ((2, 8),)),
        "timestep": with_ends(jax.random.randint(arg_keys[2], (VIDEOS,), 0, NSTEPS), jax.random.fold_in(arg_keys[2], 1), 0, NSTEPS - 1).astype(jnp.int32),
        "head_weight": bell_draw(arg_keys[3], (D, 4 * C), D ** -0.5, 0.078125, ((0, 8),)),
        "conv_in": bell_draw(arg_keys[4], (C, 27, CH), (27 * C) ** -0.5, 0.3125),
        "conv_mid": bell_draw(arg_keys[5], (CH, 27, CH), (27 * CH) ** -0.5, 0.0625, ((0, 4),)),
        "patch_weight": bell_draw(arg_keys[6], (CH, EMB), CH ** -0.5, 0.3125),
        "text_emb": bell_draw(arg_keys[7], (VIDEOS, EMB), 1.0, 6.0, ((0, 4),), jnp.float32),
    }


def silu_slope(value):
    gate = jax.nn.sigmoid(value)
    return gate * (1.0 + value * (1.0 - gate))

def scoring(pooled, video_text, patch_weight):
    embedded = jnp.dot(pooled, patch_weight.astype(jnp.float32), precision=lax.Precision.HIGHEST)
    embed_length = jnp.sqrt(lax.optimization_barrier(jnp.sum(embedded * embedded, axis=1)) + 1e-06)
    text_length = jnp.sqrt(jnp.sum(video_text * video_text) + 1e-06)
    cosine = jnp.dot(embedded, video_text, precision=lax.Precision.HIGHEST) / (embed_length * text_length)
    return 100.0 * jnp.mean(cosine)

def conv_apply(field, weight, reverse_time):
    time_pad = (0, 2) if reverse_time else (2, 0)
    padded = jnp.pad(field, (time_pad, (1, 1), (1, 1), (0, 0)))
    frames, rows, cols = (field.shape[0], field.shape[1], field.shape[2])
    width_out = weight.shape[0] if reverse_time else weight.shape[2]
    summed = jnp.zeros((frames, rows, cols, width_out), jnp.float32)
    for tap_index in range(27):
        step_time, step_rows, step_cols = (tap_index // 9, tap_index // 3 % 3, tap_index % 3)
        view = padded[step_time:step_time + frames, step_rows:step_rows + rows, step_cols:step_cols + cols].astype(jnp.float32)
        if reverse_time:
            summed = summed + jnp.einsum('thwo,io->thwi', view, weight[:, 26 - tap_index, :].astype(jnp.float32), precision=lax.Precision.HIGHEST)
        else:
            summed = summed + jnp.einsum('thwi,io->thwo', view, weight[:, tap_index, :].astype(jnp.float32), precision=lax.Precision.HIGHEST)
    return summed

def reference(hidden, mod_table, timestep, head_weight, conv_in, conv_mid, patch_weight, text_emb):
    per_video = hidden.reshape(VIDEOS, S, D)

    def one_video(packed):
        video_hidden, step_index, video_text = packed
        modulation = mod_table[step_index].astype(jnp.float32)
        gain = 1.0 + modulation[1]
        modulated = (video_hidden.astype(jnp.float32) * gain + modulation[0]).astype(jnp.bfloat16)
        token_out = jnp.dot(modulated, head_weight, preferred_element_type=jnp.float32).astype(jnp.bfloat16)
        latent = token_out.reshape(LT, LH // 2, LW // 2, 2, 2, C).transpose(0, 1, 3, 2, 4, 5).reshape(LT, LH, LW, C)
        pre_first = conv_apply(latent, conv_in, False)
        act_first = jax.nn.silu(pre_first).astype(jnp.bfloat16)
        pre_second = conv_apply(act_first, conv_mid, False)
        decoded = jax.nn.silu(pre_second).astype(jnp.bfloat16)
        pooled = lax.optimization_barrier(jnp.sum(decoded, axis=(1, 2), dtype=jnp.float32)) / (LH * LW)
        reward, pullback = jax.vjp(lambda pool_in: scoring(pool_in, video_text, patch_weight), pooled)
        pool_grad = pullback(jnp.ones((), jnp.float32))[0]
        grad_second = (pool_grad[:, None, None, :] / (LH * LW) * silu_slope(pre_second)).astype(jnp.bfloat16)
        grad_act = conv_apply(grad_second, conv_mid, True)
        grad_first = (grad_act * silu_slope(pre_first)).astype(jnp.bfloat16)
        latent_grad = conv_apply(grad_first, conv_in, True).astype(jnp.bfloat16)
        token_grad = latent_grad.reshape(LT, LH // 2, 2, LW // 2, 2, C).transpose(0, 1, 3, 2, 4, 5).reshape(S, 4 * C)
        hidden_grad = (jnp.dot(token_grad, head_weight.T, preferred_element_type=jnp.float32) * gain).astype(jnp.bfloat16)
        head_term = jnp.dot(modulated.T, token_grad, preferred_element_type=jnp.float32)
        return (reward, hidden_grad, head_term)
    rewards, hidden_grads, head_terms = lax.map(one_video, (per_video, timestep, text_emb))
    return (rewards, lax.optimization_barrier(jnp.sum(head_terms, axis=0)), hidden_grads.reshape(TOKENS, D))
```

```python
import functools

import jax
import jax.numpy as jnp
import numpy as np
from jax import lax
from jax.experimental import pallas as pl
from jax.experimental.pallas import tpu as pltpu
from jax.sharding import PartitionSpec as P

LW = 64
LT = 2
DEEP = 256
TILE = 128
PAIR_COLS = LW // 2
BF = jnp.bfloat16
F32 = jnp.float32
MIB = 1024 * 1024


def params(mib):
    return pltpu.CompilerParams(vmem_limit_bytes=mib * MIB)


def sigmoid(value):
    return 1.0 / (1.0 + jnp.exp(-value))


def dot(left, right):
    return jnp.dot(left, right, preferred_element_type=F32)


def dot_nt(left, right):
    return lax.dot_general(left, right, (((1,), (1,)), ((), ())), preferred_element_type=F32)


def selection(channels):
    pick = np.zeros((3, 3, 2, 2, channels, 4, 4, channels), np.float32)
    for pair_row in range(3):
        for row in range(2):
            patch_row = 2 * (pair_row - 1) + row + 1
            for pair_col in range(3):
                for col in range(2):
                    patch_col = 2 * (pair_col - 1) + col + 1
                    if 0 <= patch_row < 4 and 0 <= patch_col < 4:
                        for k in range(channels):
                            pick[pair_row, pair_col, row, col, k, patch_row, patch_col, k] = 1.0
    return pick.reshape(36 * channels, 16 * channels).astype(BF)


def pack_kernel(taps_hbm, packed_ref, taps, sem):
    count = taps.shape[0]
    copy = pltpu.make_async_copy(taps_hbm.at[pl.ds(taps_hbm.shape[0] - count, count)], taps, sem)
    copy.start()
    copy.wait()
    odd = lax.axis_index("mp") % 2
    lane = lax.broadcasted_iota(jnp.int32, (taps.shape[1], TILE), 1)
    for side in range(2):

        @pl.when(odd == side)
        def _():
            for pair in range(count // 2):
                first, second = taps[2 * pair], taps[2 * pair + 1]
                packed_ref[pair, :, :TILE] = first[:, side * TILE : (side + 1) * TILE]
                packed_ref[pair, :, TILE : 2 * TILE] = second[:, side * TILE : (side + 1) * TILE]
                left, right = first[:, 2 * TILE :].astype(F32), second[:, 2 * TILE :].astype(F32)
                if side == 0:
                    right = pltpu.roll(right, TILE // 2, 1)
                else:
                    left = pltpu.roll(left, TILE // 2, 1)
                packed_ref[pair, :, 2 * TILE :] = jnp.where(lane < TILE // 2, left, right).astype(BF)


def head_kernel(
    parts, step_hbm, hidden_hbm, mod_hbm, head_hbm, modulated_ref, gain_ref, send_ref, step_ref, hidden_ref, mod_ref,
    head_ref, sems
):
    copies = [
        pltpu.make_async_copy(hidden_hbm, hidden_ref, sems.at[0]),
        pltpu.make_async_copy(mod_hbm, mod_ref, sems.at[1]),
        pltpu.make_async_copy(head_hbm, head_ref, sems.at[2]),
        pltpu.make_async_copy(step_hbm, step_ref, sems.at[3]),
    ]
    for copy in copies:
        copy.start()
    for copy in copies:
        copy.wait()
    mod = mod_ref[step_ref[0]].astype(F32)
    gain = 1.0 + mod[1:2]
    modulated = (hidden_ref[...].astype(F32) * gain + mod[0:1]).astype(BF)
    modulated_ref[...] = modulated
    gain_ref[...] = gain
    terms = dot_nt(modulated, head_ref[...])
    half = terms.shape[0] // 2
    wide = jnp.concatenate([terms[:half], terms[half:]], axis=1)
    n = PAIR_COLS
    blank = jnp.zeros((n, wide.shape[1]), F32)
    lower = lax.broadcasted_iota(jnp.int32, blank.shape, 1) // (wide.shape[1] // 4) % 2 == 1

    def pair_row(i):
        return blank if i < 0 or i >= parts else wide[i * n : (i + 1) * n]

    for part in range(0, parts, 2):
        outer = jnp.where(lower, pair_row(part - 2), pair_row(part + 3))
        rows = [pair_row(part + i) for i in range(-1, 3)] + [outer]
        block = jnp.concatenate(rows, axis=0).astype(BF)
        send_ref[part] = block
        send_ref[part + 1] = block


def build_patch_weights(conv_ref, patch_w):
    channels, width = conv_ref.shape[1], conv_ref.shape[2]
    patch_w[...] = jnp.zeros_like(patch_w)
    for a in range(2):
        for b in range(3):
            for c in range(3):
                tap = conv_ref[9 * a + 3 * b + c]
                for r in range(2):
                    for s in range(2):
                        row = ((r + b) * 4 + s + c) * channels
                        col = (2 * r + s) * width
                        patch_w[a, row : row + channels, col : col + width] = tap


def weight_copies(refs, weights, sems):
    rows = refs[0].shape[1]
    return [
        pltpu.make_async_copy(ref, weights.at[:, pl.ds(i * rows, rows), :], sems.at[i]) for i, ref in enumerate(refs)
    ]


def tap_weights(refs, tap):
    pair, side = tap // 2, tap % 2
    blocks = []
    for ref in refs:
        half = ref[pair, :, 2 * TILE :]
        lane = lax.broadcasted_iota(jnp.int32, half.shape, 1)
        half = jnp.where((lane < TILE // 2) == (side == 0), half, jnp.zeros_like(half))
        blocks.append(jnp.concatenate([ref[pair, :, side * TILE : (side + 1) * TILE], half], axis=1))
    filled = sum(block.shape[0] for block in blocks)
    return jnp.concatenate(blocks + [jnp.zeros((DEEP - filled, 2 * TILE), BF)], axis=0)


def store_views(views, t, row, even, odd, odd_down, even_up):
    n, deep = PAIR_COLS, even.shape[1]
    for c, (at_even, at_odd) in enumerate(((odd_down, even), (even, odd), (odd, even_up))):
        views[t, row, 0:n, c * deep : (c + 1) * deep] = at_even
        views[t, row, n : 2 * n, c * deep : (c + 1) * deep] = at_odd


def shift_down(value):
    place = lax.broadcasted_iota(jnp.int32, value.shape, 0) % PAIR_COLS
    return jnp.where(place == 0, 0.0, pltpu.roll(value, 1, 0))


def shift_up(value):
    place = lax.broadcasted_iota(jnp.int32, value.shape, 0) % PAIR_COLS
    return jnp.where(place == PAIR_COLS - 1, 0.0, pltpu.roll(value, value.shape[0] - 1, 0))


def near_kernel(parts, blocks, info_ref, recv_ref, conv_ref, pick_ref, *refs):
    acc, far_views, slope_ref, weights, patch_w, views, sems = refs[blocks:]
    copies = weight_copies(refs[:blocks], weights, sems)
    for copy in copies:
        copy.start()
    n = PAIR_COLS
    width = conv_ref.shape[2]
    build_patch_weights(conv_ref, patch_w)

    latent = recv_ref[0].astype(F32)
    for part in range(1, parts):
        latent = latent + recv_ref[part].astype(F32)
    latent = latent.astype(BF).astype(F32)
    left, right = shift_down(latent), shift_up(latent)
    half = latent.shape[1] // 2
    stacked = []
    for t in range(LT):
        lanes = slice(t * half, (t + 1) * half)
        cols = jnp.concatenate([left[:, lanes], latent[:, lanes], right[:, lanes]], axis=1)
        above = jnp.concatenate([cols[4 * n :], cols[: 3 * n]], axis=0)
        stacked.append(jnp.concatenate([above, cols[: 4 * n], cols[n:]], axis=1))
    patches = dot(jnp.concatenate(stacked, axis=0).astype(BF), pick_ref[...]).astype(BF)

    top_scale, bottom_scale = edge_scales(parts, info_ref[0])
    group = lax.broadcasted_iota(jnp.int32, (8 * n, 1), 0) // n % 4
    scale = jnp.where(group == 0, top_scale, jnp.where(group == 3, bottom_scale, 1.0))
    for r in range(2):
        lanes = slice(2 * r * width, (2 * r + 2) * width)
        pre = dot(patches, patch_w[1, :, lanes])
        late = dot(patches[: 4 * n], patch_w[0, :, lanes])
        pre = jnp.concatenate([pre[: 4 * n], pre[4 * n :] + late], axis=0)
        gate = sigmoid(pre)
        act = pre * gate * scale
        even, odd = act[:, :width], act[:, width:]
        odd_down, even_up = shift_down(odd).astype(BF), shift_up(even).astype(BF)
        even, odd = even.astype(BF), odd.astype(BF)
        for t in range(LT):
            for g in range(4):
                at = slice((4 * t + g) * n, (4 * t + g + 1) * n)
                for target, lanes in ((views, slice(0, DEEP)), (far_views, slice(DEEP, 2 * DEEP))):
                    store_views(
                        target, t, 2 * g + r, even[at, lanes], odd[at, lanes], odd_down[at, lanes], even_up[at, lanes]
                    )
            for g in (1, 2):
                at = slice((4 * t + g) * n, (4 * t + g + 1) * n)
                own, own_gate = pre[at], gate[at]
                slope = own_gate * (1.0 + own * (1.0 - own_gate))
                base = (4 * t + 2 * (g - 1) + r) * 2 * n
                slope_ref[base : base + n, :] = slope[:, :width]
                slope_ref[base + n : base + 2 * n, :] = slope[:, width:]

    for copy in copies:
        copy.wait()
    add_taps(views, [weights], acc, None)


def edge_scales(parts, mp_index):
    place = mp_index // 2
    return jnp.where(place == 0, 0.0, 1.0).astype(F32), jnp.where(place == parts // 2 - 1, 0.0, 1.0).astype(F32)


def add_taps(views, refs, acc, base):
    half_rows = acc.shape[0] // 2
    rows = half_rows // (2 * PAIR_COLS)
    for b in range(3):
        field = views[:, b : b + rows].reshape(2 * half_rows, 3 * DEEP)
        now = dot(field, jnp.concatenate([tap_weights(refs, 9 + 3 * b + c) for c in range(3)], axis=0))
        late = dot(field[:half_rows], jnp.concatenate([tap_weights(refs, 3 * b + c) for c in range(3)], axis=0))
        so_far = acc if b else base
        if so_far is None:
            acc[:half_rows] = now[:half_rows]
            acc[half_rows:] = now[half_rows:] + late
        else:
            acc[:half_rows] = so_far[:half_rows] + now[:half_rows]
            acc[half_rows:] = so_far[half_rows:] + (now[half_rows:] + late)


def far_kernel(parts, info_ref, near_ref, views, *refs):
    sums_ref, slope_ref, acc = refs[-3:]
    add_taps(views, refs[:-3], acc, near_ref)
    n = PAIR_COLS
    top_scale, bottom_scale = edge_scales(parts, info_ref[0])
    tiles = []
    for t in range(LT):
        for row in range(6):
            part = acc[(6 * t + row) * 2 * n : (6 * t + row + 1) * 2 * n]
            half = part[:, TILE:]
            pre = jnp.concatenate([part[:, :TILE], half + pltpu.roll(half, TILE // 2, 1)], axis=1)
            gate = sigmoid(pre)
            slope = gate * (1.0 + pre * (1.0 - gate))
            if row == 0:
                slope = slope * top_scale
            elif row == 5:
                slope = slope * bottom_scale
            else:
                part_sum = jnp.sum(pre * gate, axis=0, keepdims=True)
                total = part_sum if row == 1 else total + part_sum
            slope_ref[t, row] = slope.astype(BF)
        tiles += [total[:, :TILE], total[:, TILE:]]
    sums = jnp.concatenate(tiles + [jnp.zeros((8 - len(tiles), TILE), F32)], axis=0)
    for part in range(parts):
        sums_ref[part] = sums


def three_terms(value):
    high = value.astype(BF)
    rest = value - high.astype(F32)
    middle = rest.astype(BF)
    low = (rest - middle.astype(F32)).astype(BF)
    return jnp.concatenate([high, middle, low], axis=0)


def backward_kernel(
    parts, cells, info_ref, sums_ref, patch_ref, text_ref, second_ref, slope_ref, pick_ref, patch_w, near_w, *refs
):
    far_refs = refs[:-4]
    reward_ref, send_ref, views, acc = refs[-4:]
    n = PAIR_COLS
    lane = lax.broadcasted_iota(jnp.int32, (8, TILE), 1)

    by_side = []
    for side in range(2):
        total = sums_ref[side]
        for part in range(side + 2, parts, 2):
            total = total + sums_ref[part]
        by_side.append(total)
    rows = []
    for t in range(LT):
        even, odd = [total[2 * t : 2 * t + 2] for total in by_side]
        mixed = jnp.where(lane[:1] < TILE // 2, even[1:2], odd[1:2])
        rows.append(jnp.concatenate([even[0:1], odd[0:1], mixed], axis=1))
    pooled = jnp.concatenate(rows + [jnp.zeros((8 - LT, 3 * TILE), F32)], axis=0) / cells
    products = dot(three_terms(pooled), patch_ref[...])
    embedded = products[0:8] + products[8:16] + products[16:24]
    text = text_ref[...]
    text_length = jnp.sqrt(jnp.sum(text * text, axis=1, keepdims=True) + 1e-06)
    embed_square = jnp.sum(embedded * embedded, axis=1, keepdims=True) + 1e-06
    embed_length = jnp.sqrt(embed_square)
    along = jnp.sum(embedded * text, axis=1, keepdims=True)
    cosine = along / (embed_length * text_length)
    share = 100.0 / LT
    reward_ref[0] = share * (cosine[0, 0] + cosine[1, 0])
    embed_grad = share * (text / (embed_length * text_length) - cosine * embedded / embed_square)
    products = dot_nt(three_terms(embed_grad), patch_ref[...])
    pool_grad = (products[0:8] + products[8:16] + products[16:24]) / cells

    side = info_ref[0] % 2
    third = pool_grad[:, 2 * TILE :]
    turned = pltpu.roll(third, TILE // 2, 1)
    half = jnp.where((lane < TILE // 2) == (side == 0), third, turned)
    own_grad = jnp.concatenate([jnp.where(side == 0, pool_grad[:, :TILE], pool_grad[:, TILE : 2 * TILE]), half], axis=1)

    for row in range(6):
        for t in range(LT):
            grad = second_ref[t, row].astype(F32) * own_grad[t : t + 1]
            even, odd = grad[:n], grad[n:]
            store_views(
                views, t, row, even.astype(BF), odd.astype(BF), shift_down(odd).astype(BF), shift_up(even).astype(BF)
            )

    half_rows = 8 * n
    for b in range(3):
        field = views[:, 2 - b : 6 - b].reshape(2 * half_rows, 6 * TILE)
        for blocks, lanes in (([near_w], slice(0, DEEP)), (far_refs, slice(DEEP, 2 * DEEP))):
            now = dot_nt(field, jnp.concatenate([tap_weights(blocks, 9 + 3 * b + c) for c in (2, 1, 0)], axis=1))
            early = dot_nt(
                field[half_rows:], jnp.concatenate([tap_weights(blocks, 3 * b + c) for c in (2, 1, 0)], axis=1)
            )
            if b == 0:
                acc[:half_rows, lanes] = now[:half_rows] + early
                acc[half_rows:, lanes] = now[half_rows:]
            else:
                acc[:half_rows, lanes] += now[:half_rows] + early
                acc[half_rows:, lanes] += now[half_rows:]
    grad_first = (acc[...] * slope_ref[...]).astype(BF)
    tokens = []
    for t in range(LT):
        for g in range(2):
            base = (8 * t + 4 * g) * n
            planes = [grad_first[base + i * n : base + (i + 1) * n] for i in range(4)]
            tokens.append(jnp.concatenate(planes, axis=1))
    patch_grad = dot_nt(jnp.concatenate(tokens, axis=0), patch_w[1])
    early = dot_nt(jnp.concatenate(tokens[2:], axis=0), patch_w[0])
    patch_grad = jnp.concatenate([patch_grad[: 2 * n] + early, patch_grad[2 * n :]], axis=0)
    spread_out = dot_nt(patch_grad.astype(BF), pick_ref[...])
    half = spread_out.shape[1] // 9
    blocks = [[], [], []]
    for t in range(LT):
        parts_of = []
        for g in range(2):
            rows = spread_out[(2 * t + g) * n : (2 * t + g + 1) * n]
            for pair_row in range(3):
                base = 3 * pair_row * half
                parts_of.append(
                    shift_up(rows[:, base : base + half])
                    + rows[:, base + half : base + 2 * half]
                    + shift_down(rows[:, base + 2 * half : base + 3 * half])
                )
        up, first, first_down, second_up, second, down = parts_of
        blocks[0].append(first + second_up)
        blocks[1].append(second + first_down)
        blocks[2].append(up + down)
    result = jnp.concatenate([jnp.concatenate(block, axis=1) for block in blocks], axis=0).astype(BF)
    for part in range(parts):
        send_ref[part] = result


def token_kernel(parts, recv_ref, modulated_ref, tokens_ref, head_ref):
    n = PAIR_COLS
    lanes = recv_ref.shape[2]
    sums = [recv_ref[i].astype(F32) + recv_ref[i + 1].astype(F32) for i in range(0, parts, 2)]
    blank = jnp.zeros((n, lanes), F32)
    lower = lax.broadcasted_iota(jnp.int32, blank.shape, 1) // (lanes // 4) % 2 == 1
    rows = []
    for i, block in enumerate(sums):
        from_above = sums[i - 1][2 * n :] if i else blank
        from_below = sums[i + 1][2 * n :] if i + 1 < len(sums) else blank
        rows.append(block[:n] + jnp.where(lower, 0.0, from_above))
        rows.append(block[n : 2 * n] + jnp.where(lower, from_below, 0.0))
    wide = jnp.concatenate(rows, axis=0)
    tokens = jnp.concatenate([wide[:, : lanes // 2], wide[:, lanes // 2 :]], axis=0)
    flipped = jnp.transpose(tokens).astype(BF)
    tokens_ref[...] = tokens.astype(BF)
    head_ref[...] = dot(flipped, modulated_ref[...]).astype(BF)


def hidden_kernel(tokens_ref, head_ref, gain_ref, out_ref):
    out_ref[...] = (dot(tokens_ref[...], head_ref[...]) * gain_ref[...]).astype(BF)


VMEM = pl.BlockSpec(memory_space=pltpu.VMEM)
SMEM = pl.BlockSpec(memory_space=pltpu.SMEM)
HBM = pl.BlockSpec(memory_space=pltpu.HBM)


def exchange(block, axis, flip):
    count = lax.axis_size(axis)
    return lax.ppermute(block, axis, [(i, i ^ flip) for i in range(count)])


def spread(piece):
    blocks = {0: piece}
    flip = lax.axis_size("dp") // 4
    while flip:
        for held in list(blocks):
            blocks[held ^ flip] = exchange(blocks[held], "dp", flip)
        flip //= 2
    unit, rows = 1, piece.shape[1]
    while rows * unit % 16:
        low = (lax.axis_index("dp") // unit) % 2 == 0
        merged = {}
        for held in blocks:
            if held % (2 * unit) == 0:
                mine, other = blocks[held], blocks[held ^ unit]
                merged[held] = jnp.where(
                    low, jnp.concatenate([mine, other], axis=1), jnp.concatenate([other, mine], axis=1)
                )
        blocks, unit = merged, 2 * unit
    return [blocks[held] for held in sorted(blocks)], unit


def local_channels(weight, unit):
    count = lax.axis_size("dp") // unit
    place = lax.axis_index("dp") // unit
    rows = weight.shape[2] // count
    blocks = [weight[..., i * rows : (i + 1) * rows] for i in range(count)]
    flip = count // 2
    while flip:
        swap = place // flip % 2 == 1
        blocks = [jnp.where(swap, blocks[i ^ flip], blocks[i]) for i in range(count)]
        flip //= 2
    spare = jnp.zeros(weight.shape[:2] + (DEEP - weight.shape[2] // 2,), weight.dtype)
    return jnp.concatenate(blocks[: count // 2] + [spare] + blocks[count // 2 :] + [spare], axis=2)


def body(hidden, mod_table, timestep, head_weight, conv_in, conv_mid, patch_weight, text_emb):
    parts = lax.axis_size("mp")
    groups = lax.axis_size("dp")
    tokens, depth = hidden.shape
    features = head_weight.shape[1]
    channels = features // 4
    width = conv_in.shape[2]
    n = PAIR_COLS
    pair_rows = tokens // (LT * n)
    cells = float(2 * pair_rows * LW)
    mp_index = lax.axis_index("mp")

    head_rows = head_weight.T
    taps = jnp.transpose(conv_mid, (1, 0, 2))
    rows = conv_mid.shape[0]
    far = groups // 2

    packed = pl.pallas_call(
        pack_kernel,
        in_specs=[HBM],
        out_specs=VMEM,
        out_shape=jax.ShapeDtypeStruct((9, rows, width), BF),
        scratch_shapes=[pltpu.VMEM((18, rows, width), BF), pltpu.SemaphoreType.DMA],
        compiler_params=params(56),
        name="pack",
    )(taps)
    distant = exchange(packed, "dp", far)
    modulated, gain, send = pl.pallas_call(
        functools.partial(head_kernel, parts),
        in_specs=[HBM] * 4,
        out_specs=[VMEM] * 3,
        out_shape=[
            jax.ShapeDtypeStruct((tokens, depth), BF),
            jax.ShapeDtypeStruct((1, depth), F32),
            jax.ShapeDtypeStruct((parts, 5 * n, 2 * features), BF),
        ],
        scratch_shapes=[
            pltpu.SMEM((1,), jnp.int32),
            pltpu.VMEM((tokens, depth), BF),
            pltpu.VMEM(mod_table.shape, BF),
            pltpu.VMEM((features, depth), BF),
            pltpu.SemaphoreType.DMA((4,)),
        ],
        compiler_params=params(56),
        name="head",
    )(timestep, hidden, mod_table, head_rows)
    send, conv_in = lax.optimization_barrier((send, conv_in))
    recv = lax.all_to_all(send, "mp", 0, 0, tiled=True)
    near_blocks, unit = spread(packed)
    recv, distant = lax.optimization_barrier((recv, distant))
    far_blocks, _ = spread(distant)
    blocks = len(near_blocks)
    info = jnp.reshape(mp_index, (1,)).astype(jnp.int32)
    taps_in = local_channels(jnp.transpose(conv_in[:, 9:], (1, 0, 2)), unit)
    pick = jnp.asarray(selection(channels))

    acc_shape = jax.ShapeDtypeStruct((24 * n, 2 * TILE), F32)
    views_shape = (LT, 8, 2 * n, 3 * DEEP)
    near_acc, far_views, slope, near_w, patch_w = pl.pallas_call(
        functools.partial(near_kernel, parts, blocks),
        in_specs=[SMEM, VMEM, VMEM, VMEM] + [HBM] * blocks,
        out_specs=[VMEM] * 5,
        out_shape=[
            acc_shape,
            jax.ShapeDtypeStruct(views_shape, BF),
            jax.ShapeDtypeStruct((16 * n, 2 * DEEP), F32),
            jax.ShapeDtypeStruct((9, width // 2, width), BF),
            jax.ShapeDtypeStruct((2, 16 * channels, 8 * DEEP), BF),
        ],
        scratch_shapes=[pltpu.VMEM(views_shape, BF), pltpu.SemaphoreType.DMA((blocks,))],
        cost_estimate=pl.CostEstimate(flops=4 * 10**9, bytes_accessed=10**7, transcendentals=10**6),
        compiler_params=params(20),
        name="near",
    )(info, recv, taps_in, pick, *near_blocks)
    sums, second_slope = pl.pallas_call(
        functools.partial(far_kernel, parts),
        in_specs=[SMEM] + [VMEM] * (2 + blocks),
        out_specs=[VMEM] * 2,
        out_shape=[
            jax.ShapeDtypeStruct((parts, 8, TILE), F32),
            jax.ShapeDtypeStruct((LT, 6, 2 * n, 2 * TILE), BF),
        ],
        scratch_shapes=[pltpu.VMEM(acc_shape.shape, F32)],
        compiler_params=params(16),
        name="far",
    )(info, near_acc, far_views, *far_blocks)
    all_sums = lax.all_to_all(sums, "mp", 0, 0, tiled=True)

    reward, contribution = pl.pallas_call(
        functools.partial(backward_kernel, parts, cells),
        in_specs=[SMEM] + [VMEM] * (8 + blocks),
        out_specs=[SMEM, VMEM],
        out_shape=[
            jax.ShapeDtypeStruct((1,), F32),
            jax.ShapeDtypeStruct((parts, 3 * n, 2 * features), BF),
        ],
        scratch_shapes=[pltpu.VMEM((LT, 6, 2 * n, 6 * TILE), BF), pltpu.VMEM((16 * n, 2 * DEEP), F32)],
        compiler_params=params(16),
        name="backward",
    )(info, all_sums, patch_weight, text_emb, second_slope, slope, pick, patch_w, near_w, *far_blocks)
    contributions = lax.all_to_all(contribution, "mp", 0, 0, tiled=True)

    token_grad, head_term = pl.pallas_call(
        functools.partial(token_kernel, parts),
        in_specs=[VMEM, VMEM],
        out_specs=[VMEM, VMEM],
        out_shape=[
            jax.ShapeDtypeStruct((tokens, features), BF),
            jax.ShapeDtypeStruct((features, depth), BF),
        ],
        compiler_params=params(8),
        name="token",
    )(contributions, modulated)
    flip = 1
    while flip < far:
        other = exchange(head_term, "dp", flip)
        head_term = (head_term.astype(F32) + other.astype(F32)).astype(BF)
        flip *= 2
    head_other = exchange(head_term, "dp", far)
    hidden_grad = pl.pallas_call(
        hidden_kernel,
        in_specs=[VMEM] * 3,
        out_specs=VMEM,
        out_shape=jax.ShapeDtypeStruct((tokens, depth), BF),
        compiler_params=params(8),
        name="hidden_grad",
    )(token_grad, head_rows, gain)
    head_grad = head_term.astype(F32) + head_other.astype(F32)
    return (reward, head_grad.T, hidden_grad)


def solution(mesh):
    in_specs = (
        P("dp", "mp"),
        P(None, None, "mp"),
        P("dp"),
        P("mp", None),
        P(),
        P("dp", None, None),
        P(),
        P("dp", None),
    )
    out_specs = (P("dp"), P("mp", None), P("dp", "mp"))
    return jax.shard_map(body, mesh=mesh, in_specs=in_specs, out_specs=out_specs, check_vma=False)
```

```python
import functools

import jax
import jax.numpy as jnp
import numpy as np
from jax import lax
from jax.experimental import pallas as pl
from jax.experimental.pallas import tpu as pltpu
from jax.sharding import PartitionSpec as P

LW = 64
LT = 2
DEEP = 256
TILE = 128
PAIR_COLS = LW // 2
BF = jnp.bfloat16
F32 = jnp.float32
MIB = 1024 * 1024


def params(mib):
    return pltpu.CompilerParams(vmem_limit_bytes=mib * MIB)


def sigmoid(value):
    return 1.0 / (1.0 + jnp.exp(-value))


def dot(left, right):
    return jnp.dot(left, right, preferred_element_type=F32)


def dot_nt(left, right):
    return lax.dot_general(left, right, (((1,), (1,)), ((), ())), preferred_element_type=F32)


def selection(channels):
    pick = np.zeros((3, 3, 2, 2, channels, 4, 4, channels), np.float32)
    for pair_row in range(3):
        for row in range(2):
            patch_row = 2 * (pair_row - 1) + row + 1
            for pair_col in range(3):
                for col in range(2):
                    patch_col = 2 * (pair_col - 1) + col + 1
                    if 0 <= patch_row < 4 and 0 <= patch_col < 4:
                        for k in range(channels):
                            pick[pair_row, pair_col, row, col, k, patch_row, patch_col, k] = 1.0
    return pick.reshape(36 * channels, 16 * channels).astype(BF)


def pack_kernel(taps_hbm, packed_hbm, packed, thirds, in_sems, out_sems):
    first = taps_hbm.shape[0] - 18
    odd = lax.axis_index("mp") % 2
    own = pl.ds(pl.multiple_of(odd * TILE, TILE), TILE)
    copies, results = [], []
    for chunk in range(3):
        pairs = pl.ds(3 * chunk, 3)
        here = []
        for side in range(2):
            source = taps_hbm.at[pl.ds(first + 9 * side + 3 * chunk, 3)]
            here.append((source.at[:, :, own], packed.at[pairs, :, pl.ds(side * TILE, TILE)]))
            here.append((source.at[:, :, pl.ds(2 * TILE, TILE)], thirds.at[side, pairs]))
        copies.append([pltpu.make_async_copy(*ends, in_sems.at[chunk, i]) for i, ends in enumerate(here)])
        results.append(pltpu.make_async_copy(packed.at[pairs], packed_hbm.at[pairs], out_sems.at[chunk]))
    for chunk in range(3):
        for copy in copies[chunk]:
            copy.start()
    lane = lax.broadcasted_iota(jnp.int32, thirds.shape[2:], 1)
    for chunk in range(3):
        for copy in copies[chunk]:
            copy.wait()
        for pair in range(3 * chunk, 3 * chunk + 3):
            left, right = thirds[0, pair].astype(F32), thirds[1, pair].astype(F32)
            left = jnp.where(odd == 0, left, pltpu.roll(left, TILE // 2, 1))
            right = jnp.where(odd == 0, pltpu.roll(right, TILE // 2, 1), right)
            packed[pair, :, 2 * TILE :] = jnp.where(lane < TILE // 2, left, right).astype(BF)
        results[chunk].start()
    for result in results:
        result.wait()


def head_kernel(
    parts, step_hbm, hidden_hbm, mod_hbm, head_hbm, modulated_hbm, gain_ref, send_hbm, step_ref, hidden_ref, mod_ref,
    head_ref, modulated, blocks, in_sems, out_sems, send_sems
):
    n = PAIR_COLS
    half = hidden_ref.shape[0] // LT
    frames = [pl.ds(t * half, half) for t in range(LT)]
    small = [
        pltpu.make_async_copy(step_hbm, step_ref, in_sems.at[0]),
        pltpu.make_async_copy(mod_hbm, mod_ref, in_sems.at[1]),
        pltpu.make_async_copy(head_hbm, head_ref, in_sems.at[2]),
    ]
    large = [
        pltpu.make_async_copy(hidden_hbm.at[rows], hidden_ref.at[rows], in_sems.at[3 + t])
        for t, rows in enumerate(frames)
    ]
    results = [
        pltpu.make_async_copy(modulated.at[rows], modulated_hbm.at[rows], out_sems.at[t]) for t, rows in enumerate(frames)
    ]
    for copy in small + large:
        copy.start()
    for copy in small:
        copy.wait()
    step = jnp.broadcast_to(step_ref[...], mod_ref.shape[1:])
    mod = jnp.zeros(mod_ref.shape[1:], F32)
    for i in range(mod_ref.shape[0]):
        mod = mod + jnp.where(step == i, mod_ref[i].astype(F32), 0.0)
    gain = 1.0 + mod[1:2]
    gain_ref[...] = gain
    terms = []
    for t, rows in enumerate(frames):
        large[t].wait()
        values = (hidden_ref[rows].astype(F32) * gain + mod[0:1]).astype(BF)
        modulated[rows] = values
        results[t].start()
        terms.append(dot_nt(values, head_ref[...]))
    wide = jnp.concatenate(terms, axis=1)
    blank = jnp.zeros((n, wide.shape[1]), F32)
    lower = lax.broadcasted_iota(jnp.int32, blank.shape, 1) // (wide.shape[1] // 4) % 2 == 1

    def pair_row(i):
        return blank if i < 0 or i >= parts else wide[i * n : (i + 1) * n]

    sends = []
    for part in range(0, parts, 2):
        outer = jnp.where(lower, pair_row(part - 2), pair_row(part + 3))
        rows = [pair_row(part + i) for i in range(-1, 3)] + [outer]
        blocks[part // 2] = jnp.concatenate(rows, axis=0).astype(BF)
        for i in (part, part + 1):
            sends.append(pltpu.make_async_copy(blocks.at[part // 2], send_hbm.at[i], send_sems.at[i]))
            sends[-1].start()
    for result in results + sends:
        result.wait()


def build_patch_weights(conv_ref, patch_w):
    channels, width = conv_ref.shape[1], conv_ref.shape[2]
    patch_w[...] = jnp.zeros_like(patch_w)
    for a in range(2):
        for b in range(3):
            for c in range(3):
                tap = conv_ref[9 * a + 3 * b + c]
                for r in range(2):
                    for s in range(2):
                        row = ((r + b) * 4 + s + c) * channels
                        col = (2 * r + s) * width
                        patch_w[a, row : row + channels, col : col + width] = tap


def weight_copies(refs, weights, sems):
    rows = refs[0].shape[1]
    return [
        pltpu.make_async_copy(ref, weights.at[:, pl.ds(i * rows, rows), :], sems.at[i]) for i, ref in enumerate(refs)
    ]


def tap_weights(refs, tap):
    pair, side = tap % 9, tap // 9
    blocks = []
    for ref in refs:
        half = ref[pair, :, 2 * TILE :]
        lane = lax.broadcasted_iota(jnp.int32, half.shape, 1)
        half = jnp.where((lane < TILE // 2) == (side == 0), half, jnp.zeros_like(half))
        blocks.append(jnp.concatenate([ref[pair, :, side * TILE : (side + 1) * TILE], half], axis=1))
    filled = sum(block.shape[0] for block in blocks)
    return jnp.concatenate(blocks + [jnp.zeros((DEEP - filled, 2 * TILE), BF)], axis=0)


def store_views(views, t, row, even, odd, odd_down, even_up):
    n, deep = PAIR_COLS, even.shape[1]
    for c, (at_even, at_odd) in enumerate(((odd_down, even), (even, odd), (odd, even_up))):
        views[t, row, 0:n, c * deep : (c + 1) * deep] = at_even
        views[t, row, n : 2 * n, c * deep : (c + 1) * deep] = at_odd


def shift_down(value):
    place = lax.broadcasted_iota(jnp.int32, value.shape, 0) % PAIR_COLS
    return jnp.where(place == 0, 0.0, pltpu.roll(value, 1, 0))


def shift_up(value):
    place = lax.broadcasted_iota(jnp.int32, value.shape, 0) % PAIR_COLS
    return jnp.where(place == PAIR_COLS - 1, 0.0, pltpu.roll(value, value.shape[0] - 1, 0))


def near_kernel(parts, blocks, info_ref, recv_ref, conv_ref, pick_ref, *refs):
    acc, far_views, slope_ref, weights, patch_w, views, sems = refs[blocks:]
    copies = weight_copies(refs[:blocks], weights, sems)
    for copy in copies:
        copy.start()
    n = PAIR_COLS
    width = conv_ref.shape[2]
    build_patch_weights(conv_ref, patch_w)

    latent = recv_ref[0].astype(F32)
    for part in range(1, parts):
        latent = latent + recv_ref[part].astype(F32)
    latent = latent.astype(BF).astype(F32)
    left, right = shift_down(latent), shift_up(latent)
    half = latent.shape[1] // 2
    stacked = []
    for t in range(LT):
        lanes = slice(t * half, (t + 1) * half)
        cols = jnp.concatenate([left[:, lanes], latent[:, lanes], right[:, lanes]], axis=1)
        above = jnp.concatenate([cols[4 * n :], cols[: 3 * n]], axis=0)
        stacked.append(jnp.concatenate([above, cols[: 4 * n], cols[n:]], axis=1))
    patches = dot(jnp.concatenate(stacked, axis=0).astype(BF), pick_ref[...]).astype(BF)

    top_scale, bottom_scale = edge_scales(parts, info_ref[0])
    group = lax.broadcasted_iota(jnp.int32, (8 * n, 1), 0) // n % 4
    scale = jnp.where(group == 0, top_scale, jnp.where(group == 3, bottom_scale, 1.0))
    for r in range(2):
        lanes = slice(2 * r * width, (2 * r + 2) * width)
        pre = dot(patches, patch_w[1, :, lanes])
        late = dot(patches[: 4 * n], patch_w[0, :, lanes])
        pre = jnp.concatenate([pre[: 4 * n], pre[4 * n :] + late], axis=0)
        gate = sigmoid(pre)
        act = pre * gate * scale
        even, odd = act[:, :width], act[:, width:]
        odd_down, even_up = shift_down(odd).astype(BF), shift_up(even).astype(BF)
        even, odd = even.astype(BF), odd.astype(BF)
        for t in range(LT):
            for g in range(4):
                at = slice((4 * t + g) * n, (4 * t + g + 1) * n)
                for target, lanes in ((views, slice(0, DEEP)), (far_views, slice(DEEP, 2 * DEEP))):
                    store_views(
                        target, t, 2 * g + r, even[at, lanes], odd[at, lanes], odd_down[at, lanes], even_up[at, lanes]
                    )
            for g in (1, 2):
                at = slice((4 * t + g) * n, (4 * t + g + 1) * n)
                own, own_gate = pre[at], gate[at]
                slope = own_gate * (1.0 + own * (1.0 - own_gate))
                base = (4 * t + 2 * (g - 1) + r) * 2 * n
                slope_ref[base : base + n, :] = slope[:, :width]
                slope_ref[base + n : base + 2 * n, :] = slope[:, width:]

    for copy in copies:
        copy.wait()
    add_taps(views, [weights], acc, None)


def edge_scales(parts, mp_index):
    place = mp_index // 2
    return jnp.where(place == 0, 0.0, 1.0).astype(F32), jnp.where(place == parts // 2 - 1, 0.0, 1.0).astype(F32)


def add_taps(views, refs, acc, base):
    half_rows = acc.shape[0] // 2
    rows = half_rows // (2 * PAIR_COLS)
    for b in range(3):
        field = views[:, b : b + rows].reshape(2 * half_rows, 3 * DEEP)
        now = dot(field, jnp.concatenate([tap_weights(refs, 9 + 3 * b + c) for c in range(3)], axis=0))
        late = dot(field[:half_rows], jnp.concatenate([tap_weights(refs, 3 * b + c) for c in range(3)], axis=0))
        so_far = acc if b else base
        if so_far is None:
            acc[:half_rows] = now[:half_rows]
            acc[half_rows:] = now[half_rows:] + late
        else:
            acc[:half_rows] = so_far[:half_rows] + now[:half_rows]
            acc[half_rows:] = so_far[half_rows:] + (now[half_rows:] + late)


def far_kernel(parts, info_ref, near_ref, views, *refs):
    sums_ref, slope_ref, acc = refs[-3:]
    add_taps(views, refs[:-3], acc, near_ref)
    n = PAIR_COLS
    top_scale, bottom_scale = edge_scales(parts, info_ref[0])
    tiles = []
    for t in range(LT):
        for row in range(6):
            part = acc[(6 * t + row) * 2 * n : (6 * t + row + 1) * 2 * n]
            half = part[:, TILE:]
            pre = jnp.concatenate([part[:, :TILE], half + pltpu.roll(half, TILE // 2, 1)], axis=1)
            gate = sigmoid(pre)
            slope = gate * (1.0 + pre * (1.0 - gate))
            if row == 0:
                slope = slope * top_scale
            elif row == 5:
                slope = slope * bottom_scale
            else:
                part_sum = jnp.sum(pre * gate, axis=0, keepdims=True)
                total = part_sum if row == 1 else total + part_sum
            slope_ref[t, row] = slope.astype(BF)
        tiles += [total[:, :TILE], total[:, TILE:]]
    sums = jnp.concatenate(tiles + [jnp.zeros((8 - len(tiles), TILE), F32)], axis=0)
    for part in range(parts):
        sums_ref[part] = sums


def three_terms(value):
    high = value.astype(BF)
    rest = value - high.astype(F32)
    middle = rest.astype(BF)
    low = (rest - middle.astype(F32)).astype(BF)
    return jnp.concatenate([high, middle, low], axis=0)


def backward_kernel(
    parts, cells, info_ref, sums_ref, patch_ref, text_ref, second_ref, slope_ref, pick_ref, patch_w, near_w, *refs
):
    far_refs = refs[:-4]
    reward_ref, send_ref, views, acc = refs[-4:]
    n = PAIR_COLS
    lane = lax.broadcasted_iota(jnp.int32, (8, TILE), 1)

    by_side = []
    for side in range(2):
        total = sums_ref[side]
        for part in range(side + 2, parts, 2):
            total = total + sums_ref[part]
        by_side.append(total)
    rows = []
    for t in range(LT):
        even, odd = [total[2 * t : 2 * t + 2] for total in by_side]
        mixed = jnp.where(lane[:1] < TILE // 2, even[1:2], odd[1:2])
        rows.append(jnp.concatenate([even[0:1], odd[0:1], mixed], axis=1))
    pooled = jnp.concatenate(rows + [jnp.zeros((8 - LT, 3 * TILE), F32)], axis=0) / cells
    products = dot(three_terms(pooled), patch_ref[...])
    embedded = products[0:8] + products[8:16] + products[16:24]
    text = text_ref[...]
    text_length = jnp.sqrt(jnp.sum(text * text, axis=1, keepdims=True) + 1e-06)
    embed_square = jnp.sum(embedded * embedded, axis=1, keepdims=True) + 1e-06
    embed_length = jnp.sqrt(embed_square)
    along = jnp.sum(embedded * text, axis=1, keepdims=True)
    cosine = along / (embed_length * text_length)
    share = 100.0 / LT
    reward_ref[0] = share * (cosine[0, 0] + cosine[1, 0])
    embed_grad = share * (text / (embed_length * text_length) - cosine * embedded / embed_square)
    products = dot_nt(three_terms(embed_grad), patch_ref[...])
    pool_grad = (products[0:8] + products[8:16] + products[16:24]) / cells

    side = info_ref[0] % 2
    third = pool_grad[:, 2 * TILE :]
    turned = pltpu.roll(third, TILE // 2, 1)
    half = jnp.where((lane < TILE // 2) == (side == 0), third, turned)
    own_grad = jnp.concatenate([jnp.where(side == 0, pool_grad[:, :TILE], pool_grad[:, TILE : 2 * TILE]), half], axis=1)

    for row in range(6):
        for t in range(LT):
            grad = second_ref[t, row].astype(F32) * own_grad[t : t + 1]
            even, odd = grad[:n], grad[n:]
            store_views(
                views, t, row, even.astype(BF), odd.astype(BF), shift_down(odd).astype(BF), shift_up(even).astype(BF)
            )

    half_rows = 8 * n
    for b in range(3):
        field = views[:, 2 - b : 6 - b].reshape(2 * half_rows, 6 * TILE)
        for blocks, lanes in (([near_w], slice(0, DEEP)), (far_refs, slice(DEEP, 2 * DEEP))):
            now = dot_nt(field, jnp.concatenate([tap_weights(blocks, 9 + 3 * b + c) for c in (2, 1, 0)], axis=1))
            early = dot_nt(
                field[half_rows:], jnp.concatenate([tap_weights(blocks, 3 * b + c) for c in (2, 1, 0)], axis=1)
            )
            if b == 0:
                acc[:half_rows, lanes] = now[:half_rows] + early
                acc[half_rows:, lanes] = now[half_rows:]
            else:
                acc[:half_rows, lanes] += now[:half_rows] + early
                acc[half_rows:, lanes] += now[half_rows:]
    grad_first = (acc[...] * slope_ref[...]).astype(BF)
    tokens = []
    for t in range(LT):
        for g in range(2):
            base = (8 * t + 4 * g) * n
            planes = [grad_first[base + i * n : base + (i + 1) * n] for i in range(4)]
            tokens.append(jnp.concatenate(planes, axis=1))
    patch_grad = dot_nt(jnp.concatenate(tokens, axis=0), patch_w[1])
    early = dot_nt(jnp.concatenate(tokens[2:], axis=0), patch_w[0])
    patch_grad = jnp.concatenate([patch_grad[: 2 * n] + early, patch_grad[2 * n :]], axis=0)
    spread_out = dot_nt(patch_grad.astype(BF), pick_ref[...])
    half = spread_out.shape[1] // 9
    blocks = [[], [], []]
    for t in range(LT):
        parts_of = []
        for g in range(2):
            rows = spread_out[(2 * t + g) * n : (2 * t + g + 1) * n]
            for pair_row in range(3):
                base = 3 * pair_row * half
                parts_of.append(
                    shift_up(rows[:, base : base + half])
                    + rows[:, base + half : base + 2 * half]
                    + shift_down(rows[:, base + 2 * half : base + 3 * half])
                )
        up, first, first_down, second_up, second, down = parts_of
        blocks[0].append(first + second_up)
        blocks[1].append(second + first_down)
        blocks[2].append(up + down)
    result = jnp.concatenate([jnp.concatenate(block, axis=1) for block in blocks], axis=0).astype(BF)
    for part in range(parts):
        send_ref[part] = result


def token_kernel(parts, recv_ref, modulated_ref, tokens_ref, head_ref):
    n = PAIR_COLS
    lanes = recv_ref.shape[2]
    sums = [recv_ref[i].astype(F32) + recv_ref[i + 1].astype(F32) for i in range(0, parts, 2)]
    blank = jnp.zeros((n, lanes), F32)
    lower = lax.broadcasted_iota(jnp.int32, blank.shape, 1) // (lanes // 4) % 2 == 1
    rows = []
    for i, block in enumerate(sums):
        from_above = sums[i - 1][2 * n :] if i else blank
        from_below = sums[i + 1][2 * n :] if i + 1 < len(sums) else blank
        rows.append(block[:n] + jnp.where(lower, 0.0, from_above))
        rows.append(block[n : 2 * n] + jnp.where(lower, from_below, 0.0))
    wide = jnp.concatenate(rows, axis=0)
    tokens = jnp.concatenate([wide[:, : lanes // 2], wide[:, lanes // 2 :]], axis=0)
    flipped = jnp.transpose(tokens).astype(BF)
    tokens_ref[...] = tokens.astype(BF)
    head_ref[...] = dot(flipped, modulated_ref[...]).astype(BF)


def hidden_kernel(tokens_ref, head_ref, gain_ref, out_ref):
    out_ref[...] = (dot(tokens_ref[...], head_ref[...]) * gain_ref[...]).astype(BF)


VMEM = pl.BlockSpec(memory_space=pltpu.VMEM)
SMEM = pl.BlockSpec(memory_space=pltpu.SMEM)
HBM = pl.BlockSpec(memory_space=pltpu.HBM)


def exchange(block, axis, flip):
    count = lax.axis_size(axis)
    return lax.ppermute(block, axis, [(i, i ^ flip) for i in range(count)])


def spread(piece):
    blocks = {0: piece}
    flip = lax.axis_size("dp") // 4
    while flip:
        for held in list(blocks):
            blocks[held ^ flip] = exchange(blocks[held], "dp", flip)
        flip //= 2
    unit, rows = 1, piece.shape[1]
    while rows * unit % 16:
        low = (lax.axis_index("dp") // unit) % 2 == 0
        merged = {}
        for held in blocks:
            if held % (2 * unit) == 0:
                mine, other = blocks[held], blocks[held ^ unit]
                merged[held] = jnp.where(
                    low, jnp.concatenate([mine, other], axis=1), jnp.concatenate([other, mine], axis=1)
                )
        blocks, unit = merged, 2 * unit
    return [blocks[held] for held in sorted(blocks)], unit


def local_channels(weight, unit):
    count = lax.axis_size("dp") // unit
    place = lax.axis_index("dp") // unit
    rows = weight.shape[2] // count
    blocks = [weight[..., i * rows : (i + 1) * rows] for i in range(count)]
    flip = count // 2
    while flip:
        swap = place // flip % 2 == 1
        blocks = [jnp.where(swap, blocks[i ^ flip], blocks[i]) for i in range(count)]
        flip //= 2
    spare = jnp.zeros(weight.shape[:2] + (DEEP - weight.shape[2] // 2,), weight.dtype)
    return jnp.concatenate(blocks[: count // 2] + [spare] + blocks[count // 2 :] + [spare], axis=2)


def body(hidden, mod_table, timestep, head_weight, conv_in, conv_mid, patch_weight, text_emb):
    parts = lax.axis_size("mp")
    groups = lax.axis_size("dp")
    tokens, depth = hidden.shape
    features = head_weight.shape[1]
    channels = features // 4
    width = conv_in.shape[2]
    n = PAIR_COLS
    pair_rows = tokens // (LT * n)
    cells = float(2 * pair_rows * LW)
    mp_index = lax.axis_index("mp")

    head_rows = head_weight.T
    taps = jnp.transpose(conv_mid, (1, 0, 2))
    rows = conv_mid.shape[0]
    far = groups // 2

    packed = pl.pallas_call(
        pack_kernel,
        in_specs=[HBM],
        out_specs=HBM,
        out_shape=jax.ShapeDtypeStruct((9, rows, width), BF),
        scratch_shapes=[
            pltpu.VMEM((9, rows, width), BF),
            pltpu.VMEM((2, 9, rows, TILE), BF),
            pltpu.SemaphoreType.DMA((3, 4)),
            pltpu.SemaphoreType.DMA((3,)),
        ],
        compiler_params=params(56),
        name="pack",
    )(taps)
    distant = exchange(packed, "dp", far)
    modulated, gain, send = pl.pallas_call(
        functools.partial(head_kernel, parts),
        in_specs=[HBM] * 4,
        out_specs=[HBM, VMEM, HBM],
        out_shape=[
            jax.ShapeDtypeStruct((tokens, depth), BF),
            jax.ShapeDtypeStruct((1, depth), F32),
            jax.ShapeDtypeStruct((parts, 5 * n, 2 * features), BF),
        ],
        scratch_shapes=[
            pltpu.VMEM((1, 1), jnp.int32),
            pltpu.VMEM((tokens, depth), BF),
            pltpu.VMEM(mod_table.shape, BF),
            pltpu.VMEM((features, depth), BF),
            pltpu.VMEM((tokens, depth), BF),
            pltpu.VMEM((parts // 2, 5 * n, 2 * features), BF),
            pltpu.SemaphoreType.DMA((5,)),
            pltpu.SemaphoreType.DMA((LT,)),
            pltpu.SemaphoreType.DMA((parts,)),
        ],
        compiler_params=params(56),
        name="head",
    )(timestep.reshape(1, 1), hidden, mod_table, head_rows)
    send, conv_in = lax.optimization_barrier((send, conv_in))
    recv = lax.all_to_all(send, "mp", 0, 0, tiled=True)
    near_blocks, unit = spread(packed)
    recv, distant = lax.optimization_barrier((recv, distant))
    far_blocks, _ = spread(distant)
    blocks = len(near_blocks)
    info = jnp.reshape(mp_index, (1,)).astype(jnp.int32)
    taps_in = local_channels(jnp.transpose(conv_in[:, 9:], (1, 0, 2)), unit)
    pick = jnp.asarray(selection(channels))

    acc_shape = jax.ShapeDtypeStruct((24 * n, 2 * TILE), F32)
    views_shape = (LT, 8, 2 * n, 3 * DEEP)
    near_acc, far_views, slope, near_w, patch_w = pl.pallas_call(
        functools.partial(near_kernel, parts, blocks),
        in_specs=[SMEM, VMEM, VMEM, VMEM] + [HBM] * blocks,
        out_specs=[VMEM] * 5,
        out_shape=[
            acc_shape,
            jax.ShapeDtypeStruct(views_shape, BF),
            jax.ShapeDtypeStruct((16 * n, 2 * DEEP), F32),
            jax.ShapeDtypeStruct((9, width // 2, width), BF),
            jax.ShapeDtypeStruct((2, 16 * channels, 8 * DEEP), BF),
        ],
        scratch_shapes=[pltpu.VMEM(views_shape, BF), pltpu.SemaphoreType.DMA((blocks,))],
        cost_estimate=pl.CostEstimate(flops=4 * 10**9, bytes_accessed=10**7, transcendentals=10**6),
        compiler_params=params(20),
        name="near",
    )(info, recv, taps_in, pick, *near_blocks)
    sums, second_slope = pl.pallas_call(
        functools.partial(far_kernel, parts),
        in_specs=[SMEM] + [VMEM] * (2 + blocks),
        out_specs=[VMEM] * 2,
        out_shape=[
            jax.ShapeDtypeStruct((parts, 8, TILE), F32),
            jax.ShapeDtypeStruct((LT, 6, 2 * n, 2 * TILE), BF),
        ],
        scratch_shapes=[pltpu.VMEM(acc_shape.shape, F32)],
        compiler_params=params(16),
        name="far",
    )(info, near_acc, far_views, *far_blocks)
    all_sums = lax.all_to_all(sums, "mp", 0, 0, tiled=True)

    reward, contribution = pl.pallas_call(
        functools.partial(backward_kernel, parts, cells),
        in_specs=[SMEM] + [VMEM] * (8 + blocks),
        out_specs=[SMEM, VMEM],
        out_shape=[
            jax.ShapeDtypeStruct((1,), F32),
            jax.ShapeDtypeStruct((parts, 3 * n, 2 * features), BF),
        ],
        scratch_shapes=[pltpu.VMEM((LT, 6, 2 * n, 6 * TILE), BF), pltpu.VMEM((16 * n, 2 * DEEP), F32)],
        compiler_params=params(16),
        name="backward",
    )(info, all_sums, patch_weight, text_emb, second_slope, slope, pick, patch_w, near_w, *far_blocks)
    contributions = lax.all_to_all(contribution, "mp", 0, 0, tiled=True)

    token_grad, head_term = pl.pallas_call(
        functools.partial(token_kernel, parts),
        in_specs=[VMEM, VMEM],
        out_specs=[VMEM, VMEM],
        out_shape=[
            jax.ShapeDtypeStruct((tokens, features), BF),
            jax.ShapeDtypeStruct((features, depth), BF),
        ],
        compiler_params=params(8),
        name="token",
    )(contributions, modulated)
    flip = 1
    while flip < far:
        other = exchange(head_term, "dp", flip)
        head_term = (head_term.astype(F32) + other.astype(F32)).astype(BF)
        flip *= 2
    head_other = exchange(head_term, "dp", far)
    hidden_grad = pl.pallas_call(
        hidden_kernel,
        in_specs=[VMEM] * 3,
        out_specs=VMEM,
        out_shape=jax.ShapeDtypeStruct((tokens, depth), BF),
        compiler_params=params(8),
        name="hidden_grad",
    )(token_grad, head_rows, gain)
    head_grad = head_term.astype(F32) + head_other.astype(F32)
    return (reward, head_grad.T, hidden_grad)


def solution(mesh):
    in_specs = (
        P("dp", "mp"),
        P(None, None, "mp"),
        P("dp"),
        P("mp", None),
        P(),
        P("dp", None, None),
        P(),
        P("dp", None),
    )
    out_specs = (P("dp"), P("mp", None), P("dp", "mp"))
    return jax.shard_map(body, mesh=mesh, in_specs=in_specs, out_specs=out_specs, check_vma=False)
```

```python
import functools

import jax
import jax.numpy as jnp
import numpy as np
from jax import lax
from jax.experimental import pallas as pl
from jax.experimental.pallas import tpu as pltpu
from jax.sharding import PartitionSpec as P

LW = 64
LT = 2
DEEP = 256
TILE = 128
PAIR_COLS = LW // 2
BF = jnp.bfloat16
F32 = jnp.float32
MIB = 1024 * 1024


def params(mib):
    return pltpu.CompilerParams(vmem_limit_bytes=mib * MIB)


def sigmoid(value):
    return 0.5 + 0.5 * jnp.tanh(0.5 * value)


def dot(left, right):
    return jnp.dot(left, right, preferred_element_type=F32)


def dot_nt(left, right):
    return lax.dot_general(left, right, (((1,), (1,)), ((), ())), preferred_element_type=F32)


def selection(channels):
    pick = np.zeros((3, 3, 2, 2, channels, 4, 4, channels), np.float32)
    for pair_row in range(3):
        for row in range(2):
            patch_row = 2 * (pair_row - 1) + row + 1
            for pair_col in range(3):
                for col in range(2):
                    patch_col = 2 * (pair_col - 1) + col + 1
                    if 0 <= patch_row < 4 and 0 <= patch_col < 4:
                        for k in range(channels):
                            pick[pair_row, pair_col, row, col, k, patch_row, patch_col, k] = 1.0
    return pick.reshape(36 * channels, 16 * channels).astype(BF)


def pack_kernel(taps_hbm, packed_hbm, packed, thirds, in_sems, out_sems):
    first = taps_hbm.shape[0] - 18
    odd = lax.axis_index("mp") % 2
    own = pl.ds(pl.multiple_of(odd * TILE, TILE), TILE)
    copies, results = [], []
    for chunk in range(3):
        pairs = pl.ds(3 * chunk, 3)
        here = []
        for side in range(2):
            source = taps_hbm.at[pl.ds(first + 9 * side + 3 * chunk, 3)]
            here.append((source.at[:, :, own], packed.at[pairs, :, pl.ds(side * TILE, TILE)]))
            here.append((source.at[:, :, pl.ds(2 * TILE, TILE)], thirds.at[side, pairs]))
        copies.append([pltpu.make_async_copy(*ends, in_sems.at[chunk, i]) for i, ends in enumerate(here)])
        results.append(pltpu.make_async_copy(packed.at[pairs], packed_hbm.at[pairs], out_sems.at[chunk]))
    for chunk in range(3):
        for copy in copies[chunk]:
            copy.start()
    lane = lax.broadcasted_iota(jnp.int32, thirds.shape[2:], 1)
    for chunk in range(3):
        for copy in copies[chunk]:
            copy.wait()
        for pair in range(3 * chunk, 3 * chunk + 3):
            left, right = thirds[0, pair].astype(F32), thirds[1, pair].astype(F32)
            left = jnp.where(odd == 0, left, pltpu.roll(left, TILE // 2, 1))
            right = jnp.where(odd == 0, pltpu.roll(right, TILE // 2, 1), right)
            packed[pair, :, 2 * TILE :] = jnp.where(lane < TILE // 2, left, right).astype(BF)
        results[chunk].start()
    for result in results:
        result.wait()


def head_kernel(
    parts, step_ref, hidden_hbm, mod_hbm, head_hbm, modulated_hbm, gain_ref, send_hbm, hidden_ref, mod_ref, head_ref,
    modulated, blocks, in_sems, out_sems, send_sems
):
    n = PAIR_COLS
    half = hidden_ref.shape[0] // LT
    frames = [pl.ds(t * half, half) for t in range(LT)]
    small = [
        pltpu.make_async_copy(mod_hbm, mod_ref, in_sems.at[0]),
        pltpu.make_async_copy(head_hbm, head_ref, in_sems.at[1]),
    ]
    large = [
        pltpu.make_async_copy(hidden_hbm.at[rows], hidden_ref.at[rows], in_sems.at[2 + t])
        for t, rows in enumerate(frames)
    ]
    results = [
        pltpu.make_async_copy(modulated.at[rows], modulated_hbm.at[rows], out_sems.at[t]) for t, rows in enumerate(frames)
    ]
    for copy in small + large:
        copy.start()
    for copy in small:
        copy.wait()
    mod = mod_ref[step_ref[0]].astype(F32)
    gain = 1.0 + mod[1:2]
    gain_ref[...] = gain
    terms = []
    for t, rows in enumerate(frames):
        large[t].wait()
        values = (hidden_ref[rows].astype(F32) * gain + mod[0:1]).astype(BF)
        modulated[rows] = values
        results[t].start()
        terms.append(dot_nt(values, head_ref[...]))
    wide = jnp.concatenate(terms, axis=1)
    blank = jnp.zeros((n, wide.shape[1]), F32)
    lower = lax.broadcasted_iota(jnp.int32, blank.shape, 1) // (wide.shape[1] // 4) % 2 == 1

    def pair_row(i):
        return blank if i < 0 or i >= parts else wide[i * n : (i + 1) * n]

    for part in range(0, parts, 2):
        outer = jnp.where(lower, pair_row(part - 2), pair_row(part + 3))
        rows = [pair_row(part + i) for i in range(-1, 3)] + [outer]
        blocks[part // 2] = jnp.concatenate(rows, axis=0).astype(BF)
        for i in (part, part + 1):
            results.append(pltpu.make_async_copy(blocks.at[part // 2], send_hbm.at[i], send_sems.at[i]))
            results[-1].start()

    for result in results:
        result.wait()


def build_patch_weights(conv_ref, patch_w):
    channels, width = conv_ref.shape[1], conv_ref.shape[2]
    patch_w[...] = jnp.zeros_like(patch_w)
    for a in range(2):
        for b in range(3):
            for c in range(3):
                tap = conv_ref[9 * a + 3 * b + c]
                for r in range(2):
                    for s in range(2):
                        row = ((r + b) * 4 + s + c) * channels
                        col = (2 * r + s) * width
                        patch_w[a, row : row + channels, col : col + width] = tap


def weight_copies(refs, weights, sems):
    rows = refs[0].shape[1]
    return [
        pltpu.make_async_copy(ref, weights.at[:, pl.ds(i * rows, rows), :], sems.at[i]) for i, ref in enumerate(refs)
    ]


def tap_weights(refs, tap):
    pair, side = tap % 9, tap // 9
    blocks = []
    for ref in refs:
        half = ref[pair, :, 2 * TILE :]
        lane = lax.broadcasted_iota(jnp.int32, half.shape, 1)
        half = half * jnp.where((lane < TILE // 2) == (side == 0), 1.0, 0.0).astype(BF)
        blocks.append(jnp.concatenate([ref[pair, :, side * TILE : (side + 1) * TILE], half], axis=1))
    filled = sum(block.shape[0] for block in blocks)
    return jnp.concatenate(blocks + [jnp.zeros((DEEP - filled, 2 * TILE), BF)], axis=0)


def store_views(views, t, row, even, odd, odd_down, even_up):
    n, deep = PAIR_COLS, even.shape[1]
    for c, (at_even, at_odd) in enumerate(((odd_down, even), (even, odd), (odd, even_up))):
        views[t, row, 0:n, c * deep : (c + 1) * deep] = at_even
        views[t, row, n : 2 * n, c * deep : (c + 1) * deep] = at_odd


def shift_down(value):
    place = lax.broadcasted_iota(jnp.int32, value.shape, 0) % PAIR_COLS
    return jnp.where(place == 0, 0.0, pltpu.roll(value, 1, 0))


def shift_up(value):
    place = lax.broadcasted_iota(jnp.int32, value.shape, 0) % PAIR_COLS
    return jnp.where(place == PAIR_COLS - 1, 0.0, pltpu.roll(value, value.shape[0] - 1, 0))


def near_kernel(parts, blocks, info_ref, recv_ref, conv_ref, pick_ref, *refs):
    acc, far_views, slope_ref, weights, patch_w, views, sems = refs[blocks:]
    copies = weight_copies(refs[:blocks], weights, sems)
    for copy in copies:
        copy.start()
    n = PAIR_COLS
    width = conv_ref.shape[2]
    build_patch_weights(conv_ref, patch_w)

    latent = recv_ref[0].astype(F32)
    for part in range(1, parts):
        latent = latent + recv_ref[part].astype(F32)
    latent = latent.astype(BF).astype(F32)
    left, right = shift_down(latent), shift_up(latent)
    half = latent.shape[1] // 2
    stacked = []
    for t in range(LT):
        lanes = slice(t * half, (t + 1) * half)
        cols = jnp.concatenate([left[:, lanes], latent[:, lanes], right[:, lanes]], axis=1)
        above = jnp.concatenate([cols[4 * n :], cols[: 3 * n]], axis=0)
        stacked.append(jnp.concatenate([above, cols[: 4 * n], cols[n:]], axis=1))
    patches = dot(jnp.concatenate(stacked, axis=0).astype(BF), pick_ref[...]).astype(BF)

    top_scale, bottom_scale = edge_scales(parts, info_ref[0])
    group = lax.broadcasted_iota(jnp.int32, (8 * n, 1), 0) // n % 4
    scale = jnp.where(group == 0, top_scale, jnp.where(group == 3, bottom_scale, 1.0))
    for r in range(2):
        lanes = slice(2 * r * width, (2 * r + 2) * width)
        pre = dot(patches, patch_w[1, :, lanes])
        late = dot(patches[: 4 * n], patch_w[0, :, lanes])
        pre = jnp.concatenate([pre[: 4 * n], pre[4 * n :] + late], axis=0)
        gate = sigmoid(pre)
        act = pre * gate * scale
        even, odd = act[:, :width], act[:, width:]
        odd_down, even_up = shift_down(odd).astype(BF), shift_up(even).astype(BF)
        even, odd = even.astype(BF), odd.astype(BF)
        for t in range(LT):
            for g in range(4):
                at = slice((4 * t + g) * n, (4 * t + g + 1) * n)
                for target, lanes in ((views, slice(0, DEEP)), (far_views, slice(DEEP, 2 * DEEP))):
                    store_views(
                        target, t, 2 * g + r, even[at, lanes], odd[at, lanes], odd_down[at, lanes], even_up[at, lanes]
                    )
            for g in (1, 2):
                at = slice((4 * t + g) * n, (4 * t + g + 1) * n)
                own, own_gate = pre[at], gate[at]
                slope = own_gate * (1.0 + own * (1.0 - own_gate))
                base = (4 * t + 2 * (g - 1) + r) * 2 * n
                slope_ref[base : base + n, :] = slope[:, :width]
                slope_ref[base + n : base + 2 * n, :] = slope[:, width:]

    for copy in copies:
        copy.wait()
    add_taps(views, [weights], acc, None)


def edge_scales(parts, mp_index):
    place = mp_index // 2
    return jnp.where(place == 0, 0.0, 1.0).astype(F32), jnp.where(place == parts // 2 - 1, 0.0, 1.0).astype(F32)


def add_taps(views, refs, acc, base):
    half_rows = acc.shape[0] // 2
    rows = half_rows // (2 * PAIR_COLS)
    for b in range(3):
        field = views[:, b : b + rows].reshape(2 * half_rows, 3 * DEEP)
        now = dot(field, jnp.concatenate([tap_weights(refs, 9 + 3 * b + c) for c in range(3)], axis=0))
        late = dot(field[:half_rows], jnp.concatenate([tap_weights(refs, 3 * b + c) for c in range(3)], axis=0))
        so_far = acc if b else base
        if so_far is None:
            acc[:half_rows] = now[:half_rows]
            acc[half_rows:] = now[half_rows:] + late
        else:
            acc[:half_rows] = so_far[:half_rows] + now[:half_rows]
            acc[half_rows:] = so_far[half_rows:] + (now[half_rows:] + late)


def far_kernel(parts, info_ref, near_ref, views, *refs):
    sums_ref, slope_ref, acc = refs[-3:]
    add_taps(views, refs[:-3], acc, near_ref)
    n = PAIR_COLS
    top_scale, bottom_scale = edge_scales(parts, info_ref[0])
    tiles = []
    for t in range(LT):
        for row in range(6):
            part = acc[(6 * t + row) * 2 * n : (6 * t + row + 1) * 2 * n]
            half = part[:, TILE:]
            pre = jnp.concatenate([part[:, :TILE], half + pltpu.roll(half, TILE // 2, 1)], axis=1)
            gate = sigmoid(pre)
            slope = gate * (1.0 + pre * (1.0 - gate))
            if row == 0:
                slope = slope * top_scale
            elif row == 5:
                slope = slope * bottom_scale
            else:
                part_sum = jnp.sum(pre * gate, axis=0, keepdims=True)
                total = part_sum if row == 1 else total + part_sum
            slope_ref[t, row] = slope.astype(BF)
        tiles += [total[:, :TILE], total[:, TILE:]]
    sums = jnp.concatenate(tiles + [jnp.zeros((8 - len(tiles), TILE), F32)], axis=0)
    for part in range(parts):
        sums_ref[part] = sums


def three_terms(value):
    high = value.astype(BF)
    rest = value - high.astype(F32)
    middle = rest.astype(BF)
    low = (rest - middle.astype(F32)).astype(BF)
    return jnp.concatenate([high, middle, low], axis=0)


def backward_kernel(
    parts, cells, info_ref, sums_ref, patch_ref, text_ref, second_ref, slope_ref, pick_ref, patch_w, near_w, *refs
):
    far_refs = refs[:-4]
    reward_ref, send_ref, views, acc = refs[-4:]
    n = PAIR_COLS
    lane = lax.broadcasted_iota(jnp.int32, (8, TILE), 1)

    by_side = []
    for side in range(2):
        total = sums_ref[side]
        for part in range(side + 2, parts, 2):
            total = total + sums_ref[part]
        by_side.append(total)
    rows = []
    for t in range(LT):
        even, odd = [total[2 * t : 2 * t + 2] for total in by_side]
        mixed = jnp.where(lane[:1] < TILE // 2, even[1:2], odd[1:2])
        rows.append(jnp.concatenate([even[0:1], odd[0:1], mixed], axis=1))
    pooled = jnp.concatenate(rows + [jnp.zeros((8 - LT, 3 * TILE), F32)], axis=0) / cells
    products = dot(three_terms(pooled), patch_ref[...])
    embedded = products[0:8] + products[8:16] + products[16:24]
    text = text_ref[...]
    text_length = jnp.sqrt(jnp.sum(text * text, axis=1, keepdims=True) + 1e-06)
    embed_square = jnp.sum(embedded * embedded, axis=1, keepdims=True) + 1e-06
    embed_length = jnp.sqrt(embed_square)
    along = jnp.sum(embedded * text, axis=1, keepdims=True)
    cosine = along / (embed_length * text_length)
    share = 100.0 / LT
    reward_ref[0] = share * (cosine[0, 0] + cosine[1, 0])
    embed_grad = share * (text / (embed_length * text_length) - cosine * embedded / embed_square)
    products = dot_nt(three_terms(embed_grad), patch_ref[...])
    pool_grad = (products[0:8] + products[8:16] + products[16:24]) / cells

    side = info_ref[0] % 2
    third = pool_grad[:, 2 * TILE :]
    turned = pltpu.roll(third, TILE // 2, 1)
    half = jnp.where((lane < TILE // 2) == (side == 0), third, turned)
    own_grad = jnp.concatenate([jnp.where(side == 0, pool_grad[:, :TILE], pool_grad[:, TILE : 2 * TILE]), half], axis=1)

    for row in range(6):
        for t in range(LT):
            grad = second_ref[t, row].astype(F32) * own_grad[t : t + 1]
            even, odd = grad[:n], grad[n:]
            store_views(
                views, t, row, even.astype(BF), odd.astype(BF), shift_down(odd).astype(BF), shift_up(even).astype(BF)
            )

    half_rows = 8 * n
    for b in range(3):
        field = views[:, 2 - b : 6 - b].reshape(2 * half_rows, 6 * TILE)
        for blocks, lanes in (([near_w], slice(0, DEEP)), (far_refs, slice(DEEP, 2 * DEEP))):
            now = dot_nt(field, jnp.concatenate([tap_weights(blocks, 9 + 3 * b + c) for c in (2, 1, 0)], axis=1))
            early = dot_nt(
                field[half_rows:], jnp.concatenate([tap_weights(blocks, 3 * b + c) for c in (2, 1, 0)], axis=1)
            )
            if b == 0:
                acc[:half_rows, lanes] = now[:half_rows] + early
                acc[half_rows:, lanes] = now[half_rows:]
            else:
                acc[:half_rows, lanes] += now[:half_rows] + early
                acc[half_rows:, lanes] += now[half_rows:]
    grad_first = (acc[...] * slope_ref[...]).astype(BF)
    tokens = []
    for t in range(LT):
        for g in range(2):
            base = (8 * t + 4 * g) * n
            planes = [grad_first[base + i * n : base + (i + 1) * n] for i in range(4)]
            tokens.append(jnp.concatenate(planes, axis=1))
    patch_grad = dot_nt(jnp.concatenate(tokens, axis=0), patch_w[1])
    early = dot_nt(jnp.concatenate(tokens[2:], axis=0), patch_w[0])
    patch_grad = jnp.concatenate([patch_grad[: 2 * n] + early, patch_grad[2 * n :]], axis=0)
    spread_out = dot_nt(patch_grad.astype(BF), pick_ref[...])
    half = spread_out.shape[1] // 9
    blocks = [[], [], []]
    for t in range(LT):
        parts_of = []
        for g in range(2):
            rows = spread_out[(2 * t + g) * n : (2 * t + g + 1) * n]
            for pair_row in range(3):
                base = 3 * pair_row * half
                parts_of.append(
                    shift_up(rows[:, base : base + half])
                    + rows[:, base + half : base + 2 * half]
                    + shift_down(rows[:, base + 2 * half : base + 3 * half])
                )
        up, first, first_down, second_up, second, down = parts_of
        blocks[0].append(first + second_up)
        blocks[1].append(second + first_down)
        blocks[2].append(up + down)
    result = jnp.concatenate([jnp.concatenate(block, axis=1) for block in blocks], axis=0).astype(BF)
    for part in range(parts):
        send_ref[part] = result


def token_kernel(parts, recv_ref, modulated_ref, tokens_ref, head_ref):
    n = PAIR_COLS
    lanes = recv_ref.shape[2]
    sums = [recv_ref[i].astype(F32) + recv_ref[i + 1].astype(F32) for i in range(0, parts, 2)]
    blank = jnp.zeros((n, lanes), F32)
    lower = lax.broadcasted_iota(jnp.int32, blank.shape, 1) // (lanes // 4) % 2 == 1
    rows = []
    for i, block in enumerate(sums):
        from_above = sums[i - 1][2 * n :] if i else blank
        from_below = sums[i + 1][2 * n :] if i + 1 < len(sums) else blank
        rows.append(block[:n] + jnp.where(lower, 0.0, from_above))
        rows.append(block[n : 2 * n] + jnp.where(lower, from_below, 0.0))
    wide = jnp.concatenate(rows, axis=0)
    tokens = jnp.concatenate([wide[:, : lanes // 2], wide[:, lanes // 2 :]], axis=0)
    flipped = jnp.transpose(tokens).astype(BF)
    tokens_ref[...] = tokens.astype(BF)
    head_ref[...] = dot(flipped, modulated_ref[...]).astype(BF)


def hidden_kernel(tokens_ref, head_ref, gain_ref, out_ref):
    out_ref[...] = (dot(tokens_ref[...], head_ref[...]) * gain_ref[...]).astype(BF)


VMEM = pl.BlockSpec(memory_space=pltpu.VMEM)
SMEM = pl.BlockSpec(memory_space=pltpu.SMEM)
HBM = pl.BlockSpec(memory_space=pltpu.HBM)


def exchange(block, axis, flip):
    count = lax.axis_size(axis)
    return lax.ppermute(block, axis, [(i, i ^ flip) for i in range(count)])


def spread(piece):
    blocks = {0: piece}
    flip = lax.axis_size("dp") // 4
    while flip:
        for held in list(blocks):
            blocks[held ^ flip] = exchange(blocks[held], "dp", flip)
        flip //= 2
    unit, rows = 1, piece.shape[1]
    while rows * unit % 16:
        low = (lax.axis_index("dp") // unit) % 2 == 0
        merged = {}
        for held in blocks:
            if held % (2 * unit) == 0:
                mine, other = blocks[held], blocks[held ^ unit]
                merged[held] = jnp.where(
                    low, jnp.concatenate([mine, other], axis=1), jnp.concatenate([other, mine], axis=1)
                )
        blocks, unit = merged, 2 * unit
    return [blocks[held] for held in sorted(blocks)], unit


def half_sum(term):
    total, flip = term.astype(F32), 1
    while flip < lax.axis_size("dp") // 2:
        other = exchange(term, "dp", flip)
        total = total + other.astype(F32)
        term, flip = total.astype(BF), 2 * flip
    return total


def local_channels(weight, unit):
    count = lax.axis_size("dp") // unit
    place = lax.axis_index("dp") // unit
    rows = weight.shape[2] // count
    blocks = [weight[..., i * rows : (i + 1) * rows] for i in range(count)]
    flip = count // 2
    while flip:
        swap = place // flip % 2 == 1
        blocks = [jnp.where(swap, blocks[i ^ flip], blocks[i]) for i in range(count)]
        flip //= 2
    spare = jnp.zeros(weight.shape[:2] + (DEEP - weight.shape[2] // 2,), weight.dtype)
    return jnp.concatenate(blocks[: count // 2] + [spare] + blocks[count // 2 :] + [spare], axis=2)


def body(hidden, mod_table, timestep, head_weight, conv_in, conv_mid, patch_weight, text_emb):
    parts = lax.axis_size("mp")
    groups = lax.axis_size("dp")
    tokens, depth = hidden.shape
    features = head_weight.shape[1]
    channels = features // 4
    width = conv_in.shape[2]
    n = PAIR_COLS
    pair_rows = tokens // (LT * n)
    cells = float(2 * pair_rows * LW)
    mp_index = lax.axis_index("mp")

    head_rows = head_weight.T
    taps = jnp.transpose(conv_mid, (1, 0, 2))
    rows = conv_mid.shape[0]
    far = groups // 2

    packed = pl.pallas_call(
        pack_kernel,
        in_specs=[HBM],
        out_specs=HBM,
        out_shape=jax.ShapeDtypeStruct((9, rows, width), BF),
        scratch_shapes=[
            pltpu.VMEM((9, rows, width), BF),
            pltpu.VMEM((2, 9, rows, TILE), BF),
            pltpu.SemaphoreType.DMA((3, 4)),
            pltpu.SemaphoreType.DMA((3,)),
        ],
        compiler_params=params(56),
        name="pack",
    )(taps)
    distant = exchange(packed, "dp", far)
    modulated, gain, send = pl.pallas_call(
        functools.partial(head_kernel, parts),
        in_specs=[SMEM] + [HBM] * 3,
        out_specs=[HBM, VMEM, HBM],
        out_shape=[
            jax.ShapeDtypeStruct((tokens, depth), BF),
            jax.ShapeDtypeStruct((1, depth), F32),
            jax.ShapeDtypeStruct((parts, 5 * n, 2 * features), BF),
        ],
        scratch_shapes=[
            pltpu.VMEM((tokens, depth), BF),
            pltpu.VMEM(mod_table.shape, BF),
            pltpu.VMEM((features, depth), BF),
            pltpu.VMEM((tokens, depth), BF),
            pltpu.VMEM((parts // 2, 5 * n, 2 * features), BF),
            pltpu.SemaphoreType.DMA((2 + LT,)),
            pltpu.SemaphoreType.DMA((LT,)),
            pltpu.SemaphoreType.DMA((parts,)),
        ],
        compiler_params=params(56),
        name="head",
    )(timestep, hidden, mod_table, head_rows)
    send, conv_in = lax.optimization_barrier((send, conv_in))
    recv = lax.all_to_all(send, "mp", 0, 0, tiled=True)
    near_blocks, unit = spread(packed)
    recv, distant = lax.optimization_barrier((recv, distant))
    far_blocks, _ = spread(distant)
    blocks = len(near_blocks)
    info = jnp.reshape(mp_index, (1,)).astype(jnp.int32)
    taps_in = local_channels(jnp.transpose(conv_in[:, 9:], (1, 0, 2)), unit)
    pick = jnp.asarray(selection(channels))

    acc_shape = jax.ShapeDtypeStruct((24 * n, 2 * TILE), F32)
    views_shape = (LT, 8, 2 * n, 3 * DEEP)
    near_acc, far_views, slope, near_w, patch_w = pl.pallas_call(
        functools.partial(near_kernel, parts, blocks),
        in_specs=[SMEM, VMEM, VMEM, VMEM] + [HBM] * blocks,
        out_specs=[VMEM] * 5,
        out_shape=[
            acc_shape,
            jax.ShapeDtypeStruct(views_shape, BF),
            jax.ShapeDtypeStruct((16 * n, 2 * DEEP), F32),
            jax.ShapeDtypeStruct((9, width // 2, width), BF),
            jax.ShapeDtypeStruct((2, 16 * channels, 8 * DEEP), BF),
        ],
        scratch_shapes=[pltpu.VMEM(views_shape, BF), pltpu.SemaphoreType.DMA((blocks,))],
        cost_estimate=pl.CostEstimate(flops=4 * 10**9, bytes_accessed=10**7, transcendentals=10**6),
        compiler_params=params(20),
        name="near",
    )(info, recv, taps_in, pick, *near_blocks)
    sums, second_slope = pl.pallas_call(
        functools.partial(far_kernel, parts),
        in_specs=[SMEM] + [VMEM] * (2 + blocks),
        out_specs=[VMEM] * 2,
        out_shape=[
            jax.ShapeDtypeStruct((parts, 8, TILE), F32),
            jax.ShapeDtypeStruct((LT, 6, 2 * n, 2 * TILE), BF),
        ],
        scratch_shapes=[pltpu.VMEM(acc_shape.shape, F32)],
        compiler_params=params(16),
        name="far",
    )(info, near_acc, far_views, *far_blocks)
    all_sums = lax.all_to_all(sums, "mp", 0, 0, tiled=True)

    reward, contribution = pl.pallas_call(
        functools.partial(backward_kernel, parts, cells),
        in_specs=[SMEM] + [VMEM] * (8 + blocks),
        out_specs=[SMEM, VMEM],
        out_shape=[
            jax.ShapeDtypeStruct((1,), F32),
            jax.ShapeDtypeStruct((parts, 3 * n, 2 * features), BF),
        ],
        scratch_shapes=[pltpu.VMEM((LT, 6, 2 * n, 6 * TILE), BF), pltpu.VMEM((16 * n, 2 * DEEP), F32)],
        compiler_params=params(16),
        name="backward",
    )(info, all_sums, patch_weight, text_emb, second_slope, slope, pick, patch_w, near_w, *far_blocks)
    contributions = lax.all_to_all(contribution, "mp", 0, 0, tiled=True)

    token_grad, head_term = pl.pallas_call(
        functools.partial(token_kernel, parts),
        in_specs=[VMEM, VMEM],
        out_specs=[VMEM, VMEM],
        out_shape=[
            jax.ShapeDtypeStruct((tokens, features), BF),
            jax.ShapeDtypeStruct((features, depth), BF),
        ],
        compiler_params=params(8),
        name="token",
    )(contributions, modulated)
    from_far = exchange(head_term, "dp", far)
    hidden_grad = pl.pallas_call(
        hidden_kernel,
        in_specs=[VMEM] * 3,
        out_specs=VMEM,
        out_shape=jax.ShapeDtypeStruct((tokens, depth), BF),
        compiler_params=params(8),
        name="hidden_grad",
    )(token_grad, head_rows, gain)
    head_grad = half_sum(head_term) + half_sum(from_far)
    return (reward, head_grad.T, hidden_grad)


def solution(mesh):
    in_specs = (
        P("dp", "mp"),
        P(None, None, "mp"),
        P("dp"),
        P("mp", None),
        P(),
        P("dp", None, None),
        P(),
        P("dp", None),
    )
    out_specs = (P("dp"), P("mp", None), P("dp", "mp"))
    return jax.shard_map(body, mesh=mesh, in_specs=in_specs, out_specs=out_specs, check_vma=False)
```

```python
import functools

import jax
import jax.numpy as jnp
import numpy as np
from jax import lax
from jax.experimental import pallas as pl
from jax.experimental.pallas import tpu as pltpu
from jax.sharding import PartitionSpec as P

LW = 64
LT = 2
DEEP = 256
TILE = 128
PAIR_COLS = LW // 2
BF = jnp.bfloat16
F32 = jnp.float32
MIB = 1024 * 1024


def params(mib):
    return pltpu.CompilerParams(vmem_limit_bytes=mib * MIB)


def sigmoid(value):
    return pl.reciprocal(1.0 + jnp.exp(-value), approx=True)


def dot(left, right):
    return jnp.dot(left, right, preferred_element_type=F32)


def dot_nt(left, right):
    return lax.dot_general(left, right, (((1,), (1,)), ((), ())), preferred_element_type=F32)


def selection(channels):
    pick = np.zeros((3, 3, 2, 2, channels, 4, 4, channels), np.float32)
    for pair_row in range(3):
        for row in range(2):
            patch_row = 2 * (pair_row - 1) + row + 1
            for pair_col in range(3):
                for col in range(2):
                    patch_col = 2 * (pair_col - 1) + col + 1
                    if 0 <= patch_row < 4 and 0 <= patch_col < 4:
                        for k in range(channels):
                            pick[pair_row, pair_col, row, col, k, patch_row, patch_col, k] = 1.0
    return pick.reshape(36 * channels, 16 * channels).astype(BF)


def pack_kernel(taps_hbm, packed_hbm, packed, thirds, in_sems, out_sems):
    first = taps_hbm.shape[0] - 18
    odd = lax.axis_index("mp") % 2
    own = pl.ds(pl.multiple_of(odd * TILE, TILE), TILE)
    copies, results = [], []
    for chunk in range(3):
        pairs = pl.ds(3 * chunk, 3)
        here = []
        for side in range(2):
            source = taps_hbm.at[pl.ds(first + 9 * side + 3 * chunk, 3)]
            here.append((source.at[:, :, own], packed.at[pairs, :, pl.ds(side * TILE, TILE)]))
            here.append((source.at[:, :, pl.ds(2 * TILE, TILE)], thirds.at[side, pairs]))
        copies.append([pltpu.make_async_copy(*ends, in_sems.at[chunk, i]) for i, ends in enumerate(here)])
        results.append(pltpu.make_async_copy(packed.at[pairs], packed_hbm.at[pairs], out_sems.at[chunk]))
    for chunk in range(3):
        for copy in copies[chunk]:
            copy.start()
    lane = lax.broadcasted_iota(jnp.int32, thirds.shape[2:], 1)
    for chunk in range(3):
        for copy in copies[chunk]:
            copy.wait()
        for pair in range(3 * chunk, 3 * chunk + 3):
            left, right = thirds[0, pair].astype(F32), thirds[1, pair].astype(F32)
            left = jnp.where(odd == 0, left, pltpu.roll(left, TILE // 2, 1))
            right = jnp.where(odd == 0, pltpu.roll(right, TILE // 2, 1), right)
            packed[pair, :, 2 * TILE :] = jnp.where(lane < TILE // 2, left, right).astype(BF)
        results[chunk].start()
    for result in results:
        result.wait()


def head_kernel(
    parts, step_ref, hidden_hbm, mod_hbm, head_hbm, modulated_ref, gain_ref, send_ref, hidden_ref, mod_ref, head_ref,
    sems
):
    copies = [
        pltpu.make_async_copy(hidden_hbm, hidden_ref, sems.at[0]),
        pltpu.make_async_copy(mod_hbm, mod_ref, sems.at[1]),
        pltpu.make_async_copy(head_hbm, head_ref, sems.at[2]),
    ]
    for copy in copies:
        copy.start()
    for copy in copies:
        copy.wait()
    mod = mod_ref[step_ref[0]].astype(F32)
    gain = 1.0 + mod[1:2]
    modulated = (hidden_ref[...].astype(F32) * gain + mod[0:1]).astype(BF)
    modulated_ref[...] = modulated
    gain_ref[...] = gain
    terms = dot_nt(modulated, head_ref[...])
    half = terms.shape[0] // 2
    wide = jnp.concatenate([terms[:half], terms[half:]], axis=1)
    n = PAIR_COLS
    blank = jnp.zeros((n, wide.shape[1]), F32)
    lower = lax.broadcasted_iota(jnp.int32, blank.shape, 1) // (wide.shape[1] // 4) % 2 == 1

    def pair_row(i):
        return blank if i < 0 or i >= parts else wide[i * n : (i + 1) * n]

    for part in range(0, parts, 2):
        outer = jnp.where(lower, pair_row(part - 2), pair_row(part + 3))
        rows = [pair_row(part + i) for i in range(-1, 3)] + [outer]
        block = jnp.concatenate(rows, axis=0).astype(BF)
        send_ref[part] = block
        send_ref[part + 1] = block


def build_patch_weights(conv_ref, patch_w):
    channels, width = conv_ref.shape[1], conv_ref.shape[2]
    patch_w[...] = jnp.zeros_like(patch_w)
    for a in range(2):
        for b in range(3):
            for c in range(3):
                tap = conv_ref[9 * a + 3 * b + c]
                for r in range(2):
                    for s in range(2):
                        row = ((r + b) * 4 + s + c) * channels
                        col = (2 * r + s) * width
                        patch_w[a, row : row + channels, col : col + width] = tap


def weight_copies(refs, weights, sems):
    rows = refs[0].shape[1]
    return [
        pltpu.make_async_copy(ref, weights.at[:, pl.ds(i * rows, rows), :], sems.at[i]) for i, ref in enumerate(refs)
    ]


def tap_weights(refs, tap):
    pair, side = tap % 9, tap // 9
    blocks = []
    for ref in refs:
        half = ref[pair, :, 2 * TILE :]
        lane = lax.broadcasted_iota(jnp.int32, half.shape, 1)
        half = half * jnp.where((lane < TILE // 2) == (side == 0), 1.0, 0.0).astype(BF)
        blocks.append(jnp.concatenate([ref[pair, :, side * TILE : (side + 1) * TILE], half], axis=1))
    filled = sum(block.shape[0] for block in blocks)
    return jnp.concatenate(blocks + [jnp.zeros((DEEP - filled, 2 * TILE), BF)], axis=0)


def store_views(views, t, row, even, odd, odd_down, even_up):
    n, deep = PAIR_COLS, even.shape[1]
    for c, (at_even, at_odd) in enumerate(((odd_down, even), (even, odd), (odd, even_up))):
        views[t, row, 0:n, c * deep : (c + 1) * deep] = at_even
        views[t, row, n : 2 * n, c * deep : (c + 1) * deep] = at_odd


def shift_down(value):
    place = lax.broadcasted_iota(jnp.int32, value.shape, 0) % PAIR_COLS
    return jnp.where(place == 0, 0.0, pltpu.roll(value, 1, 0))


def shift_up(value):
    place = lax.broadcasted_iota(jnp.int32, value.shape, 0) % PAIR_COLS
    return jnp.where(place == PAIR_COLS - 1, 0.0, pltpu.roll(value, value.shape[0] - 1, 0))


def near_kernel(parts, blocks, info_ref, recv_ref, conv_ref, pick_ref, *refs):
    acc, far_views, slope_ref, weights, patch_w, views, sems = refs[blocks:]
    copies = weight_copies(refs[:blocks], weights, sems)
    for copy in copies:
        copy.start()
    n = PAIR_COLS
    width = conv_ref.shape[2]
    build_patch_weights(conv_ref, patch_w)

    latent = recv_ref[0].astype(F32)
    for part in range(1, parts):
        latent = latent + recv_ref[part].astype(F32)
    latent = latent.astype(BF).astype(F32)
    left, right = shift_down(latent), shift_up(latent)
    half = latent.shape[1] // 2
    stacked = []
    for t in range(LT):
        lanes = slice(t * half, (t + 1) * half)
        cols = jnp.concatenate([left[:, lanes], latent[:, lanes], right[:, lanes]], axis=1)
        above = jnp.concatenate([cols[4 * n :], cols[: 3 * n]], axis=0)
        stacked.append(jnp.concatenate([above, cols[: 4 * n], cols[n:]], axis=1))
    patches = dot(jnp.concatenate(stacked, axis=0).astype(BF), pick_ref[...]).astype(BF)

    top_scale, bottom_scale = edge_scales(parts, info_ref[0])
    group = lax.broadcasted_iota(jnp.int32, (8 * n, 1), 0) // n % 4
    scale = jnp.where(group == 0, top_scale, jnp.where(group == 3, bottom_scale, 1.0))
    for r in range(2):
        lanes = slice(2 * r * width, (2 * r + 2) * width)
        pre = dot(patches, patch_w[1, :, lanes])
        late = dot(patches[: 4 * n], patch_w[0, :, lanes])
        pre = jnp.concatenate([pre[: 4 * n], pre[4 * n :] + late], axis=0)
        gate = sigmoid(pre)
        act = pre * gate * scale
        even, odd = act[:, :width], act[:, width:]
        odd_down, even_up = shift_down(odd).astype(BF), shift_up(even).astype(BF)
        even, odd = even.astype(BF), odd.astype(BF)
        for t in range(LT):
            for g in range(4):
                at = slice((4 * t + g) * n, (4 * t + g + 1) * n)
                for target, lanes in ((views, slice(0, DEEP)), (far_views, slice(DEEP, 2 * DEEP))):
                    store_views(
                        target, t, 2 * g + r, even[at, lanes], odd[at, lanes], odd_down[at, lanes], even_up[at, lanes]
                    )
            for g in (1, 2):
                at = slice((4 * t + g) * n, (4 * t + g + 1) * n)
                own, own_gate = pre[at], gate[at]
                slope = own_gate * (1.0 + own * (1.0 - own_gate))
                base = (4 * t + 2 * (g - 1) + r) * 2 * n
                slope_ref[base : base + n, :] = slope[:, :width]
                slope_ref[base + n : base + 2 * n, :] = slope[:, width:]

    for copy in copies:
        copy.wait()
    add_taps(views, [weights], acc, None)


def edge_scales(parts, mp_index):
    place = mp_index // 2
    return jnp.where(place == 0, 0.0, 1.0).astype(F32), jnp.where(place == parts // 2 - 1, 0.0, 1.0).astype(F32)


def add_taps(views, refs, acc, base):
    half_rows = acc.shape[0] // 2
    rows = half_rows // (2 * PAIR_COLS)
    for b in range(3):
        field = views[:, b : b + rows].reshape(2 * half_rows, 3 * DEEP)
        now = dot(field, jnp.concatenate([tap_weights(refs, 9 + 3 * b + c) for c in range(3)], axis=0))
        late = dot(field[:half_rows], jnp.concatenate([tap_weights(refs, 3 * b + c) for c in range(3)], axis=0))
        so_far = acc if b else base
        if so_far is None:
            acc[:half_rows] = now[:half_rows]
            acc[half_rows:] = now[half_rows:] + late
        else:
            acc[:half_rows] = so_far[:half_rows] + now[:half_rows]
            acc[half_rows:] = so_far[half_rows:] + (now[half_rows:] + late)


def far_kernel(parts, info_ref, near_ref, views, *refs):
    sums_ref, slope_ref, acc = refs[-3:]
    add_taps(views, refs[:-3], acc, near_ref)
    n = PAIR_COLS
    top_scale, bottom_scale = edge_scales(parts, info_ref[0])
    tiles = []
    for t in range(LT):
        for row in range(6):
            part = acc[(6 * t + row) * 2 * n : (6 * t + row + 1) * 2 * n]
            half = part[:, TILE:]
            pre = jnp.concatenate([part[:, :TILE], half + pltpu.roll(half, TILE // 2, 1)], axis=1)
            gate = sigmoid(pre)
            slope = gate * (1.0 + pre * (1.0 - gate))
            if row == 0:
                slope = slope * top_scale
            elif row == 5:
                slope = slope * bottom_scale
            else:
                part_sum = jnp.sum(pre * gate, axis=0, keepdims=True)
                total = part_sum if row == 1 else total + part_sum
            slope_ref[t, row] = slope.astype(BF)
        tiles += [total[:, :TILE], total[:, TILE:]]
    sums = jnp.concatenate(tiles + [jnp.zeros((8 - len(tiles), TILE), F32)], axis=0)
    for part in range(parts):
        sums_ref[part] = sums


def three_terms(value):
    high = value.astype(BF)
    rest = value - high.astype(F32)
    middle = rest.astype(BF)
    low = (rest - middle.astype(F32)).astype(BF)
    return jnp.concatenate([high, middle, low], axis=0)


def backward_kernel(
    parts, cells, info_ref, sums_ref, patch_ref, text_ref, second_ref, slope_ref, pick_ref, patch_w, near_w, *refs
):
    far_refs = refs[:-4]
    reward_ref, send_ref, views, acc = refs[-4:]
    n = PAIR_COLS
    lane = lax.broadcasted_iota(jnp.int32, (8, TILE), 1)

    by_side = []
    for side in range(2):
        total = sums_ref[side]
        for part in range(side + 2, parts, 2):
            total = total + sums_ref[part]
        by_side.append(total)
    rows = []
    for t in range(LT):
        even, odd = [total[2 * t : 2 * t + 2] for total in by_side]
        mixed = jnp.where(lane[:1] < TILE // 2, even[1:2], odd[1:2])
        rows.append(jnp.concatenate([even[0:1], odd[0:1], mixed], axis=1))
    pooled = jnp.concatenate(rows + [jnp.zeros((8 - LT, 3 * TILE), F32)], axis=0) / cells
    products = dot(three_terms(pooled), patch_ref[...])
    embedded = products[0:8] + products[8:16] + products[16:24]
    text = text_ref[...]
    text_length = jnp.sqrt(jnp.sum(text * text, axis=1, keepdims=True) + 1e-06)
    embed_square = jnp.sum(embedded * embedded, axis=1, keepdims=True) + 1e-06
    embed_length = jnp.sqrt(embed_square)
    along = jnp.sum(embedded * text, axis=1, keepdims=True)
    cosine = along / (embed_length * text_length)
    share = 100.0 / LT
    reward_ref[0] = share * (cosine[0, 0] + cosine[1, 0])
    embed_grad = share * (text / (embed_length * text_length) - cosine * embedded / embed_square)
    products = dot_nt(three_terms(embed_grad), patch_ref[...])
    pool_grad = (products[0:8] + products[8:16] + products[16:24]) / cells

    side = info_ref[0] % 2
    third = pool_grad[:, 2 * TILE :]
    turned = pltpu.roll(third, TILE // 2, 1)
    half = jnp.where((lane < TILE // 2) == (side == 0), third, turned)
    own_grad = jnp.concatenate([jnp.where(side == 0, pool_grad[:, :TILE], pool_grad[:, TILE : 2 * TILE]), half], axis=1)

    for row in range(6):
        for t in range(LT):
            grad = second_ref[t, row].astype(F32) * own_grad[t : t + 1]
            even, odd = grad[:n], grad[n:]
            store_views(
                views, t, row, even.astype(BF), odd.astype(BF), shift_down(odd).astype(BF), shift_up(even).astype(BF)
            )

    half_rows = 8 * n
    for b in range(3):
        field = views[:, 2 - b : 6 - b].reshape(2 * half_rows, 6 * TILE)
        for blocks, lanes in (([near_w], slice(0, DEEP)), (far_refs, slice(DEEP, 2 * DEEP))):
            now = dot_nt(field, jnp.concatenate([tap_weights(blocks, 9 + 3 * b + c) for c in (2, 1, 0)], axis=1))
            early = dot_nt(
                field[half_rows:], jnp.concatenate([tap_weights(blocks, 3 * b + c) for c in (2, 1, 0)], axis=1)
            )
            if b == 0:
                acc[:half_rows, lanes] = now[:half_rows] + early
                acc[half_rows:, lanes] = now[half_rows:]
            else:
                acc[:half_rows, lanes] += now[:half_rows] + early
                acc[half_rows:, lanes] += now[half_rows:]
    grad_first = (acc[...] * slope_ref[...]).astype(BF)
    tokens = []
    for t in range(LT):
        for g in range(2):
            base = (8 * t + 4 * g) * n
            planes = [grad_first[base + i * n : base + (i + 1) * n] for i in range(4)]
            tokens.append(jnp.concatenate(planes, axis=1))
    patch_grad = dot_nt(jnp.concatenate(tokens, axis=0), patch_w[1])
    early = dot_nt(jnp.concatenate(tokens[2:], axis=0), patch_w[0])
    patch_grad = jnp.concatenate([patch_grad[: 2 * n] + early, patch_grad[2 * n :]], axis=0)
    spread_out = dot_nt(patch_grad.astype(BF), pick_ref[...])
    half = spread_out.shape[1] // 9
    blocks = [[], [], []]
    for t in range(LT):
        parts_of = []
        for g in range(2):
            rows = spread_out[(2 * t + g) * n : (2 * t + g + 1) * n]
            for pair_row in range(3):
                base = 3 * pair_row * half
                parts_of.append(
                    shift_up(rows[:, base : base + half])
                    + rows[:, base + half : base + 2 * half]
                    + shift_down(rows[:, base + 2 * half : base + 3 * half])
                )
        up, first, first_down, second_up, second, down = parts_of
        blocks[0].append(first + second_up)
        blocks[1].append(second + first_down)
        blocks[2].append(up + down)
    result = jnp.concatenate([jnp.concatenate(block, axis=1) for block in blocks], axis=0).astype(BF)
    for part in range(parts):
        send_ref[part] = result


def token_kernel(parts, recv_ref, modulated_ref, tokens_ref, head_ref):
    n = PAIR_COLS
    lanes = recv_ref.shape[2]
    sums = [recv_ref[i].astype(F32) + recv_ref[i + 1].astype(F32) for i in range(0, parts, 2)]
    blank = jnp.zeros((n, lanes), F32)
    lower = lax.broadcasted_iota(jnp.int32, blank.shape, 1) // (lanes // 4) % 2 == 1
    rows = []
    for i, block in enumerate(sums):
        from_above = sums[i - 1][2 * n :] if i else blank
        from_below = sums[i + 1][2 * n :] if i + 1 < len(sums) else blank
        rows.append(block[:n] + jnp.where(lower, 0.0, from_above))
        rows.append(block[n : 2 * n] + jnp.where(lower, from_below, 0.0))
    wide = jnp.concatenate(rows, axis=0)
    tokens = jnp.concatenate([wide[:, : lanes // 2], wide[:, lanes // 2 :]], axis=0)
    flipped = jnp.transpose(tokens).astype(BF)
    tokens_ref[...] = tokens.astype(BF)
    head_ref[...] = dot(flipped, modulated_ref[...]).astype(BF)


def hidden_kernel(tokens_ref, head_ref, gain_ref, out_ref):
    out_ref[...] = (dot(tokens_ref[...], head_ref[...]) * gain_ref[...]).astype(BF)


VMEM = pl.BlockSpec(memory_space=pltpu.VMEM)
SMEM = pl.BlockSpec(memory_space=pltpu.SMEM)
HBM = pl.BlockSpec(memory_space=pltpu.HBM)


def exchange(block, axis, flip):
    count = lax.axis_size(axis)
    return lax.ppermute(block, axis, [(i, i ^ flip) for i in range(count)])


def spread(piece):
    blocks = {0: piece}
    flip = lax.axis_size("dp") // 4
    while flip:
        for held in list(blocks):
            blocks[held ^ flip] = exchange(blocks[held], "dp", flip)
        flip //= 2
    unit, rows = 1, piece.shape[1]
    while rows * unit % 16:
        low = (lax.axis_index("dp") // unit) % 2 == 0
        merged = {}
        for held in blocks:
            if held % (2 * unit) == 0:
                mine, other = blocks[held], blocks[held ^ unit]
                merged[held] = jnp.where(
                    low, jnp.concatenate([mine, other], axis=1), jnp.concatenate([other, mine], axis=1)
                )
        blocks, unit = merged, 2 * unit
    return [blocks[held] for held in sorted(blocks)], unit


def half_sum(term):
    total, flip = term.astype(F32), 1
    while flip < lax.axis_size("dp") // 2:
        other = exchange(term, "dp", flip)
        total = total + other.astype(F32)
        term, flip = total.astype(BF), 2 * flip
    return total


def local_channels(weight, unit):
    count = lax.axis_size("dp") // unit
    place = lax.axis_index("dp") // unit
    rows = weight.shape[2] // count
    blocks = [weight[..., i * rows : (i + 1) * rows] for i in range(count)]
    flip = count // 2
    while flip:
        swap = place // flip % 2 == 1
        blocks = [jnp.where(swap, blocks[i ^ flip], blocks[i]) for i in range(count)]
        flip //= 2
    spare = jnp.zeros(weight.shape[:2] + (DEEP - weight.shape[2] // 2,), weight.dtype)
    return jnp.concatenate(blocks[: count // 2] + [spare] + blocks[count // 2 :] + [spare], axis=2)


def body(hidden, mod_table, timestep, head_weight, conv_in, conv_mid, patch_weight, text_emb):
    parts = lax.axis_size("mp")
    groups = lax.axis_size("dp")
    tokens, depth = hidden.shape
    features = head_weight.shape[1]
    channels = features // 4
    width = conv_in.shape[2]
    n = PAIR_COLS
    pair_rows = tokens // (LT * n)
    cells = float(2 * pair_rows * LW)
    mp_index = lax.axis_index("mp")

    head_rows = head_weight.T
    taps = jnp.transpose(conv_mid, (1, 0, 2))
    rows = conv_mid.shape[0]
    far = groups // 2

    packed = pl.pallas_call(
        pack_kernel,
        in_specs=[HBM],
        out_specs=HBM,
        out_shape=jax.ShapeDtypeStruct((9, rows, width), BF),
        scratch_shapes=[
            pltpu.VMEM((9, rows, width), BF),
            pltpu.VMEM((2, 9, rows, TILE), BF),
            pltpu.SemaphoreType.DMA((3, 4)),
            pltpu.SemaphoreType.DMA((3,)),
        ],
        compiler_params=params(56),
        name="pack",
    )(taps)
    distant = exchange(packed, "dp", far)
    modulated, gain, send = pl.pallas_call(
        functools.partial(head_kernel, parts),
        in_specs=[SMEM] + [HBM] * 3,
        out_specs=[VMEM] * 3,
        out_shape=[
            jax.ShapeDtypeStruct((tokens, depth), BF),
            jax.ShapeDtypeStruct((1, depth), F32),
            jax.ShapeDtypeStruct((parts, 5 * n, 2 * features), BF),
        ],
        scratch_shapes=[
            pltpu.VMEM((tokens, depth), BF),
            pltpu.VMEM(mod_table.shape, BF),
            pltpu.VMEM((features, depth), BF),
            pltpu.SemaphoreType.DMA((3,)),
        ],
        compiler_params=params(56),
        name="head",
    )(timestep, hidden, mod_table, head_rows)
    send, conv_in = lax.optimization_barrier((send, conv_in))
    recv = lax.all_to_all(send, "mp", 0, 0, tiled=True)
    near_blocks, unit = spread(packed)
    recv, distant = lax.optimization_barrier((recv, distant))
    far_blocks, _ = spread(distant)
    blocks = len(near_blocks)
    info = jnp.reshape(mp_index, (1,)).astype(jnp.int32)
    taps_in = local_channels(jnp.transpose(conv_in[:, 9:], (1, 0, 2)), unit)
    pick = jnp.asarray(selection(channels))

    acc_shape = jax.ShapeDtypeStruct((24 * n, 2 * TILE), F32)
    views_shape = (LT, 8, 2 * n, 3 * DEEP)
    near_acc, far_views, slope, near_w, patch_w = pl.pallas_call(
        functools.partial(near_kernel, parts, blocks),
        in_specs=[SMEM, VMEM, VMEM, VMEM] + [HBM] * blocks,
        out_specs=[VMEM] * 5,
        out_shape=[
            acc_shape,
            jax.ShapeDtypeStruct(views_shape, BF),
            jax.ShapeDtypeStruct((16 * n, 2 * DEEP), F32),
            jax.ShapeDtypeStruct((9, width // 2, width), BF),
            jax.ShapeDtypeStruct((2, 16 * channels, 8 * DEEP), BF),
        ],
        scratch_shapes=[pltpu.VMEM(views_shape, BF), pltpu.SemaphoreType.DMA((blocks,))],
        cost_estimate=pl.CostEstimate(flops=4 * 10**9, bytes_accessed=10**7, transcendentals=10**6),
        compiler_params=params(20),
        name="near",
    )(info, recv, taps_in, pick, *near_blocks)
    sums, second_slope = pl.pallas_call(
        functools.partial(far_kernel, parts),
        in_specs=[SMEM] + [VMEM] * (2 + blocks),
        out_specs=[VMEM] * 2,
        out_shape=[
            jax.ShapeDtypeStruct((parts, 8, TILE), F32),
            jax.ShapeDtypeStruct((LT, 6, 2 * n, 2 * TILE), BF),
        ],
        scratch_shapes=[pltpu.VMEM(acc_shape.shape, F32)],
        compiler_params=params(16),
        name="far",
    )(info, near_acc, far_views, *far_blocks)
    all_sums = lax.all_to_all(sums, "mp", 0, 0, tiled=True)

    reward, contribution = pl.pallas_call(
        functools.partial(backward_kernel, parts, cells),
        in_specs=[SMEM] + [VMEM] * (8 + blocks),
        out_specs=[SMEM, VMEM],
        out_shape=[
            jax.ShapeDtypeStruct((1,), F32),
            jax.ShapeDtypeStruct((parts, 3 * n, 2 * features), BF),
        ],
        scratch_shapes=[pltpu.VMEM((LT, 6, 2 * n, 6 * TILE), BF), pltpu.VMEM((16 * n, 2 * DEEP), F32)],
        compiler_params=params(16),
        name="backward",
    )(info, all_sums, patch_weight, text_emb, second_slope, slope, pick, patch_w, near_w, *far_blocks)
    contributions = lax.all_to_all(contribution, "mp", 0, 0, tiled=True)

    token_grad, head_term = pl.pallas_call(
        functools.partial(token_kernel, parts),
        in_specs=[VMEM, VMEM],
        out_specs=[VMEM, VMEM],
        out_shape=[
            jax.ShapeDtypeStruct((tokens, features), BF),
            jax.ShapeDtypeStruct((features, depth), BF),
        ],
        compiler_params=params(8),
        name="token",
    )(contributions, modulated)
    from_far = exchange(head_term, "dp", far)
    hidden_grad = pl.pallas_call(
        hidden_kernel,
        in_specs=[VMEM] * 3,
        out_specs=VMEM,
        out_shape=jax.ShapeDtypeStruct((tokens, depth), BF),
        compiler_params=params(8),
        name="hidden_grad",
    )(token_grad, head_rows, gain)
    hidden_grad, from_far = lax.optimization_barrier((hidden_grad, from_far))
    head_grad = half_sum(head_term) + half_sum(from_far)
    return (reward, head_grad.T, hidden_grad)


def solution(mesh):
    in_specs = (
        P("dp", "mp"),
        P(None, None, "mp"),
        P("dp"),
        P("mp", None),
        P(),
        P("dp", None, None),
        P(),
        P("dp", None),
    )
    out_specs = (P("dp"), P("mp", None), P("dp", "mp"))
    return jax.shard_map(body, mesh=mesh, in_specs=in_specs, out_specs=out_specs, check_vma=False)
```

```python
import functools

import jax
import jax.numpy as jnp
import numpy as np
from jax import lax
from jax.experimental import pallas as pl
from jax.experimental.pallas import tpu as pltpu
from jax.sharding import PartitionSpec as P

LW = 64
LT = 2
DEEP = 256
TILE = 128
PAIR_COLS = LW // 2
BF = jnp.bfloat16
F32 = jnp.float32
MIB = 1024 * 1024


def params(mib):
    return pltpu.CompilerParams(vmem_limit_bytes=mib * MIB)


def sigmoid(value):
    return 1.0 / (1.0 + jnp.exp(-value))


def dot(left, right):
    return jnp.dot(left, right, preferred_element_type=F32)


def dot_nt(left, right):
    return lax.dot_general(left, right, (((1,), (1,)), ((), ())), preferred_element_type=F32)


def selection(channels):
    pick = np.zeros((3, 3, 2, 2, channels, 4, 4, channels), np.float32)
    for pair_row in range(3):
        for row in range(2):
            patch_row = 2 * (pair_row - 1) + row + 1
            for pair_col in range(3):
                for col in range(2):
                    patch_col = 2 * (pair_col - 1) + col + 1
                    if 0 <= patch_row < 4 and 0 <= patch_col < 4:
                        for k in range(channels):
                            pick[pair_row, pair_col, row, col, k, patch_row, patch_col, k] = 1.0
    return pick.reshape(36 * channels, 16 * channels).astype(BF)


def head_kernel(
    parts, step_ref, hidden_hbm, mod_hbm, head_hbm, taps_hbm, modulated_hbm, gain_ref, send_hbm, packed_hbm, hidden_ref,
    mod_ref, head_ref, modulated, blocks, packed, thirds, in_sems, out_sems, send_sems, tap_sems, packed_sems
):
    n = PAIR_COLS
    half = hidden_ref.shape[0] // LT
    frames = [pl.ds(t * half, half) for t in range(LT)]
    small = [
        pltpu.make_async_copy(mod_hbm, mod_ref, in_sems.at[0]),
        pltpu.make_async_copy(head_hbm, head_ref, in_sems.at[1]),
    ]
    large = [
        pltpu.make_async_copy(hidden_hbm.at[rows], hidden_ref.at[rows], in_sems.at[2 + t])
        for t, rows in enumerate(frames)
    ]
    results = [
        pltpu.make_async_copy(modulated.at[rows], modulated_hbm.at[rows], out_sems.at[t]) for t, rows in enumerate(frames)
    ]
    first = taps_hbm.shape[0] - 18
    odd = lax.axis_index("mp") % 2
    own = pl.ds(pl.multiple_of(odd * TILE, TILE), TILE)
    tap_copies, packed_results = [], []
    for chunk in range(3):
        pairs = pl.ds(3 * chunk, 3)
        ends = []
        for side in range(2):
            source = taps_hbm.at[pl.ds(first + 9 * side + 3 * chunk, 3)]
            ends.append((source.at[:, :, own], packed.at[pairs, :, pl.ds(side * TILE, TILE)]))
            ends.append((source.at[:, :, pl.ds(2 * TILE, TILE)], thirds.at[side, pairs]))
        tap_copies.append([pltpu.make_async_copy(*pair, tap_sems.at[chunk, i]) for i, pair in enumerate(ends)])
        packed_results.append(pltpu.make_async_copy(packed.at[pairs], packed_hbm.at[pairs], packed_sems.at[chunk]))
    for copy in small + large:
        copy.start()
    for chunk in tap_copies:
        for copy in chunk:
            copy.start()

    for copy in small:
        copy.wait()
    mod = mod_ref[step_ref[0]].astype(F32)
    gain = 1.0 + mod[1:2]
    gain_ref[...] = gain
    terms = []
    for t, rows in enumerate(frames):
        large[t].wait()
        values = (hidden_ref[rows].astype(F32) * gain + mod[0:1]).astype(BF)
        modulated[rows] = values
        results[t].start()
        terms.append(dot_nt(values, head_ref[...]))
    wide = jnp.concatenate(terms, axis=1)
    blank = jnp.zeros((n, wide.shape[1]), F32)
    lower = lax.broadcasted_iota(jnp.int32, blank.shape, 1) // (wide.shape[1] // 4) % 2 == 1

    def pair_row(i):
        return blank if i < 0 or i >= parts else wide[i * n : (i + 1) * n]

    for part in range(0, parts, 2):
        outer = jnp.where(lower, pair_row(part - 2), pair_row(part + 3))
        rows = [pair_row(part + i) for i in range(-1, 3)] + [outer]
        blocks[part // 2] = jnp.concatenate(rows, axis=0).astype(BF)
        for i in (part, part + 1):
            results.append(pltpu.make_async_copy(blocks.at[part // 2], send_hbm.at[i], send_sems.at[i]))
            results[-1].start()

    lane = lax.broadcasted_iota(jnp.int32, thirds.shape[2:], 1)
    for chunk in range(3):
        for copy in tap_copies[chunk]:
            copy.wait()
        for pair in range(3 * chunk, 3 * chunk + 3):
            left, right = thirds[0, pair].astype(F32), thirds[1, pair].astype(F32)
            left = jnp.where(odd == 0, left, pltpu.roll(left, TILE // 2, 1))
            right = jnp.where(odd == 0, pltpu.roll(right, TILE // 2, 1), right)
            packed[pair, :, 2 * TILE :] = jnp.where(lane < TILE // 2, left, right).astype(BF)
        packed_results[chunk].start()
    for result in results + packed_results:
        result.wait()


def build_patch_weights(conv_ref, patch_w):
    channels, width = conv_ref.shape[1], conv_ref.shape[2]
    patch_w[...] = jnp.zeros_like(patch_w)
    for a in range(2):
        for b in range(3):
            for c in range(3):
                tap = conv_ref[9 * a + 3 * b + c]
                for r in range(2):
                    for s in range(2):
                        row = ((r + b) * 4 + s + c) * channels
                        col = (2 * r + s) * width
                        patch_w[a, row : row + channels, col : col + width] = tap


def weight_copies(refs, weights, sems):
    rows = refs[0].shape[1]
    return [
        pltpu.make_async_copy(ref, weights.at[:, pl.ds(i * rows, rows), :], sems.at[i]) for i, ref in enumerate(refs)
    ]


def tap_weights(refs, tap):
    pair, side = tap % 9, tap // 9
    blocks = []
    for ref in refs:
        half = ref[pair, :, 2 * TILE :]
        lane = lax.broadcasted_iota(jnp.int32, half.shape, 1)
        half = jnp.where((lane < TILE // 2) == (side == 0), half, jnp.zeros_like(half))
        blocks.append(jnp.concatenate([ref[pair, :, side * TILE : (side + 1) * TILE], half], axis=1))
    filled = sum(block.shape[0] for block in blocks)
    return jnp.concatenate(blocks + [jnp.zeros((DEEP - filled, 2 * TILE), BF)], axis=0)


def store_views(views, t, row, even, odd, odd_down, even_up):
    n, deep = PAIR_COLS, even.shape[1]
    for c, (at_even, at_odd) in enumerate(((odd_down, even), (even, odd), (odd, even_up))):
        views[t, row, 0:n, c * deep : (c + 1) * deep] = at_even
        views[t, row, n : 2 * n, c * deep : (c + 1) * deep] = at_odd


def shift_down(value):
    place = lax.broadcasted_iota(jnp.int32, value.shape, 0) % PAIR_COLS
    return jnp.where(place == 0, 0.0, pltpu.roll(value, 1, 0))


def shift_up(value):
    place = lax.broadcasted_iota(jnp.int32, value.shape, 0) % PAIR_COLS
    return jnp.where(place == PAIR_COLS - 1, 0.0, pltpu.roll(value, value.shape[0] - 1, 0))


def near_kernel(parts, blocks, info_ref, recv_ref, conv_ref, pick_ref, *refs):
    acc, far_views, slope_ref, weights, patch_w, views, sems = refs[blocks:]
    copies = weight_copies(refs[:blocks], weights, sems)
    for copy in copies:
        copy.start()
    n = PAIR_COLS
    width = conv_ref.shape[2]
    build_patch_weights(conv_ref, patch_w)

    latent = recv_ref[0].astype(F32)
    for part in range(1, parts):
        latent = latent + recv_ref[part].astype(F32)
    latent = latent.astype(BF).astype(F32)
    left, right = shift_down(latent), shift_up(latent)
    half = latent.shape[1] // 2
    stacked = []
    for t in range(LT):
        lanes = slice(t * half, (t + 1) * half)
        cols = jnp.concatenate([left[:, lanes], latent[:, lanes], right[:, lanes]], axis=1)
        above = jnp.concatenate([cols[4 * n :], cols[: 3 * n]], axis=0)
        stacked.append(jnp.concatenate([above, cols[: 4 * n], cols[n:]], axis=1))
    patches = dot(jnp.concatenate(stacked, axis=0).astype(BF), pick_ref[...]).astype(BF)

    top_scale, bottom_scale = edge_scales(parts, info_ref[0])
    group = lax.broadcasted_iota(jnp.int32, (8 * n, 1), 0) // n % 4
    scale = jnp.where(group == 0, top_scale, jnp.where(group == 3, bottom_scale, 1.0))
    for r in range(2):
        lanes = slice(2 * r * width, (2 * r + 2) * width)
        pre = dot(patches, patch_w[1, :, lanes])
        late = dot(patches[: 4 * n], patch_w[0, :, lanes])
        pre = jnp.concatenate([pre[: 4 * n], pre[4 * n :] + late], axis=0)
        gate = sigmoid(pre)
        act = pre * gate * scale
        even, odd = act[:, :width], act[:, width:]
        odd_down, even_up = shift_down(odd).astype(BF), shift_up(even).astype(BF)
        even, odd = even.astype(BF), odd.astype(BF)
        for t in range(LT):
            for g in range(4):
                at = slice((4 * t + g) * n, (4 * t + g + 1) * n)
                for target, lanes in ((views, slice(0, DEEP)), (far_views, slice(DEEP, 2 * DEEP))):
                    store_views(
                        target, t, 2 * g + r, even[at, lanes], odd[at, lanes], odd_down[at, lanes], even_up[at, lanes]
                    )
            for g in (1, 2):
                at = slice((4 * t + g) * n, (4 * t + g + 1) * n)
                own, own_gate = pre[at], gate[at]
                slope = own_gate * (1.0 + own * (1.0 - own_gate))
                base = (4 * t + 2 * (g - 1) + r) * 2 * n
                slope_ref[base : base + n, :] = slope[:, :width]
                slope_ref[base + n : base + 2 * n, :] = slope[:, width:]

    for copy in copies:
        copy.wait()
    add_taps(views, [weights], acc, None)


def edge_scales(parts, mp_index):
    place = mp_index // 2
    return jnp.where(place == 0, 0.0, 1.0).astype(F32), jnp.where(place == parts // 2 - 1, 0.0, 1.0).astype(F32)


def add_taps(views, refs, acc, base):
    half_rows = acc.shape[0] // 2
    rows = half_rows // (2 * PAIR_COLS)
    for b in range(3):
        field = views[:, b : b + rows].reshape(2 * half_rows, 3 * DEEP)
        now = dot(field, jnp.concatenate([tap_weights(refs, 9 + 3 * b + c) for c in range(3)], axis=0))
        late = dot(field[:half_rows], jnp.concatenate([tap_weights(refs, 3 * b + c) for c in range(3)], axis=0))
        so_far = acc if b else base
        if so_far is None:
            acc[:half_rows] = now[:half_rows]
            acc[half_rows:] = now[half_rows:] + late
        else:
            acc[:half_rows] = so_far[:half_rows] + now[:half_rows]
            acc[half_rows:] = so_far[half_rows:] + (now[half_rows:] + late)


def far_kernel(parts, info_ref, near_ref, views, *refs):
    sums_ref, slope_ref, acc = refs[-3:]
    add_taps(views, refs[:-3], acc, near_ref)
    n = PAIR_COLS
    top_scale, bottom_scale = edge_scales(parts, info_ref[0])
    tiles = []
    for t in range(LT):
        for row in range(6):
            part = acc[(6 * t + row) * 2 * n : (6 * t + row + 1) * 2 * n]
            half = part[:, TILE:]
            pre = jnp.concatenate([part[:, :TILE], half + pltpu.roll(half, TILE // 2, 1)], axis=1)
            gate = sigmoid(pre)
            slope = gate * (1.0 + pre * (1.0 - gate))
            if row == 0:
                slope = slope * top_scale
            elif row == 5:
                slope = slope * bottom_scale
            else:
                part_sum = jnp.sum(pre * gate, axis=0, keepdims=True)
                total = part_sum if row == 1 else total + part_sum
            slope_ref[t, row] = slope.astype(BF)
        tiles += [total[:, :TILE], total[:, TILE:]]
    sums = jnp.concatenate(tiles + [jnp.zeros((8 - len(tiles), TILE), F32)], axis=0)
    for part in range(parts):
        sums_ref[part] = sums


def three_terms(value):
    high = value.astype(BF)
    rest = value - high.astype(F32)
    middle = rest.astype(BF)
    low = (rest - middle.astype(F32)).astype(BF)
    return jnp.concatenate([high, middle, low], axis=0)


def backward_kernel(
    parts, cells, info_ref, sums_ref, patch_ref, text_ref, second_ref, slope_ref, pick_ref, patch_w, near_w, *refs
):
    far_refs = refs[:-4]
    reward_ref, send_ref, views, acc = refs[-4:]
    n = PAIR_COLS
    lane = lax.broadcasted_iota(jnp.int32, (8, TILE), 1)

    by_side = []
    for side in range(2):
        total = sums_ref[side]
        for part in range(side + 2, parts, 2):
            total = total + sums_ref[part]
        by_side.append(total)
    rows = []
    for t in range(LT):
        even, odd = [total[2 * t : 2 * t + 2] for total in by_side]
        mixed = jnp.where(lane[:1] < TILE // 2, even[1:2], odd[1:2])
        rows.append(jnp.concatenate([even[0:1], odd[0:1], mixed], axis=1))
    pooled = jnp.concatenate(rows + [jnp.zeros((8 - LT, 3 * TILE), F32)], axis=0) / cells
    products = dot(three_terms(pooled), patch_ref[...])
    embedded = products[0:8] + products[8:16] + products[16:24]
    text = text_ref[...]
    text_length = jnp.sqrt(jnp.sum(text * text, axis=1, keepdims=True) + 1e-06)
    embed_square = jnp.sum(embedded * embedded, axis=1, keepdims=True) + 1e-06
    embed_length = jnp.sqrt(embed_square)
    along = jnp.sum(embedded * text, axis=1, keepdims=True)
    cosine = along / (embed_length * text_length)
    share = 100.0 / LT
    reward_ref[0] = share * (cosine[0, 0] + cosine[1, 0])
    embed_grad = share * (text / (embed_length * text_length) - cosine * embedded / embed_square)
    products = dot_nt(three_terms(embed_grad), patch_ref[...])
    pool_grad = (products[0:8] + products[8:16] + products[16:24]) / cells

    side = info_ref[0] % 2
    third = pool_grad[:, 2 * TILE :]
    turned = pltpu.roll(third, TILE // 2, 1)
    half = jnp.where((lane < TILE // 2) == (side == 0), third, turned)
    own_grad = jnp.concatenate([jnp.where(side == 0, pool_grad[:, :TILE], pool_grad[:, TILE : 2 * TILE]), half], axis=1)

    for row in range(6):
        for t in range(LT):
            grad = second_ref[t, row].astype(F32) * own_grad[t : t + 1]
            even, odd = grad[:n], grad[n:]
            store_views(
                views, t, row, even.astype(BF), odd.astype(BF), shift_down(odd).astype(BF), shift_up(even).astype(BF)
            )

    half_rows = 8 * n
    for b in range(3):
        field = views[:, 2 - b : 6 - b].reshape(2 * half_rows, 6 * TILE)
        for blocks, lanes in (([near_w], slice(0, DEEP)), (far_refs, slice(DEEP, 2 * DEEP))):
            now = dot_nt(field, jnp.concatenate([tap_weights(blocks, 9 + 3 * b + c) for c in (2, 1, 0)], axis=1))
            early = dot_nt(
                field[half_rows:], jnp.concatenate([tap_weights(blocks, 3 * b + c) for c in (2, 1, 0)], axis=1)
            )
            if b == 0:
                acc[:half_rows, lanes] = now[:half_rows] + early
                acc[half_rows:, lanes] = now[half_rows:]
            else:
                acc[:half_rows, lanes] += now[:half_rows] + early
                acc[half_rows:, lanes] += now[half_rows:]
    grad_first = (acc[...] * slope_ref[...]).astype(BF)
    tokens = []
    for t in range(LT):
        for g in range(2):
            base = (8 * t + 4 * g) * n
            planes = [grad_first[base + i * n : base + (i + 1) * n] for i in range(4)]
            tokens.append(jnp.concatenate(planes, axis=1))
    patch_grad = dot_nt(jnp.concatenate(tokens, axis=0), patch_w[1])
    early = dot_nt(jnp.concatenate(tokens[2:], axis=0), patch_w[0])
    patch_grad = jnp.concatenate([patch_grad[: 2 * n] + early, patch_grad[2 * n :]], axis=0)
    spread_out = dot_nt(patch_grad.astype(BF), pick_ref[...])
    half = spread_out.shape[1] // 9
    blocks = [[], [], []]
    for t in range(LT):
        parts_of = []
        for g in range(2):
            rows = spread_out[(2 * t + g) * n : (2 * t + g + 1) * n]
            for pair_row in range(3):
                base = 3 * pair_row * half
                parts_of.append(
                    shift_up(rows[:, base : base + half])
                    + rows[:, base + half : base + 2 * half]
                    + shift_down(rows[:, base + 2 * half : base + 3 * half])
                )
        up, first, first_down, second_up, second, down = parts_of
        blocks[0].append(first + second_up)
        blocks[1].append(second + first_down)
        blocks[2].append(up + down)
    result = jnp.concatenate([jnp.concatenate(block, axis=1) for block in blocks], axis=0).astype(BF)
    for part in range(parts):
        send_ref[part] = result


def token_kernel(parts, recv_ref, modulated_ref, tokens_ref, head_ref):
    n = PAIR_COLS
    lanes = recv_ref.shape[2]
    sums = [recv_ref[i].astype(F32) + recv_ref[i + 1].astype(F32) for i in range(0, parts, 2)]
    blank = jnp.zeros((n, lanes), F32)
    lower = lax.broadcasted_iota(jnp.int32, blank.shape, 1) // (lanes // 4) % 2 == 1
    rows = []
    for i, block in enumerate(sums):
        from_above = sums[i - 1][2 * n :] if i else blank
        from_below = sums[i + 1][2 * n :] if i + 1 < len(sums) else blank
        rows.append(block[:n] + jnp.where(lower, 0.0, from_above))
        rows.append(block[n : 2 * n] + jnp.where(lower, from_below, 0.0))
    wide = jnp.concatenate(rows, axis=0)
    tokens = jnp.concatenate([wide[:, : lanes // 2], wide[:, lanes // 2 :]], axis=0)
    flipped = jnp.transpose(tokens).astype(BF)
    tokens_ref[...] = tokens.astype(BF)
    head_ref[...] = dot(flipped, modulated_ref[...]).astype(BF)


def hidden_kernel(tokens_ref, head_ref, gain_ref, out_ref):
    out_ref[...] = (dot(tokens_ref[...], head_ref[...]) * gain_ref[...]).astype(BF)


VMEM = pl.BlockSpec(memory_space=pltpu.VMEM)
SMEM = pl.BlockSpec(memory_space=pltpu.SMEM)
HBM = pl.BlockSpec(memory_space=pltpu.HBM)


def exchange(block, axis, flip):
    count = lax.axis_size(axis)
    return lax.ppermute(block, axis, [(i, i ^ flip) for i in range(count)])


def spread(piece):
    blocks = {0: piece}
    flip = lax.axis_size("dp") // 4
    while flip:
        for held in list(blocks):
            blocks[held ^ flip] = exchange(blocks[held], "dp", flip)
        flip //= 2
    unit, rows = 1, piece.shape[1]
    while rows * unit % 16:
        low = (lax.axis_index("dp") // unit) % 2 == 0
        merged = {}
        for held in blocks:
            if held % (2 * unit) == 0:
                mine, other = blocks[held], blocks[held ^ unit]
                merged[held] = jnp.where(
                    low, jnp.concatenate([mine, other], axis=1), jnp.concatenate([other, mine], axis=1)
                )
        blocks, unit = merged, 2 * unit
    return [blocks[held] for held in sorted(blocks)], unit


def local_channels(weight, unit):
    count = lax.axis_size("dp") // unit
    place = lax.axis_index("dp") // unit
    rows = weight.shape[2] // count
    blocks = [weight[..., i * rows : (i + 1) * rows] for i in range(count)]
    flip = count // 2
    while flip:
        swap = place // flip % 2 == 1
        blocks = [jnp.where(swap, blocks[i ^ flip], blocks[i]) for i in range(count)]
        flip //= 2
    spare = jnp.zeros(weight.shape[:2] + (DEEP - weight.shape[2] // 2,), weight.dtype)
    return jnp.concatenate(blocks[: count // 2] + [spare] + blocks[count // 2 :] + [spare], axis=2)


def body(hidden, mod_table, timestep, head_weight, conv_in, conv_mid, patch_weight, text_emb):
    parts = lax.axis_size("mp")
    groups = lax.axis_size("dp")
    tokens, depth = hidden.shape
    features = head_weight.shape[1]
    channels = features // 4
    width = conv_in.shape[2]
    n = PAIR_COLS
    pair_rows = tokens // (LT * n)
    cells = float(2 * pair_rows * LW)
    mp_index = lax.axis_index("mp")

    head_rows = head_weight.T
    taps = jnp.transpose(conv_mid, (1, 0, 2))
    rows = conv_mid.shape[0]
    far = groups // 2

    modulated, gain, send, packed = pl.pallas_call(
        functools.partial(head_kernel, parts),
        in_specs=[SMEM] + [HBM] * 4,
        out_specs=[HBM, VMEM, HBM, HBM],
        out_shape=[
            jax.ShapeDtypeStruct((tokens, depth), BF),
            jax.ShapeDtypeStruct((1, depth), F32),
            jax.ShapeDtypeStruct((parts, 5 * n, 2 * features), BF),
            jax.ShapeDtypeStruct((9, rows, width), BF),
        ],
        scratch_shapes=[
            pltpu.VMEM((tokens, depth), BF),
            pltpu.VMEM(mod_table.shape, BF),
            pltpu.VMEM((features, depth), BF),
            pltpu.VMEM((tokens, depth), BF),
            pltpu.VMEM((parts // 2, 5 * n, 2 * features), BF),
            pltpu.VMEM((9, rows, width), BF),
            pltpu.VMEM((2, 9, rows, TILE), BF),
            pltpu.SemaphoreType.DMA((2 + LT,)),
            pltpu.SemaphoreType.DMA((LT,)),
            pltpu.SemaphoreType.DMA((parts,)),
            pltpu.SemaphoreType.DMA((3, 4)),
            pltpu.SemaphoreType.DMA((3,)),
        ],
        compiler_params=params(56),
        name="head",
    )(timestep, hidden, mod_table, head_rows, taps)
    distant = exchange(packed, "dp", far)
    send, conv_in = lax.optimization_barrier((send, conv_in))
    recv = lax.all_to_all(send, "mp", 0, 0, tiled=True)
    near_blocks, unit = spread(packed)
    blocks = len(near_blocks)
    info = jnp.reshape(mp_index, (1,)).astype(jnp.int32)
    taps_in = local_channels(jnp.transpose(conv_in[:, 9:], (1, 0, 2)), unit)
    pick = jnp.asarray(selection(channels))

    acc_shape = jax.ShapeDtypeStruct((24 * n, 2 * TILE), F32)
    views_shape = (LT, 8, 2 * n, 3 * DEEP)
    near_acc, far_views, slope, near_w, patch_w = pl.pallas_call(
        functools.partial(near_kernel, parts, blocks),
        in_specs=[SMEM, VMEM, VMEM, VMEM] + [HBM] * blocks,
        out_specs=[VMEM] * 5,
        out_shape=[
            acc_shape,
            jax.ShapeDtypeStruct(views_shape, BF),
            jax.ShapeDtypeStruct((16 * n, 2 * DEEP), F32),
            jax.ShapeDtypeStruct((9, width // 2, width), BF),
            jax.ShapeDtypeStruct((2, 16 * channels, 8 * DEEP), BF),
        ],
        scratch_shapes=[pltpu.VMEM(views_shape, BF), pltpu.SemaphoreType.DMA((blocks,))],
        compiler_params=params(20),
        name="near",
    )(info, recv, taps_in, pick, *near_blocks)
    near_acc, distant = lax.optimization_barrier((near_acc, distant))
    far_blocks, _ = spread(distant)
    sums, second_slope = pl.pallas_call(
        functools.partial(far_kernel, parts),
        in_specs=[SMEM] + [VMEM] * (2 + blocks),
        out_specs=[VMEM] * 2,
        out_shape=[
            jax.ShapeDtypeStruct((parts, 8, TILE), F32),
            jax.ShapeDtypeStruct((LT, 6, 2 * n, 2 * TILE), BF),
        ],
        scratch_shapes=[pltpu.VMEM(acc_shape.shape, F32)],
        compiler_params=params(16),
        name="far",
    )(info, near_acc, far_views, *far_blocks)
    all_sums = lax.all_to_all(sums, "mp", 0, 0, tiled=True)

    reward, contribution = pl.pallas_call(
        functools.partial(backward_kernel, parts, cells),
        in_specs=[SMEM] + [VMEM] * (8 + blocks),
        out_specs=[SMEM, VMEM],
        out_shape=[
            jax.ShapeDtypeStruct((1,), F32),
            jax.ShapeDtypeStruct((parts, 3 * n, 2 * features), BF),
        ],
        scratch_shapes=[pltpu.VMEM((LT, 6, 2 * n, 6 * TILE), BF), pltpu.VMEM((16 * n, 2 * DEEP), F32)],
        compiler_params=params(16),
        name="backward",
    )(info, all_sums, patch_weight, text_emb, second_slope, slope, pick, patch_w, near_w, *far_blocks)
    contributions = lax.all_to_all(contribution, "mp", 0, 0, tiled=True)

    token_grad, head_term = pl.pallas_call(
        functools.partial(token_kernel, parts),
        in_specs=[VMEM, VMEM],
        out_specs=[VMEM, VMEM],
        out_shape=[
            jax.ShapeDtypeStruct((tokens, features), BF),
            jax.ShapeDtypeStruct((features, depth), BF),
        ],
        compiler_params=params(8),
        name="token",
    )(contributions, modulated)
    flip = 1
    while flip < far:
        other = exchange(head_term, "dp", flip)
        head_term = (head_term.astype(F32) + other.astype(F32)).astype(BF)
        flip *= 2
    head_other = exchange(head_term, "dp", far)
    hidden_grad = pl.pallas_call(
        hidden_kernel,
        in_specs=[VMEM] * 3,
        out_specs=VMEM,
        out_shape=jax.ShapeDtypeStruct((tokens, depth), BF),
        compiler_params=params(8),
        name="hidden_grad",
    )(token_grad, head_rows, gain)
    head_grad = head_term.astype(F32) + head_other.astype(F32)
    return (reward, head_grad.T, hidden_grad)


def solution(mesh):
    in_specs = (
        P("dp", "mp"),
        P(None, None, "mp"),
        P("dp"),
        P("mp", None),
        P(),
        P("dp", None, None),
        P(),
        P("dp", None),
    )
    out_specs = (P("dp"), P("mp", None), P("dp", "mp"))
    return jax.shard_map(body, mesh=mesh, in_specs=in_specs, out_specs=out_specs, check_vma=False)
```

```python
import functools

import jax
import jax.numpy as jnp
import numpy as np
from jax import lax
from jax.experimental import pallas as pl
from jax.experimental.pallas import tpu as pltpu
from jax.sharding import PartitionSpec as P

LW = 64
LT = 2
DEEP = 256
TILE = 128
PAIR_COLS = LW // 2
BF = jnp.bfloat16
F32 = jnp.float32
MIB = 1024 * 1024


def params(mib):
    return pltpu.CompilerParams(vmem_limit_bytes=mib * MIB)


def sigmoid(value):
    return pl.reciprocal(1.0 + jnp.exp(-value), approx=True)


def dot(left, right):
    return jnp.dot(left, right, preferred_element_type=F32)


def dot_nt(left, right):
    return lax.dot_general(left, right, (((1,), (1,)), ((), ())), preferred_element_type=F32)


def selection(channels):
    pick = np.zeros((3, 3, 2, 2, channels, 4, 4, channels), np.float32)
    for pair_row in range(3):
        for row in range(2):
            patch_row = 2 * (pair_row - 1) + row + 1
            for pair_col in range(3):
                for col in range(2):
                    patch_col = 2 * (pair_col - 1) + col + 1
                    if 0 <= patch_row < 4 and 0 <= patch_col < 4:
                        for k in range(channels):
                            pick[pair_row, pair_col, row, col, k, patch_row, patch_col, k] = 1.0
    return pick.reshape(36 * channels, 16 * channels).astype(BF)


def pack_kernel(taps_hbm, packed, thirds, in_sems):
    first = taps_hbm.shape[0] - 18
    odd = lax.axis_index("mp") % 2
    own = pl.ds(pl.multiple_of(odd * TILE, TILE), TILE)
    copies = []
    for chunk in range(3):
        pairs = pl.ds(3 * chunk, 3)
        here = []
        for side in range(2):
            source = taps_hbm.at[pl.ds(first + 9 * side + 3 * chunk, 3)]
            here.append((source.at[:, :, own], packed.at[pairs, :, pl.ds(side * TILE, TILE)]))
            here.append((source.at[:, :, pl.ds(2 * TILE, TILE)], thirds.at[side, pairs]))
        copies.append([pltpu.make_async_copy(*ends, in_sems.at[chunk, i]) for i, ends in enumerate(here)])
    for chunk in range(3):
        for copy in copies[chunk]:
            copy.start()
    lane = lax.broadcasted_iota(jnp.int32, thirds.shape[2:], 1)
    for chunk in range(3):
        for copy in copies[chunk]:
            copy.wait()
        for pair in range(3 * chunk, 3 * chunk + 3):
            left, right = thirds[0, pair].astype(F32), thirds[1, pair].astype(F32)
            left = jnp.where(odd == 0, left, pltpu.roll(left, TILE // 2, 1))
            right = jnp.where(odd == 0, pltpu.roll(right, TILE // 2, 1), right)
            packed[pair, :, 2 * TILE :] = jnp.where(lane < TILE // 2, left, right).astype(BF)


def head_kernel(
    parts, step_ref, hidden_hbm, mod_hbm, head_hbm, modulated_ref, gain_ref, send_ref, hidden_ref, mod_ref, head_ref,
    sems
):
    copies = [
        pltpu.make_async_copy(hidden_hbm, hidden_ref, sems.at[0]),
        pltpu.make_async_copy(mod_hbm, mod_ref, sems.at[1]),
        pltpu.make_async_copy(head_hbm, head_ref, sems.at[2]),
    ]
    for copy in copies:
        copy.start()
    for copy in copies:
        copy.wait()
    mod = mod_ref[step_ref[0]].astype(F32)
    gain = 1.0 + mod[1:2]
    modulated = (hidden_ref[...].astype(F32) * gain + mod[0:1]).astype(BF)
    modulated_ref[...] = modulated
    gain_ref[...] = gain
    terms = dot_nt(modulated, head_ref[...])
    half = terms.shape[0] // 2
    wide = jnp.concatenate([terms[:half], terms[half:]], axis=1)
    n = PAIR_COLS
    blank = jnp.zeros((n, wide.shape[1]), F32)
    lower = lax.broadcasted_iota(jnp.int32, blank.shape, 1) // (wide.shape[1] // 4) % 2 == 1

    def pair_row(i):
        return blank if i < 0 or i >= parts else wide[i * n : (i + 1) * n]

    for part in range(0, parts, 2):
        outer = jnp.where(lower, pair_row(part - 2), pair_row(part + 3))
        rows = [pair_row(part + i) for i in range(-1, 3)] + [outer]
        block = jnp.concatenate(rows, axis=0).astype(BF)
        send_ref[part] = block
        send_ref[part + 1] = block


def build_patch_weights(conv_ref, patch_w):
    channels, width = conv_ref.shape[1], conv_ref.shape[2]
    patch_w[...] = jnp.zeros_like(patch_w)
    for a in range(2):
        for b in range(3):
            for c in range(3):
                tap = conv_ref[9 * a + 3 * b + c]
                for r in range(2):
                    for s in range(2):
                        row = ((r + b) * 4 + s + c) * channels
                        col = (2 * r + s) * width
                        patch_w[a, row : row + channels, col : col + width] = tap


def weight_copies(refs, weights, sems):
    rows = refs[0].shape[1]
    return [
        pltpu.make_async_copy(ref, weights.at[:, pl.ds(i * rows, rows), :], sems.at[i]) for i, ref in enumerate(refs)
    ]


def tap_weights(refs, tap):
    pair, side = tap % 9, tap // 9
    blocks = []
    for ref in refs:
        half = ref[pair, :, 2 * TILE :]
        lane = lax.broadcasted_iota(jnp.int32, half.shape, 1)
        half = half * jnp.where((lane < TILE // 2) == (side == 0), 1.0, 0.0).astype(BF)
        blocks.append(jnp.concatenate([ref[pair, :, side * TILE : (side + 1) * TILE], half], axis=1))
    filled = sum(block.shape[0] for block in blocks)
    return jnp.concatenate(blocks + [jnp.zeros((DEEP - filled, 2 * TILE), BF)], axis=0)


def store_views(views, t, row, even, odd, odd_down, even_up):
    n, deep = PAIR_COLS, even.shape[1]
    for c, (at_even, at_odd) in enumerate(((odd_down, even), (even, odd), (odd, even_up))):
        views[t, row, 0:n, c * deep : (c + 1) * deep] = at_even
        views[t, row, n : 2 * n, c * deep : (c + 1) * deep] = at_odd


def shift_down(value):
    place = lax.broadcasted_iota(jnp.int32, value.shape, 0) % PAIR_COLS
    return jnp.where(place == 0, 0.0, pltpu.roll(value, 1, 0))


def shift_up(value):
    place = lax.broadcasted_iota(jnp.int32, value.shape, 0) % PAIR_COLS
    return jnp.where(place == PAIR_COLS - 1, 0.0, pltpu.roll(value, value.shape[0] - 1, 0))


def near_kernel(parts, blocks, info_ref, recv_ref, conv_ref, pick_ref, *refs):
    acc, far_views, slope_ref, weights, patch_w, views, sems = refs[blocks:]
    copies = weight_copies(refs[:blocks], weights, sems)
    for copy in copies:
        copy.start()
    n = PAIR_COLS
    width = conv_ref.shape[2]
    build_patch_weights(conv_ref, patch_w)

    latent = recv_ref[0].astype(F32)
    for part in range(1, parts):
        latent = latent + recv_ref[part].astype(F32)
    latent = latent.astype(BF).astype(F32)
    left, right = shift_down(latent), shift_up(latent)
    half = latent.shape[1] // 2
    stacked = []
    for t in range(LT):
        lanes = slice(t * half, (t + 1) * half)
        cols = jnp.concatenate([left[:, lanes], latent[:, lanes], right[:, lanes]], axis=1)
        above = jnp.concatenate([cols[4 * n :], cols[: 3 * n]], axis=0)
        stacked.append(jnp.concatenate([above, cols[: 4 * n], cols[n:]], axis=1))
    patches = dot(jnp.concatenate(stacked, axis=0).astype(BF), pick_ref[...]).astype(BF)

    top_scale, bottom_scale = edge_scales(parts, info_ref[0])
    group = lax.broadcasted_iota(jnp.int32, (8 * n, 1), 0) // n % 4
    scale = jnp.where(group == 0, top_scale, jnp.where(group == 3, bottom_scale, 1.0))
    for r in range(2):
        lanes = slice(2 * r * width, (2 * r + 2) * width)
        pre = dot(patches, patch_w[1, :, lanes])
        late = dot(patches[: 4 * n], patch_w[0, :, lanes])
        pre = jnp.concatenate([pre[: 4 * n], pre[4 * n :] + late], axis=0)
        gate = sigmoid(pre)
        act = pre * gate * scale
        even, odd = act[:, :width], act[:, width:]
        odd_down, even_up = shift_down(odd).astype(BF), shift_up(even).astype(BF)
        even, odd = even.astype(BF), odd.astype(BF)
        for t in range(LT):
            for g in range(4):
                at = slice((4 * t + g) * n, (4 * t + g + 1) * n)
                for target, lanes in ((views, slice(0, DEEP)), (far_views, slice(DEEP, 2 * DEEP))):
                    store_views(
                        target, t, 2 * g + r, even[at, lanes], odd[at, lanes], odd_down[at, lanes], even_up[at, lanes]
                    )
            for g in (1, 2):
                at = slice((4 * t + g) * n, (4 * t + g + 1) * n)
                own, own_gate = pre[at], gate[at]
                slope = own_gate * (1.0 + own * (1.0 - own_gate))
                base = (4 * t + 2 * (g - 1) + r) * 2 * n
                slope_ref[base : base + n, :] = slope[:, :width]
                slope_ref[base + n : base + 2 * n, :] = slope[:, width:]

    for copy in copies:
        copy.wait()
    add_taps(views, [weights], acc, None)


def edge_scales(parts, mp_index):
    place = mp_index // 2
    return jnp.where(place == 0, 0.0, 1.0).astype(F32), jnp.where(place == parts // 2 - 1, 0.0, 1.0).astype(F32)


def add_taps(views, refs, acc, base):
    half_rows = acc.shape[0] // 2
    rows = half_rows // (2 * PAIR_COLS)
    for b in range(3):
        field = views[:, b : b + rows].reshape(2 * half_rows, 3 * DEEP)
        now = dot(field, jnp.concatenate([tap_weights(refs, 9 + 3 * b + c) for c in range(3)], axis=0))
        late = dot(field[:half_rows], jnp.concatenate([tap_weights(refs, 3 * b + c) for c in range(3)], axis=0))
        so_far = acc if b else base
        if so_far is None:
            acc[:half_rows] = now[:half_rows]
            acc[half_rows:] = now[half_rows:] + late
        else:
            acc[:half_rows] = so_far[:half_rows] + now[:half_rows]
            acc[half_rows:] = so_far[half_rows:] + (now[half_rows:] + late)


def far_kernel(parts, info_ref, near_ref, views, *refs):
    sums_ref, slope_ref, acc = refs[-3:]
    add_taps(views, refs[:-3], acc, near_ref)
    n = PAIR_COLS
    top_scale, bottom_scale = edge_scales(parts, info_ref[0])
    tiles = []
    for t in range(LT):
        for row in range(6):
            part = acc[(6 * t + row) * 2 * n : (6 * t + row + 1) * 2 * n]
            half = part[:, TILE:]
            pre = jnp.concatenate([part[:, :TILE], half + pltpu.roll(half, TILE // 2, 1)], axis=1)
            gate = sigmoid(pre)
            slope = gate * (1.0 + pre * (1.0 - gate))
            if row == 0:
                slope = slope * top_scale
            elif row == 5:
                slope = slope * bottom_scale
            else:
                part_sum = jnp.sum(pre * gate, axis=0, keepdims=True)
                total = part_sum if row == 1 else total + part_sum
            slope_ref[t, row] = slope.astype(BF)
        tiles += [total[:, :TILE], total[:, TILE:]]
    sums = jnp.concatenate(tiles + [jnp.zeros((8 - len(tiles), TILE), F32)], axis=0)
    for part in range(parts):
        sums_ref[part] = sums


def three_terms(value):
    high = value.astype(BF)
    rest = value - high.astype(F32)
    middle = rest.astype(BF)
    low = (rest - middle.astype(F32)).astype(BF)
    return jnp.concatenate([high, middle, low], axis=0)


def backward_kernel(
    parts, cells, info_ref, sums_ref, patch_ref, text_ref, second_ref, slope_ref, pick_ref, patch_w, near_w, *refs
):
    far_refs = refs[:-4]
    reward_ref, send_ref, views, acc = refs[-4:]
    n = PAIR_COLS
    lane = lax.broadcasted_iota(jnp.int32, (8, TILE), 1)

    by_side = []
    for side in range(2):
        total = sums_ref[side]
        for part in range(side + 2, parts, 2):
            total = total + sums_ref[part]
        by_side.append(total)
    rows = []
    for t in range(LT):
        even, odd = [total[2 * t : 2 * t + 2] for total in by_side]
        mixed = jnp.where(lane[:1] < TILE // 2, even[1:2], odd[1:2])
        rows.append(jnp.concatenate([even[0:1], odd[0:1], mixed], axis=1))
    pooled = jnp.concatenate(rows + [jnp.zeros((8 - LT, 3 * TILE), F32)], axis=0) / cells
    products = dot(three_terms(pooled), patch_ref[...])
    embedded = products[0:8] + products[8:16] + products[16:24]
    text = text_ref[...]
    text_length = jnp.sqrt(jnp.sum(text * text, axis=1, keepdims=True) + 1e-06)
    embed_square = jnp.sum(embedded * embedded, axis=1, keepdims=True) + 1e-06
    embed_length = jnp.sqrt(embed_square)
    along = jnp.sum(embedded * text, axis=1, keepdims=True)
    cosine = along / (embed_length * text_length)
    share = 100.0 / LT
    reward_ref[0] = share * (cosine[0, 0] + cosine[1, 0])
    embed_grad = share * (text / (embed_length * text_length) - cosine * embedded / embed_square)
    products = dot_nt(three_terms(embed_grad), patch_ref[...])
    pool_grad = (products[0:8] + products[8:16] + products[16:24]) / cells

    side = info_ref[0] % 2
    third = pool_grad[:, 2 * TILE :]
    turned = pltpu.roll(third, TILE // 2, 1)
    half = jnp.where((lane < TILE // 2) == (side == 0), third, turned)
    own_grad = jnp.concatenate([jnp.where(side == 0, pool_grad[:, :TILE], pool_grad[:, TILE : 2 * TILE]), half], axis=1)

    for row in range(6):
        for t in range(LT):
            grad = second_ref[t, row].astype(F32) * own_grad[t : t + 1]
            even, odd = grad[:n], grad[n:]
            store_views(
                views, t, row, even.astype(BF), odd.astype(BF), shift_down(odd).astype(BF), shift_up(even).astype(BF)
            )

    half_rows = 8 * n
    for b in range(3):
        field = views[:, 2 - b : 6 - b].reshape(2 * half_rows, 6 * TILE)
        for blocks, lanes in (([near_w], slice(0, DEEP)), (far_refs, slice(DEEP, 2 * DEEP))):
            now = dot_nt(field, jnp.concatenate([tap_weights(blocks, 9 + 3 * b + c) for c in (2, 1, 0)], axis=1))
            early = dot_nt(
                field[half_rows:], jnp.concatenate([tap_weights(blocks, 3 * b + c) for c in (2, 1, 0)], axis=1)
            )
            if b == 0:
                acc[:half_rows, lanes] = now[:half_rows] + early
                acc[half_rows:, lanes] = now[half_rows:]
            else:
                acc[:half_rows, lanes] += now[:half_rows] + early
                acc[half_rows:, lanes] += now[half_rows:]
    grad_first = (acc[...] * slope_ref[...]).astype(BF)
    tokens = []
    for t in range(LT):
        for g in range(2):
            base = (8 * t + 4 * g) * n
            planes = [grad_first[base + i * n : base + (i + 1) * n] for i in range(4)]
            tokens.append(jnp.concatenate(planes, axis=1))
    patch_grad = dot_nt(jnp.concatenate(tokens, axis=0), patch_w[1])
    early = dot_nt(jnp.concatenate(tokens[2:], axis=0), patch_w[0])
    patch_grad = jnp.concatenate([patch_grad[: 2 * n] + early, patch_grad[2 * n :]], axis=0)
    spread_out = dot_nt(patch_grad.astype(BF), pick_ref[...])
    half = spread_out.shape[1] // 9
    blocks = [[], [], []]
    for t in range(LT):
        parts_of = []
        for g in range(2):
            rows = spread_out[(2 * t + g) * n : (2 * t + g + 1) * n]
            for pair_row in range(3):
                base = 3 * pair_row * half
                parts_of.append(
                    shift_up(rows[:, base : base + half])
                    + rows[:, base + half : base + 2 * half]
                    + shift_down(rows[:, base + 2 * half : base + 3 * half])
                )
        up, first, first_down, second_up, second, down = parts_of
        blocks[0].append(first + second_up)
        blocks[1].append(second + first_down)
        blocks[2].append(up + down)
    result = jnp.concatenate([jnp.concatenate(block, axis=1) for block in blocks], axis=0).astype(BF)
    for part in range(parts):
        send_ref[part] = result


def token_kernel(parts, recv_ref, modulated_ref, tokens_ref, head_ref):
    n = PAIR_COLS
    lanes = recv_ref.shape[2]
    sums = [recv_ref[i].astype(F32) + recv_ref[i + 1].astype(F32) for i in range(0, parts, 2)]
    blank = jnp.zeros((n, lanes), F32)
    lower = lax.broadcasted_iota(jnp.int32, blank.shape, 1) // (lanes // 4) % 2 == 1
    rows = []
    for i, block in enumerate(sums):
        from_above = sums[i - 1][2 * n :] if i else blank
        from_below = sums[i + 1][2 * n :] if i + 1 < len(sums) else blank
        rows.append(block[:n] + jnp.where(lower, 0.0, from_above))
        rows.append(block[n : 2 * n] + jnp.where(lower, from_below, 0.0))
    wide = jnp.concatenate(rows, axis=0)
    tokens = jnp.concatenate([wide[:, : lanes // 2], wide[:, lanes // 2 :]], axis=0)
    flipped = jnp.transpose(tokens).astype(BF)
    tokens_ref[...] = tokens.astype(BF)
    head_ref[...] = dot(flipped, modulated_ref[...]).astype(BF)


def hidden_kernel(tokens_ref, head_ref, gain_ref, out_ref):
    out_ref[...] = (dot(tokens_ref[...], head_ref[...]) * gain_ref[...]).astype(BF)


VMEM = pl.BlockSpec(memory_space=pltpu.VMEM)
SMEM = pl.BlockSpec(memory_space=pltpu.SMEM)
HBM = pl.BlockSpec(memory_space=pltpu.HBM)


def exchange(block, axis, flip):
    count = lax.axis_size(axis)
    return lax.ppermute(block, axis, [(i, i ^ flip) for i in range(count)])


def spread(piece):
    blocks = {0: piece}
    flip = lax.axis_size("dp") // 4
    while flip:
        for held in list(blocks):
            blocks[held ^ flip] = exchange(blocks[held], "dp", flip)
        flip //= 2
    unit, rows = 1, piece.shape[1]
    while rows * unit % 16:
        low = (lax.axis_index("dp") // unit) % 2 == 0
        merged = {}
        for held in blocks:
            if held % (2 * unit) == 0:
                mine, other = blocks[held], blocks[held ^ unit]
                merged[held] = jnp.where(
                    low, jnp.concatenate([mine, other], axis=1), jnp.concatenate([other, mine], axis=1)
                )
        blocks, unit = merged, 2 * unit
    return [blocks[held] for held in sorted(blocks)], unit


def half_sum(term):
    total, flip = term.astype(F32), 1
    while flip < lax.axis_size("dp") // 2:
        other = exchange(term, "dp", flip)
        total = total + other.astype(F32)
        term, flip = total.astype(BF), 2 * flip
    return total


def local_channels(weight, unit):
    count = lax.axis_size("dp") // unit
    place = lax.axis_index("dp") // unit
    rows = weight.shape[2] // count
    blocks = [weight[..., i * rows : (i + 1) * rows] for i in range(count)]
    flip = count // 2
    while flip:
        swap = place // flip % 2 == 1
        blocks = [jnp.where(swap, blocks[i ^ flip], blocks[i]) for i in range(count)]
        flip //= 2
    spare = jnp.zeros(weight.shape[:2] + (DEEP - weight.shape[2] // 2,), weight.dtype)
    return jnp.concatenate(blocks[: count // 2] + [spare] + blocks[count // 2 :] + [spare], axis=2)


def body(hidden, mod_table, timestep, head_weight, conv_in, conv_mid, patch_weight, text_emb):
    parts = lax.axis_size("mp")
    groups = lax.axis_size("dp")
    tokens, depth = hidden.shape
    features = head_weight.shape[1]
    channels = features // 4
    width = conv_in.shape[2]
    n = PAIR_COLS
    pair_rows = tokens // (LT * n)
    cells = float(2 * pair_rows * LW)
    mp_index = lax.axis_index("mp")

    head_rows = head_weight.T
    taps = jnp.transpose(conv_mid, (1, 0, 2))
    rows = conv_mid.shape[0]
    far = groups // 2

    packed = pl.pallas_call(
        pack_kernel,
        in_specs=[HBM],
        out_specs=VMEM,
        out_shape=jax.ShapeDtypeStruct((9, rows, width), BF),
        scratch_shapes=[pltpu.VMEM((2, 9, rows, TILE), BF), pltpu.SemaphoreType.DMA((3, 4))],
        compiler_params=params(53),
        name="pack",
    )(taps)
    distant = exchange(packed, "dp", far)
    modulated, gain, send = pl.pallas_call(
        functools.partial(head_kernel, parts),
        in_specs=[SMEM] + [HBM] * 3,
        out_specs=[VMEM] * 3,
        out_shape=[
            jax.ShapeDtypeStruct((tokens, depth), BF),
            jax.ShapeDtypeStruct((1, depth), F32),
            jax.ShapeDtypeStruct((parts, 5 * n, 2 * features), BF),
        ],
        scratch_shapes=[
            pltpu.VMEM((tokens, depth), BF),
            pltpu.VMEM(mod_table.shape, BF),
            pltpu.VMEM((features, depth), BF),
            pltpu.SemaphoreType.DMA((3,)),
        ],
        compiler_params=params(56),
        name="head",
    )(timestep, hidden, mod_table, head_rows)
    send, conv_in = lax.optimization_barrier((send, conv_in))
    recv = lax.all_to_all(send, "mp", 0, 0, tiled=True)
    near_blocks, unit = spread(packed)
    recv, distant = lax.optimization_barrier((recv, distant))
    far_blocks, _ = spread(distant)
    blocks = len(near_blocks)
    info = jnp.reshape(mp_index, (1,)).astype(jnp.int32)
    taps_in = local_channels(jnp.transpose(conv_in[:, 9:], (1, 0, 2)), unit)
    pick = jnp.asarray(selection(channels))

    acc_shape = jax.ShapeDtypeStruct((24 * n, 2 * TILE), F32)
    views_shape = (LT, 8, 2 * n, 3 * DEEP)
    near_acc, far_views, slope, near_w, patch_w = pl.pallas_call(
        functools.partial(near_kernel, parts, blocks),
        in_specs=[SMEM, VMEM, VMEM, VMEM] + [HBM] * blocks,
        out_specs=[VMEM] * 5,
        out_shape=[
            acc_shape,
            jax.ShapeDtypeStruct(views_shape, BF),
            jax.ShapeDtypeStruct((16 * n, 2 * DEEP), F32),
            jax.ShapeDtypeStruct((9, width // 2, width), BF),
            jax.ShapeDtypeStruct((2, 16 * channels, 8 * DEEP), BF),
        ],
        scratch_shapes=[pltpu.VMEM(views_shape, BF), pltpu.SemaphoreType.DMA((blocks,))],
        cost_estimate=pl.CostEstimate(flops=4 * 10**9, bytes_accessed=10**7, transcendentals=10**6),
        compiler_params=params(20),
        name="near",
    )(info, recv, taps_in, pick, *near_blocks)
    sums, second_slope = pl.pallas_call(
        functools.partial(far_kernel, parts),
        in_specs=[SMEM] + [VMEM] * (2 + blocks),
        out_specs=[VMEM] * 2,
        out_shape=[
            jax.ShapeDtypeStruct((parts, 8, TILE), F32),
            jax.ShapeDtypeStruct((LT, 6, 2 * n, 2 * TILE), BF),
        ],
        scratch_shapes=[pltpu.VMEM(acc_shape.shape, F32)],
        compiler_params=params(16),
        name="far",
    )(info, near_acc, far_views, *far_blocks)
    all_sums = lax.all_to_all(sums, "mp", 0, 0, tiled=True)

    reward, contribution = pl.pallas_call(
        functools.partial(backward_kernel, parts, cells),
        in_specs=[SMEM] + [VMEM] * (8 + blocks),
        out_specs=[SMEM, VMEM],
        out_shape=[
            jax.ShapeDtypeStruct((1,), F32),
            jax.ShapeDtypeStruct((parts, 3 * n, 2 * features), BF),
        ],
        scratch_shapes=[pltpu.VMEM((LT, 6, 2 * n, 6 * TILE), BF), pltpu.VMEM((16 * n, 2 * DEEP), F32)],
        compiler_params=params(16),
        name="backward",
    )(info, all_sums, patch_weight, text_emb, second_slope, slope, pick, patch_w, near_w, *far_blocks)
    contributions = lax.all_to_all(contribution, "mp", 0, 0, tiled=True)

    token_grad, head_term = pl.pallas_call(
        functools.partial(token_kernel, parts),
        in_specs=[VMEM, VMEM],
        out_specs=[VMEM, VMEM],
        out_shape=[
            jax.ShapeDtypeStruct((tokens, features), BF),
            jax.ShapeDtypeStruct((features, depth), BF),
        ],
        compiler_params=params(8),
        name="token",
    )(contributions, modulated)
    from_far = exchange(head_term, "dp", far)
    hidden_grad = pl.pallas_call(
        hidden_kernel,
        in_specs=[VMEM] * 3,
        out_specs=VMEM,
        out_shape=jax.ShapeDtypeStruct((tokens, depth), BF),
        compiler_params=params(8),
        name="hidden_grad",
    )(token_grad, head_rows, gain)
    hidden_grad, from_far = lax.optimization_barrier((hidden_grad, from_far))
    head_grad = half_sum(head_term) + half_sum(from_far)
    return (reward, head_grad.T, hidden_grad)


def solution(mesh):
    in_specs = (
        P("dp", "mp"),
        P(None, None, "mp"),
        P("dp"),
        P("mp", None),
        P(),
        P("dp", None, None),
        P(),
        P("dp", None),
    )
    out_specs = (P("dp"), P("mp", None), P("dp", "mp"))
    return jax.shard_map(body, mesh=mesh, in_specs=in_specs, out_specs=out_specs, check_vma=False)
```

```python
import functools

import jax
import jax.numpy as jnp
import numpy as np
from jax import lax
from jax.experimental import pallas as pl
from jax.experimental.pallas import tpu as pltpu
from jax.sharding import PartitionSpec as P

LW = 64
LT = 2
DEEP = 256
TILE = 128
PAIR_COLS = LW // 2
BF = jnp.bfloat16
F32 = jnp.float32
MIB = 1024 * 1024


def params(mib):
    return pltpu.CompilerParams(vmem_limit_bytes=mib * MIB)


def sigmoid(value):
    return pl.reciprocal(1.0 + jnp.exp(-value), approx=True)


def dot(left, right):
    return jnp.dot(left, right, preferred_element_type=F32)


def dot_nt(left, right):
    return lax.dot_general(left, right, (((1,), (1,)), ((), ())), preferred_element_type=F32)


def selection(channels):
    pick = np.zeros((3, 3, 2, 2, channels, 4, 4, channels), np.float32)
    for pair_row in range(3):
        for row in range(2):
            patch_row = 2 * (pair_row - 1) + row + 1
            for pair_col in range(3):
                for col in range(2):
                    patch_col = 2 * (pair_col - 1) + col + 1
                    if 0 <= patch_row < 4 and 0 <= patch_col < 4:
                        for k in range(channels):
                            pick[pair_row, pair_col, row, col, k, patch_row, patch_col, k] = 1.0
    return pick.reshape(36 * channels, 16 * channels).astype(BF)


def pack_kernel(taps_hbm, packed, thirds, in_sems):
    first = taps_hbm.shape[0] - 18
    odd = lax.axis_index("mp") % 2
    own = pl.ds(pl.multiple_of(odd * TILE, TILE), TILE)
    copies = []
    for chunk in range(3):
        pairs = pl.ds(3 * chunk, 3)
        here = []
        for side in range(2):
            source = taps_hbm.at[pl.ds(first + 9 * side + 3 * chunk, 3)]
            here.append((source.at[:, :, own], packed.at[pairs, :, pl.ds(side * TILE, TILE)]))
            here.append((source.at[:, :, pl.ds(2 * TILE, TILE)], thirds.at[side, pairs]))
        copies.append([pltpu.make_async_copy(*ends, in_sems.at[chunk, i]) for i, ends in enumerate(here)])
    for chunk in range(3):
        for copy in copies[chunk]:
            copy.start()
    lane = lax.broadcasted_iota(jnp.int32, thirds.shape[2:], 1)
    for chunk in range(3):
        for copy in copies[chunk]:
            copy.wait()
        for pair in range(3 * chunk, 3 * chunk + 3):
            left, right = thirds[0, pair].astype(F32), thirds[1, pair].astype(F32)
            left = jnp.where(odd == 0, left, pltpu.roll(left, TILE // 2, 1))
            right = jnp.where(odd == 0, pltpu.roll(right, TILE // 2, 1), right)
            packed[pair, :, 2 * TILE :] = jnp.where(lane < TILE // 2, left, right).astype(BF)


def head_kernel(
    parts, step_ref, hidden_hbm, mod_hbm, head_hbm, modulated_ref, gain_ref, send_ref, hidden_ref, mod_ref, head_ref,
    sems
):
    copies = [
        pltpu.make_async_copy(hidden_hbm, hidden_ref, sems.at[0]),
        pltpu.make_async_copy(mod_hbm, mod_ref, sems.at[1]),
        pltpu.make_async_copy(head_hbm, head_ref, sems.at[2]),
    ]
    for copy in copies:
        copy.start()
    for copy in copies:
        copy.wait()
    mod = mod_ref[step_ref[0]].astype(F32)
    gain = 1.0 + mod[1:2]
    modulated = (hidden_ref[...].astype(F32) * gain + mod[0:1]).astype(BF)
    modulated_ref[...] = modulated
    gain_ref[...] = gain
    terms = dot_nt(modulated, head_ref[...])
    half = terms.shape[0] // 2
    wide = jnp.concatenate([terms[:half], terms[half:]], axis=1)
    n = PAIR_COLS
    blank = jnp.zeros((n, wide.shape[1]), F32)
    lower = lax.broadcasted_iota(jnp.int32, blank.shape, 1) // (wide.shape[1] // 4) % 2 == 1

    def pair_row(i):
        return blank if i < 0 or i >= parts else wide[i * n : (i + 1) * n]

    for part in range(0, parts, 2):
        outer = jnp.where(lower, pair_row(part - 2), pair_row(part + 3))
        rows = [pair_row(part + i) for i in range(-1, 3)] + [outer]
        block = jnp.concatenate(rows, axis=0).astype(BF)
        send_ref[part] = block
        send_ref[part + 1] = block


def build_patch_weights(conv_ref, patch_w):
    channels, width = conv_ref.shape[1], conv_ref.shape[2]
    patch_w[...] = jnp.zeros_like(patch_w)
    for a in range(2):
        for b in range(3):
            for c in range(3):
                tap = conv_ref[9 * a + 3 * b + c]
                for r in range(2):
                    for s in range(2):
                        row = ((r + b) * 4 + s + c) * channels
                        col = (2 * r + s) * width
                        patch_w[a, row : row + channels, col : col + width] = tap


def weight_copies(refs, weights, sems):
    rows = refs[0].shape[1]
    return [
        pltpu.make_async_copy(ref, weights.at[:, pl.ds(i * rows, rows), :], sems.at[i]) for i, ref in enumerate(refs)
    ]


def tap_weights(refs, tap):
    pair, side = tap % 9, tap // 9
    blocks = []
    for ref in refs:
        half = ref[pair, :, 2 * TILE :]
        lane = lax.broadcasted_iota(jnp.int32, half.shape, 1)
        half = half * jnp.where((lane < TILE // 2) == (side == 0), 1.0, 0.0).astype(BF)
        blocks.append(jnp.concatenate([ref[pair, :, side * TILE : (side + 1) * TILE], half], axis=1))
    filled = sum(block.shape[0] for block in blocks)
    return jnp.concatenate(blocks + [jnp.zeros((DEEP - filled, 2 * TILE), BF)], axis=0)


def store_views(views, t, row, even, odd, odd_down, even_up):
    n, deep = PAIR_COLS, even.shape[1]
    for c, (at_even, at_odd) in enumerate(((odd_down, even), (even, odd), (odd, even_up))):
        views[t, row, 0:n, c * deep : (c + 1) * deep] = at_even
        views[t, row, n : 2 * n, c * deep : (c + 1) * deep] = at_odd


def shift_down(value):
    place = lax.broadcasted_iota(jnp.int32, value.shape, 0) % PAIR_COLS
    return jnp.where(place == 0, 0.0, pltpu.roll(value, 1, 0))


def shift_up(value):
    place = lax.broadcasted_iota(jnp.int32, value.shape, 0) % PAIR_COLS
    return jnp.where(place == PAIR_COLS - 1, 0.0, pltpu.roll(value, value.shape[0] - 1, 0))


def near_kernel(parts, blocks, info_ref, recv_ref, conv_ref, pick_ref, *refs):
    acc, far_views, slope_ref, weights, patch_w, views, sems = refs[blocks:]
    copies = weight_copies(refs[:blocks], weights, sems)
    for copy in copies:
        copy.start()
    n = PAIR_COLS
    width = conv_ref.shape[2]
    build_patch_weights(conv_ref, patch_w)

    latent = recv_ref[0].astype(F32)
    for part in range(1, parts):
        latent = latent + recv_ref[part].astype(F32)
    latent = latent.astype(BF).astype(F32)
    left, right = shift_down(latent), shift_up(latent)
    half = latent.shape[1] // 2
    stacked = []
    for t in range(LT):
        lanes = slice(t * half, (t + 1) * half)
        cols = jnp.concatenate([left[:, lanes], latent[:, lanes], right[:, lanes]], axis=1)
        above = jnp.concatenate([cols[4 * n :], cols[: 3 * n]], axis=0)
        stacked.append(jnp.concatenate([above, cols[: 4 * n], cols[n:]], axis=1))
    patches = dot(jnp.concatenate(stacked, axis=0).astype(BF), pick_ref[...]).astype(BF)

    top_scale, bottom_scale = edge_scales(parts, info_ref[0])
    group = lax.broadcasted_iota(jnp.int32, (8 * n, 1), 0) // n % 4
    scale = jnp.where(group == 0, top_scale, jnp.where(group == 3, bottom_scale, 1.0))
    for r in range(2):
        lanes = slice(2 * r * width, (2 * r + 2) * width)
        pre = dot(patches, patch_w[1, :, lanes])
        late = dot(patches[: 4 * n], patch_w[0, :, lanes])
        pre = jnp.concatenate([pre[: 4 * n], pre[4 * n :] + late], axis=0)
        gate = sigmoid(pre)
        act = pre * gate * scale
        even, odd = act[:, :width], act[:, width:]
        odd_down, even_up = shift_down(odd).astype(BF), shift_up(even).astype(BF)
        even, odd = even.astype(BF), odd.astype(BF)
        for t in range(LT):
            for g in range(4):
                at = slice((4 * t + g) * n, (4 * t + g + 1) * n)
                for target, lanes in ((views, slice(0, DEEP)), (far_views, slice(DEEP, 2 * DEEP))):
                    store_views(
                        target, t, 2 * g + r, even[at, lanes], odd[at, lanes], odd_down[at, lanes], even_up[at, lanes]
                    )
            for g in (1, 2):
                at = slice((4 * t + g) * n, (4 * t + g + 1) * n)
                own, own_gate = pre[at], gate[at]
                slope = own_gate * (1.0 + own * (1.0 - own_gate))
                base = (4 * t + 2 * (g - 1) + r) * 2 * n
                slope_ref[base : base + n, :] = slope[:, :width]
                slope_ref[base + n : base + 2 * n, :] = slope[:, width:]

    for copy in copies:
        copy.wait()
    add_taps(views, [weights], acc, None)


def edge_scales(parts, mp_index):
    place = mp_index // 2
    return jnp.where(place == 0, 0.0, 1.0).astype(F32), jnp.where(place == parts // 2 - 1, 0.0, 1.0).astype(F32)


def add_taps(views, refs, acc, base):
    half_rows = acc.shape[0] // 2
    rows = half_rows // (2 * PAIR_COLS)
    for b in range(3):
        field = views[:, b : b + rows].reshape(2 * half_rows, 3 * DEEP)
        now = dot(field, jnp.concatenate([tap_weights(refs, 9 + 3 * b + c) for c in range(3)], axis=0))
        late = dot(field[:half_rows], jnp.concatenate([tap_weights(refs, 3 * b + c) for c in range(3)], axis=0))
        so_far = acc if b else base
        if so_far is None:
            acc[:half_rows] = now[:half_rows]
            acc[half_rows:] = now[half_rows:] + late
        else:
            acc[:half_rows] = so_far[:half_rows] + now[:half_rows]
            acc[half_rows:] = so_far[half_rows:] + (now[half_rows:] + late)


def far_kernel(parts, info_ref, near_ref, views, *refs):
    sums_ref, slope_ref, acc = refs[-3:]
    add_taps(views, refs[:-3], acc, near_ref)
    n = PAIR_COLS
    top_scale, bottom_scale = edge_scales(parts, info_ref[0])
    tiles = []
    for t in range(LT):
        for row in range(6):
            part = acc[(6 * t + row) * 2 * n : (6 * t + row + 1) * 2 * n]
            half = part[:, TILE:]
            pre = jnp.concatenate([part[:, :TILE], half + pltpu.roll(half, TILE // 2, 1)], axis=1)
            gate = sigmoid(pre)
            slope = gate * (1.0 + pre * (1.0 - gate))
            if row == 0:
                slope = slope * top_scale
            elif row == 5:
                slope = slope * bottom_scale
            else:
                part_sum = jnp.sum(pre * gate, axis=0, keepdims=True)
                total = part_sum if row == 1 else total + part_sum
            slope_ref[t, row] = slope.astype(BF)
        tiles += [total[:, :TILE], total[:, TILE:]]
    sums = jnp.concatenate(tiles + [jnp.zeros((8 - len(tiles), TILE), F32)], axis=0)
    for part in range(parts):
        sums_ref[part] = sums


def three_terms(value):
    high = value.astype(BF)
    rest = value - high.astype(F32)
    middle = rest.astype(BF)
    low = (rest - middle.astype(F32)).astype(BF)
    return jnp.concatenate([high, middle, low], axis=0)


def backward_kernel(
    parts, cells, info_ref, sums_ref, patch_ref, text_ref, second_ref, slope_ref, pick_ref, patch_w, near_w, *refs
):
    far_refs = refs[:-4]
    reward_ref, send_ref, views, acc = refs[-4:]
    n = PAIR_COLS
    lane = lax.broadcasted_iota(jnp.int32, (8, TILE), 1)

    by_side = []
    for side in range(2):
        total = sums_ref[side]
        for part in range(side + 2, parts, 2):
            total = total + sums_ref[part]
        by_side.append(total)
    rows = []
    for t in range(LT):
        even, odd = [total[2 * t : 2 * t + 2] for total in by_side]
        mixed = jnp.where(lane[:1] < TILE // 2, even[1:2], odd[1:2])
        rows.append(jnp.concatenate([even[0:1], odd[0:1], mixed], axis=1))
    pooled = jnp.concatenate(rows + [jnp.zeros((8 - LT, 3 * TILE), F32)], axis=0) / cells
    products = dot(three_terms(pooled), patch_ref[...])
    embedded = products[0:8] + products[8:16] + products[16:24]
    text = text_ref[...]
    text_length = jnp.sqrt(jnp.sum(text * text, axis=1, keepdims=True) + 1e-06)
    embed_square = jnp.sum(embedded * embedded, axis=1, keepdims=True) + 1e-06
    embed_length = jnp.sqrt(embed_square)
    along = jnp.sum(embedded * text, axis=1, keepdims=True)
    cosine = along / (embed_length * text_length)
    share = 100.0 / LT
    reward_ref[0] = share * (cosine[0, 0] + cosine[1, 0])
    embed_grad = share * (text / (embed_length * text_length) - cosine * embedded / embed_square)
    products = dot_nt(three_terms(embed_grad), patch_ref[...])
    pool_grad = (products[0:8] + products[8:16] + products[16:24]) / cells

    side = info_ref[0] % 2
    third = pool_grad[:, 2 * TILE :]
    turned = pltpu.roll(third, TILE // 2, 1)
    half = jnp.where((lane < TILE // 2) == (side == 0), third, turned)
    own_grad = jnp.concatenate([jnp.where(side == 0, pool_grad[:, :TILE], pool_grad[:, TILE : 2 * TILE]), half], axis=1)

    for row in range(6):
        for t in range(LT):
            grad = second_ref[t, row].astype(F32) * own_grad[t : t + 1]
            even, odd = grad[:n], grad[n:]
            store_views(
                views, t, row, even.astype(BF), odd.astype(BF), shift_down(odd).astype(BF), shift_up(even).astype(BF)
            )

    half_rows = 8 * n
    for b in range(3):
        field = views[:, 2 - b : 6 - b].reshape(2 * half_rows, 6 * TILE)
        for blocks, lanes in (([near_w], slice(0, DEEP)), (far_refs, slice(DEEP, 2 * DEEP))):
            now = dot_nt(field, jnp.concatenate([tap_weights(blocks, 9 + 3 * b + c) for c in (2, 1, 0)], axis=1))
            early = dot_nt(
                field[half_rows:], jnp.concatenate([tap_weights(blocks, 3 * b + c) for c in (2, 1, 0)], axis=1)
            )
            if b == 0:
                acc[:half_rows, lanes] = now[:half_rows] + early
                acc[half_rows:, lanes] = now[half_rows:]
            else:
                acc[:half_rows, lanes] += now[:half_rows] + early
                acc[half_rows:, lanes] += now[half_rows:]
    grad_first = (acc[...] * slope_ref[...]).astype(BF)
    tokens = []
    for t in range(LT):
        for g in range(2):
            base = (8 * t + 4 * g) * n
            planes = [grad_first[base + i * n : base + (i + 1) * n] for i in range(4)]
            tokens.append(jnp.concatenate(planes, axis=1))
    patch_grad = dot_nt(jnp.concatenate(tokens, axis=0), patch_w[1])
    early = dot_nt(jnp.concatenate(tokens[2:], axis=0), patch_w[0])
    patch_grad = jnp.concatenate([patch_grad[: 2 * n] + early, patch_grad[2 * n :]], axis=0)
    spread_out = dot_nt(patch_grad.astype(BF), pick_ref[...])
    half = spread_out.shape[1] // 9
    blocks = [[], [], []]
    for t in range(LT):
        parts_of = []
        for g in range(2):
            rows = spread_out[(2 * t + g) * n : (2 * t + g + 1) * n]
            for pair_row in range(3):
                base = 3 * pair_row * half
                parts_of.append(
                    shift_up(rows[:, base : base + half])
                    + rows[:, base + half : base + 2 * half]
                    + shift_down(rows[:, base + 2 * half : base + 3 * half])
                )
        up, first, first_down, second_up, second, down = parts_of
        blocks[0].append(first + second_up)
        blocks[1].append(second + first_down)
        blocks[2].append(up + down)
    result = jnp.concatenate([jnp.concatenate(block, axis=1) for block in blocks], axis=0).astype(BF)
    for part in range(parts):
        send_ref[part] = result


def token_kernel(parts, recv_ref, modulated_ref, tokens_ref, head_ref):
    n = PAIR_COLS
    lanes = recv_ref.shape[2]
    sums = [recv_ref[i].astype(F32) + recv_ref[i + 1].astype(F32) for i in range(0, parts, 2)]
    blank = jnp.zeros((n, lanes), F32)
    lower = lax.broadcasted_iota(jnp.int32, blank.shape, 1) // (lanes // 4) % 2 == 1
    rows = []
    for i, block in enumerate(sums):
        from_above = sums[i - 1][2 * n :] if i else blank
        from_below = sums[i + 1][2 * n :] if i + 1 < len(sums) else blank
        rows.append(block[:n] + jnp.where(lower, 0.0, from_above))
        rows.append(block[n : 2 * n] + jnp.where(lower, from_below, 0.0))
    wide = jnp.concatenate(rows, axis=0)
    tokens = jnp.concatenate([wide[:, : lanes // 2], wide[:, lanes // 2 :]], axis=0)
    flipped = jnp.transpose(tokens).astype(BF)
    tokens_ref[...] = tokens.astype(BF)
    head_ref[...] = dot(flipped, modulated_ref[...]).astype(BF)


def hidden_kernel(tokens_ref, head_ref, gain_ref, out_ref):
    out_ref[...] = (dot(tokens_ref[...], head_ref[...]) * gain_ref[...]).astype(BF)


VMEM = pl.BlockSpec(memory_space=pltpu.VMEM)
SMEM = pl.BlockSpec(memory_space=pltpu.SMEM)
HBM = pl.BlockSpec(memory_space=pltpu.HBM)


def exchange(block, axis, flip):
    count = lax.axis_size(axis)
    return lax.ppermute(block, axis, [(i, i ^ flip) for i in range(count)])


def spread(piece):
    blocks = {0: piece}
    flip = lax.axis_size("dp") // 4
    while flip:
        for held in list(blocks):
            blocks[held ^ flip] = exchange(blocks[held], "dp", flip)
        flip //= 2
    unit, rows = 1, piece.shape[1]
    while rows * unit % 16:
        low = (lax.axis_index("dp") // unit) % 2 == 0
        merged = {}
        for held in blocks:
            if held % (2 * unit) == 0:
                mine, other = blocks[held], blocks[held ^ unit]
                merged[held] = jnp.where(
                    low, jnp.concatenate([mine, other], axis=1), jnp.concatenate([other, mine], axis=1)
                )
        blocks, unit = merged, 2 * unit
    return [blocks[held] for held in sorted(blocks)], unit


def local_channels(weight, unit):
    count = lax.axis_size("dp") // unit
    place = lax.axis_index("dp") // unit
    rows = weight.shape[2] // count
    blocks = [weight[..., i * rows : (i + 1) * rows] for i in range(count)]
    flip = count // 2
    while flip:
        swap = place // flip % 2 == 1
        blocks = [jnp.where(swap, blocks[i ^ flip], blocks[i]) for i in range(count)]
        flip //= 2
    spare = jnp.zeros(weight.shape[:2] + (DEEP - weight.shape[2] // 2,), weight.dtype)
    return jnp.concatenate(blocks[: count // 2] + [spare] + blocks[count // 2 :] + [spare], axis=2)


def body(hidden, mod_table, timestep, head_weight, conv_in, conv_mid, patch_weight, text_emb):
    parts = lax.axis_size("mp")
    groups = lax.axis_size("dp")
    tokens, depth = hidden.shape
    features = head_weight.shape[1]
    channels = features // 4
    width = conv_in.shape[2]
    n = PAIR_COLS
    pair_rows = tokens // (LT * n)
    cells = float(2 * pair_rows * LW)
    mp_index = lax.axis_index("mp")

    head_rows = head_weight.T
    taps = jnp.transpose(conv_mid, (1, 0, 2))
    rows = conv_mid.shape[0]
    far = groups // 2

    packed = pl.pallas_call(
        pack_kernel,
        in_specs=[HBM],
        out_specs=VMEM,
        out_shape=jax.ShapeDtypeStruct((9, rows, width), BF),
        scratch_shapes=[pltpu.VMEM((2, 9, rows, TILE), BF), pltpu.SemaphoreType.DMA((3, 4))],
        compiler_params=params(53),
        name="pack",
    )(taps)
    distant = exchange(packed, "dp", far)
    modulated, gain, send = pl.pallas_call(
        functools.partial(head_kernel, parts),
        in_specs=[SMEM] + [HBM] * 3,
        out_specs=[VMEM] * 3,
        out_shape=[
            jax.ShapeDtypeStruct((tokens, depth), BF),
            jax.ShapeDtypeStruct((1, depth), F32),
            jax.ShapeDtypeStruct((parts, 5 * n, 2 * features), BF),
        ],
        scratch_shapes=[
            pltpu.VMEM((tokens, depth), BF),
            pltpu.VMEM(mod_table.shape, BF),
            pltpu.VMEM((features, depth), BF),
            pltpu.SemaphoreType.DMA((3,)),
        ],
        compiler_params=params(56),
        name="head",
    )(timestep, hidden, mod_table, head_rows)
    send, conv_in = lax.optimization_barrier((send, conv_in))
    recv = lax.all_to_all(send, "mp", 0, 0, tiled=True)
    near_blocks, unit = spread(packed)
    recv, distant = lax.optimization_barrier((recv, distant))
    far_blocks, _ = spread(distant)
    blocks = len(near_blocks)
    info = jnp.reshape(mp_index, (1,)).astype(jnp.int32)
    taps_in = local_channels(jnp.transpose(conv_in[:, 9:], (1, 0, 2)), unit)
    pick = jnp.asarray(selection(channels))

    acc_shape = jax.ShapeDtypeStruct((24 * n, 2 * TILE), F32)
    views_shape = (LT, 8, 2 * n, 3 * DEEP)
    near_acc, far_views, slope, near_w, patch_w = pl.pallas_call(
        functools.partial(near_kernel, parts, blocks),
        in_specs=[SMEM, VMEM, VMEM, VMEM] + [HBM] * blocks,
        out_specs=[VMEM] * 5,
        out_shape=[
            acc_shape,
            jax.ShapeDtypeStruct(views_shape, BF),
            jax.ShapeDtypeStruct((16 * n, 2 * DEEP), F32),
            jax.ShapeDtypeStruct((9, width // 2, width), BF),
            jax.ShapeDtypeStruct((2, 16 * channels, 8 * DEEP), BF),
        ],
        scratch_shapes=[pltpu.VMEM(views_shape, BF), pltpu.SemaphoreType.DMA((blocks,))],
        cost_estimate=pl.CostEstimate(flops=4 * 10**9, bytes_accessed=10**7, transcendentals=10**6),
        compiler_params=params(20),
        name="near",
    )(info, recv, taps_in, pick, *near_blocks)
    sums, second_slope = pl.pallas_call(
        functools.partial(far_kernel, parts),
        in_specs=[SMEM] + [VMEM] * (2 + blocks),
        out_specs=[VMEM] * 2,
        out_shape=[
            jax.ShapeDtypeStruct((parts, 8, TILE), F32),
            jax.ShapeDtypeStruct((LT, 6, 2 * n, 2 * TILE), BF),
        ],
        scratch_shapes=[pltpu.VMEM(acc_shape.shape, F32)],
        compiler_params=params(16),
        name="far",
    )(info, near_acc, far_views, *far_blocks)
    all_sums = lax.all_to_all(sums, "mp", 0, 0, tiled=True)

    reward, contribution = pl.pallas_call(
        functools.partial(backward_kernel, parts, cells),
        in_specs=[SMEM] + [VMEM] * (8 + blocks),
        out_specs=[SMEM, VMEM],
        out_shape=[
            jax.ShapeDtypeStruct((1,), F32),
            jax.ShapeDtypeStruct((parts, 3 * n, 2 * features), BF),
        ],
        scratch_shapes=[pltpu.VMEM((LT, 6, 2 * n, 6 * TILE), BF), pltpu.VMEM((16 * n, 2 * DEEP), F32)],
        compiler_params=params(16),
        name="backward",
    )(info, all_sums, patch_weight, text_emb, second_slope, slope, pick, patch_w, near_w, *far_blocks)
    contributions = lax.all_to_all(contribution, "mp", 0, 0, tiled=True)

    token_grad, head_term = pl.pallas_call(
        functools.partial(token_kernel, parts),
        in_specs=[VMEM, VMEM],
        out_specs=[VMEM, VMEM],
        out_shape=[
            jax.ShapeDtypeStruct((tokens, features), BF),
            jax.ShapeDtypeStruct((features, depth), BF),
        ],
        compiler_params=params(8),
        name="token",
    )(contributions, modulated)
    flip = 1
    while flip < far:
        other = exchange(head_term, "dp", flip)
        head_term = (head_term.astype(F32) + other.astype(F32)).astype(BF)
        flip *= 2
    head_other = exchange(head_term, "dp", far)
    hidden_grad = pl.pallas_call(
        hidden_kernel,
        in_specs=[VMEM] * 3,
        out_specs=VMEM,
        out_shape=jax.ShapeDtypeStruct((tokens, depth), BF),
        compiler_params=params(8),
        name="hidden_grad",
    )(token_grad, head_rows, gain)
    head_grad = head_term.astype(F32) + head_other.astype(F32)
    return (reward, head_grad.T, hidden_grad)


def solution(mesh):
    in_specs = (
        P("dp", "mp"),
        P(None, None, "mp"),
        P("dp"),
        P("mp", None),
        P(),
        P("dp", None, None),
        P(),
        P("dp", None),
    )
    out_specs = (P("dp"), P("mp", None), P("dp", "mp"))
    return jax.shard_map(body, mesh=mesh, in_specs=in_specs, out_specs=out_specs, check_vma=False)
```

```python
import functools

import jax
import jax.numpy as jnp
import numpy as np
from jax import lax
from jax.experimental import pallas as pl
from jax.experimental.pallas import tpu as pltpu
from jax.sharding import PartitionSpec as P

LW = 64
LT = 2
DEEP = 256
TILE = 128
PAIR_COLS = LW // 2
BF = jnp.bfloat16
F32 = jnp.float32
MIB = 1024 * 1024


def params(mib):
    return pltpu.CompilerParams(vmem_limit_bytes=mib * MIB)


def sigmoid(value):
    return pl.reciprocal(1.0 + jnp.exp(-value), approx=True)


def dot(left, right):
    return jnp.dot(left, right, preferred_element_type=F32)


def dot_nt(left, right):
    return lax.dot_general(left, right, (((1,), (1,)), ((), ())), preferred_element_type=F32)


def selection(channels):
    pick = np.zeros((3, 3, 2, 2, channels, 4, 4, channels), np.float32)
    for pair_row in range(3):
        for row in range(2):
            patch_row = 2 * (pair_row - 1) + row + 1
            for pair_col in range(3):
                for col in range(2):
                    patch_col = 2 * (pair_col - 1) + col + 1
                    if 0 <= patch_row < 4 and 0 <= patch_col < 4:
                        for k in range(channels):
                            pick[pair_row, pair_col, row, col, k, patch_row, patch_col, k] = 1.0
    return pick.reshape(36 * channels, 16 * channels).astype(BF)


def pack_kernel(taps_hbm, packed, thirds, in_sems):
    first = taps_hbm.shape[0] - 18
    odd = lax.axis_index("mp") % 2
    own = pl.ds(pl.multiple_of(odd * TILE, TILE), TILE)
    copies = []
    for chunk in range(3):
        pairs = pl.ds(3 * chunk, 3)
        here = []
        for side in range(2):
            source = taps_hbm.at[pl.ds(first + 9 * side + 3 * chunk, 3)]
            here.append((source.at[:, :, own], packed.at[pairs, :, pl.ds(side * TILE, TILE)]))
            here.append((source.at[:, :, pl.ds(2 * TILE, TILE)], thirds.at[side, pairs]))
        copies.append([pltpu.make_async_copy(*ends, in_sems.at[chunk, i]) for i, ends in enumerate(here)])
    for chunk in range(3):
        for copy in copies[chunk]:
            copy.start()
    lane = lax.broadcasted_iota(jnp.int32, thirds.shape[2:], 1)
    for chunk in range(3):
        for copy in copies[chunk]:
            copy.wait()
        for pair in range(3 * chunk, 3 * chunk + 3):
            left, right = thirds[0, pair].astype(F32), thirds[1, pair].astype(F32)
            left = jnp.where(odd == 0, left, pltpu.roll(left, TILE // 2, 1))
            right = jnp.where(odd == 0, pltpu.roll(right, TILE // 2, 1), right)
            packed[pair, :, 2 * TILE :] = jnp.where(lane < TILE // 2, left, right).astype(BF)


def modulate(hidden, modulation):
    return (hidden.astype(F32) * modulation[0:1] + modulation[1:2]).astype(BF)


def head_kernel(
    parts, step_ref, hidden_hbm, mod_hbm, head_hbm, modulation_ref, send_ref, hidden_ref, mod_ref, head_ref, sems
):
    copies = [
        pltpu.make_async_copy(hidden_hbm, hidden_ref, sems.at[0]),
        pltpu.make_async_copy(mod_hbm, mod_ref, sems.at[1]),
        pltpu.make_async_copy(head_hbm, head_ref, sems.at[2]),
    ]
    for copy in copies:
        copy.start()
    for copy in copies:
        copy.wait()
    mod = mod_ref[step_ref[0]].astype(F32)
    modulation = jnp.concatenate([1.0 + mod[1:2], mod[0:1]], axis=0)
    modulation_ref[...] = modulation
    modulated = modulate(hidden_ref[...], modulation)
    terms = dot_nt(modulated, head_ref[...])
    half = terms.shape[0] // 2
    wide = jnp.concatenate([terms[:half], terms[half:]], axis=1)
    n = PAIR_COLS
    blank = jnp.zeros((n, wide.shape[1]), F32)
    lower = lax.broadcasted_iota(jnp.int32, blank.shape, 1) // (wide.shape[1] // 4) % 2 == 1

    def pair_row(i):
        return blank if i < 0 or i >= parts else wide[i * n : (i + 1) * n]

    for part in range(0, parts, 2):
        outer = jnp.where(lower, pair_row(part - 2), pair_row(part + 3))
        rows = [pair_row(part + i) for i in range(-1, 3)] + [outer]
        block = jnp.concatenate(rows, axis=0).astype(BF)
        send_ref[part] = block
        send_ref[part + 1] = block


def build_patch_weights(conv_ref, patch_w):
    channels, width = conv_ref.shape[1], conv_ref.shape[2]
    patch_w[...] = jnp.zeros_like(patch_w)
    for a in range(2):
        for b in range(3):
            for c in range(3):
                tap = conv_ref[9 * a + 3 * b + c]
                for r in range(2):
                    for s in range(2):
                        row = ((r + b) * 4 + s + c) * channels
                        col = (2 * r + s) * width
                        patch_w[a, row : row + channels, col : col + width] = tap


def weight_copies(refs, weights, sems):
    rows = refs[0].shape[1]
    return [
        pltpu.make_async_copy(ref, weights.at[:, pl.ds(i * rows, rows), :], sems.at[i]) for i, ref in enumerate(refs)
    ]


def tap_weights(refs, tap):
    pair, side = tap % 9, tap // 9
    blocks = []
    for ref in refs:
        half = ref[pair, :, 2 * TILE :]
        lane = lax.broadcasted_iota(jnp.int32, half.shape, 1)
        half = half * jnp.where((lane < TILE // 2) == (side == 0), 1.0, 0.0).astype(BF)
        blocks.append(jnp.concatenate([ref[pair, :, side * TILE : (side + 1) * TILE], half], axis=1))
    filled = sum(block.shape[0] for block in blocks)
    return jnp.concatenate(blocks + [jnp.zeros((DEEP - filled, 2 * TILE), BF)], axis=0)


def store_views(views, t, row, even, odd, odd_down, even_up):
    n, deep = PAIR_COLS, even.shape[1]
    for c, (at_even, at_odd) in enumerate(((odd_down, even), (even, odd), (odd, even_up))):
        views[t, row, 0:n, c * deep : (c + 1) * deep] = at_even
        views[t, row, n : 2 * n, c * deep : (c + 1) * deep] = at_odd


def shift_down(value):
    place = lax.broadcasted_iota(jnp.int32, value.shape, 0) % PAIR_COLS
    return jnp.where(place == 0, 0.0, pltpu.roll(value, 1, 0))


def shift_up(value):
    place = lax.broadcasted_iota(jnp.int32, value.shape, 0) % PAIR_COLS
    return jnp.where(place == PAIR_COLS - 1, 0.0, pltpu.roll(value, value.shape[0] - 1, 0))


def near_kernel(parts, blocks, info_ref, recv_ref, conv_ref, pick_ref, *refs):
    acc, far_views, slope_ref, weights, patch_w, views, sems = refs[blocks:]
    copies = weight_copies(refs[:blocks], weights, sems)
    for copy in copies:
        copy.start()
    n = PAIR_COLS
    width = conv_ref.shape[2]
    build_patch_weights(conv_ref, patch_w)

    latent = recv_ref[0].astype(F32)
    for part in range(1, parts):
        latent = latent + recv_ref[part].astype(F32)
    latent = latent.astype(BF).astype(F32)
    left, right = shift_down(latent), shift_up(latent)
    half = latent.shape[1] // 2
    stacked = []
    for t in range(LT):
        lanes = slice(t * half, (t + 1) * half)
        cols = jnp.concatenate([left[:, lanes], latent[:, lanes], right[:, lanes]], axis=1)
        above = jnp.concatenate([cols[4 * n :], cols[: 3 * n]], axis=0)
        stacked.append(jnp.concatenate([above, cols[: 4 * n], cols[n:]], axis=1))
    patches = dot(jnp.concatenate(stacked, axis=0).astype(BF), pick_ref[...]).astype(BF)

    top_scale, bottom_scale = edge_scales(parts, info_ref[0])
    group = lax.broadcasted_iota(jnp.int32, (8 * n, 1), 0) // n % 4
    scale = jnp.where(group == 0, top_scale, jnp.where(group == 3, bottom_scale, 1.0))
    for r in range(2):
        lanes = slice(2 * r * width, (2 * r + 2) * width)
        pre = dot(patches, patch_w[1, :, lanes])
        late = dot(patches[: 4 * n], patch_w[0, :, lanes])
        pre = jnp.concatenate([pre[: 4 * n], pre[4 * n :] + late], axis=0)
        gate = sigmoid(pre)
        act = pre * gate * scale
        even, odd = act[:, :width], act[:, width:]
        odd_down, even_up = shift_down(odd).astype(BF), shift_up(even).astype(BF)
        even, odd = even.astype(BF), odd.astype(BF)
        for t in range(LT):
            for g in range(4):
                at = slice((4 * t + g) * n, (4 * t + g + 1) * n)
                for target, lanes in ((views, slice(0, DEEP)), (far_views, slice(DEEP, 2 * DEEP))):
                    store_views(
                        target, t, 2 * g + r, even[at, lanes], odd[at, lanes], odd_down[at, lanes], even_up[at, lanes]
                    )
            for g in (1, 2):
                at = slice((4 * t + g) * n, (4 * t + g + 1) * n)
                own, own_gate = pre[at], gate[at]
                slope = own_gate * (1.0 + own * (1.0 - own_gate))
                base = (4 * t + 2 * (g - 1) + r) * 2 * n
                slope_ref[base : base + n, :] = slope[:, :width]
                slope_ref[base + n : base + 2 * n, :] = slope[:, width:]

    for copy in copies:
        copy.wait()
    add_taps(views, [weights], acc, None)


def edge_scales(parts, mp_index):
    place = mp_index // 2
    return jnp.where(place == 0, 0.0, 1.0).astype(F32), jnp.where(place == parts // 2 - 1, 0.0, 1.0).astype(F32)


def add_taps(views, refs, acc, base):
    half_rows = acc.shape[0] // 2
    rows = half_rows // (2 * PAIR_COLS)
    for b in range(3):
        field = views[:, b : b + rows].reshape(2 * half_rows, 3 * DEEP)
        now = dot(field, jnp.concatenate([tap_weights(refs, 9 + 3 * b + c) for c in range(3)], axis=0))
        late = dot(field[:half_rows], jnp.concatenate([tap_weights(refs, 3 * b + c) for c in range(3)], axis=0))
        so_far = acc if b else base
        if so_far is None:
            acc[:half_rows] = now[:half_rows]
            acc[half_rows:] = now[half_rows:] + late
        else:
            acc[:half_rows] = so_far[:half_rows] + now[:half_rows]
            acc[half_rows:] = so_far[half_rows:] + (now[half_rows:] + late)


def far_kernel(parts, info_ref, near_ref, views, *refs):
    sums_ref, slope_ref, acc = refs[-3:]
    add_taps(views, refs[:-3], acc, near_ref)
    n = PAIR_COLS
    top_scale, bottom_scale = edge_scales(parts, info_ref[0])
    tiles = []
    for t in range(LT):
        for row in range(6):
            part = acc[(6 * t + row) * 2 * n : (6 * t + row + 1) * 2 * n]
            half = part[:, TILE:]
            pre = jnp.concatenate([part[:, :TILE], half + pltpu.roll(half, TILE // 2, 1)], axis=1)
            gate = sigmoid(pre)
            slope = gate * (1.0 + pre * (1.0 - gate))
            if row == 0:
                slope = slope * top_scale
            elif row == 5:
                slope = slope * bottom_scale
            else:
                part_sum = jnp.sum(pre * gate, axis=0, keepdims=True)
                total = part_sum if row == 1 else total + part_sum
            slope_ref[t, row] = slope.astype(BF)
        tiles += [total[:, :TILE], total[:, TILE:]]
    sums = jnp.concatenate(tiles + [jnp.zeros((8 - len(tiles), TILE), F32)], axis=0)
    for part in range(parts):
        sums_ref[part] = sums


def three_terms(value):
    high = value.astype(BF)
    rest = value - high.astype(F32)
    middle = rest.astype(BF)
    low = (rest - middle.astype(F32)).astype(BF)
    return jnp.concatenate([high, middle, low], axis=0)


def backward_kernel(
    parts, cells, info_ref, sums_ref, patch_ref, text_ref, second_ref, slope_ref, pick_ref, patch_w, near_w, *refs
):
    far_refs = refs[:-4]
    reward_ref, send_ref, views, acc = refs[-4:]
    n = PAIR_COLS
    lane = lax.broadcasted_iota(jnp.int32, (8, TILE), 1)

    by_side = []
    for side in range(2):
        total = sums_ref[side]
        for part in range(side + 2, parts, 2):
            total = total + sums_ref[part]
        by_side.append(total)
    rows = []
    for t in range(LT):
        even, odd = [total[2 * t : 2 * t + 2] for total in by_side]
        mixed = jnp.where(lane[:1] < TILE // 2, even[1:2], odd[1:2])
        rows.append(jnp.concatenate([even[0:1], odd[0:1], mixed], axis=1))
    pooled = jnp.concatenate(rows + [jnp.zeros((8 - LT, 3 * TILE), F32)], axis=0) / cells
    products = dot(three_terms(pooled), patch_ref[...])
    embedded = products[0:8] + products[8:16] + products[16:24]
    text = text_ref[...]
    text_length = jnp.sqrt(jnp.sum(text * text, axis=1, keepdims=True) + 1e-06)
    embed_square = jnp.sum(embedded * embedded, axis=1, keepdims=True) + 1e-06
    embed_length = jnp.sqrt(embed_square)
    along = jnp.sum(embedded * text, axis=1, keepdims=True)
    cosine = along / (embed_length * text_length)
    share = 100.0 / LT
    reward_ref[0] = share * (cosine[0, 0] + cosine[1, 0])
    embed_grad = share * (text / (embed_length * text_length) - cosine * embedded / embed_square)
    products = dot_nt(three_terms(embed_grad), patch_ref[...])
    pool_grad = (products[0:8] + products[8:16] + products[16:24]) / cells

    side = info_ref[0] % 2
    third = pool_grad[:, 2 * TILE :]
    turned = pltpu.roll(third, TILE // 2, 1)
    half = jnp.where((lane < TILE // 2) == (side == 0), third, turned)
    own_grad = jnp.concatenate([jnp.where(side == 0, pool_grad[:, :TILE], pool_grad[:, TILE : 2 * TILE]), half], axis=1)

    for row in range(6):
        for t in range(LT):
            grad = second_ref[t, row].astype(F32) * own_grad[t : t + 1]
            even, odd = grad[:n], grad[n:]
            store_views(
                views, t, row, even.astype(BF), odd.astype(BF), shift_down(odd).astype(BF), shift_up(even).astype(BF)
            )

    half_rows = 8 * n
    for b in range(3):
        field = views[:, 2 - b : 6 - b].reshape(2 * half_rows, 6 * TILE)
        for blocks, lanes in (([near_w], slice(0, DEEP)), (far_refs, slice(DEEP, 2 * DEEP))):
            now = dot_nt(field, jnp.concatenate([tap_weights(blocks, 9 + 3 * b + c) for c in (2, 1, 0)], axis=1))
            early = dot_nt(
                field[half_rows:], jnp.concatenate([tap_weights(blocks, 3 * b + c) for c in (2, 1, 0)], axis=1)
            )
            if b == 0:
                acc[:half_rows, lanes] = now[:half_rows] + early
                acc[half_rows:, lanes] = now[half_rows:]
            else:
                acc[:half_rows, lanes] += now[:half_rows] + early
                acc[half_rows:, lanes] += now[half_rows:]
    grad_first = (acc[...] * slope_ref[...]).astype(BF)
    tokens = []
    for t in range(LT):
        for g in range(2):
            base = (8 * t + 4 * g) * n
            planes = [grad_first[base + i * n : base + (i + 1) * n] for i in range(4)]
            tokens.append(jnp.concatenate(planes, axis=1))
    patch_grad = dot_nt(jnp.concatenate(tokens, axis=0), patch_w[1])
    early = dot_nt(jnp.concatenate(tokens[2:], axis=0), patch_w[0])
    patch_grad = jnp.concatenate([patch_grad[: 2 * n] + early, patch_grad[2 * n :]], axis=0)
    spread_out = dot_nt(patch_grad.astype(BF), pick_ref[...])
    half = spread_out.shape[1] // 9
    blocks = [[], [], []]
    for t in range(LT):
        parts_of = []
        for g in range(2):
            rows = spread_out[(2 * t + g) * n : (2 * t + g + 1) * n]
            for pair_row in range(3):
                base = 3 * pair_row * half
                parts_of.append(
                    shift_up(rows[:, base : base + half])
                    + rows[:, base + half : base + 2 * half]
                    + shift_down(rows[:, base + 2 * half : base + 3 * half])
                )
        up, first, first_down, second_up, second, down = parts_of
        blocks[0].append(first + second_up)
        blocks[1].append(second + first_down)
        blocks[2].append(up + down)
    result = jnp.concatenate([jnp.concatenate(block, axis=1) for block in blocks], axis=0).astype(BF)
    for part in range(parts):
        send_ref[part] = result


def token_kernel(parts, recv_ref, hidden_ref, modulation_ref, tokens_ref, head_ref):
    n = PAIR_COLS
    lanes = recv_ref.shape[2]
    sums = [recv_ref[i].astype(F32) + recv_ref[i + 1].astype(F32) for i in range(0, parts, 2)]
    blank = jnp.zeros((n, lanes), F32)
    lower = lax.broadcasted_iota(jnp.int32, blank.shape, 1) // (lanes // 4) % 2 == 1
    rows = []
    for i, block in enumerate(sums):
        from_above = sums[i - 1][2 * n :] if i else blank
        from_below = sums[i + 1][2 * n :] if i + 1 < len(sums) else blank
        rows.append(block[:n] + jnp.where(lower, 0.0, from_above))
        rows.append(block[n : 2 * n] + jnp.where(lower, from_below, 0.0))
    wide = jnp.concatenate(rows, axis=0)
    tokens = jnp.concatenate([wide[:, : lanes // 2], wide[:, lanes // 2 :]], axis=0)
    flipped = jnp.transpose(tokens).astype(BF)
    tokens_ref[...] = tokens.astype(BF)
    head_ref[...] = dot(flipped, modulate(hidden_ref[...], modulation_ref[...])).astype(BF)


def hidden_kernel(tokens_ref, head_ref, modulation_ref, out_ref):
    out_ref[...] = (dot(tokens_ref[...], head_ref[...]) * modulation_ref[0:1]).astype(BF)


VMEM = pl.BlockSpec(memory_space=pltpu.VMEM)
SMEM = pl.BlockSpec(memory_space=pltpu.SMEM)
HBM = pl.BlockSpec(memory_space=pltpu.HBM)


def exchange(block, axis, flip):
    count = lax.axis_size(axis)
    return lax.ppermute(block, axis, [(i, i ^ flip) for i in range(count)])


def spread(piece):
    blocks = {0: piece}
    flip = lax.axis_size("dp") // 4
    while flip:
        for held in list(blocks):
            blocks[held ^ flip] = exchange(blocks[held], "dp", flip)
        flip //= 2
    unit, rows = 1, piece.shape[1]
    while rows * unit % 16:
        low = (lax.axis_index("dp") // unit) % 2 == 0
        merged = {}
        for held in blocks:
            if held % (2 * unit) == 0:
                mine, other = blocks[held], blocks[held ^ unit]
                merged[held] = jnp.where(
                    low, jnp.concatenate([mine, other], axis=1), jnp.concatenate([other, mine], axis=1)
                )
        blocks, unit = merged, 2 * unit
    return [blocks[held] for held in sorted(blocks)], unit


def half_sum(term):
    total, flip = term.astype(F32), 1
    while flip < lax.axis_size("dp") // 2:
        other = exchange(term, "dp", flip)
        total = total + other.astype(F32)
        term, flip = total.astype(BF), 2 * flip
    return total


def local_channels(weight, unit):
    count = lax.axis_size("dp") // unit
    place = lax.axis_index("dp") // unit
    rows = weight.shape[2] // count
    blocks = [weight[..., i * rows : (i + 1) * rows] for i in range(count)]
    flip = count // 2
    while flip:
        swap = place // flip % 2 == 1
        blocks = [jnp.where(swap, blocks[i ^ flip], blocks[i]) for i in range(count)]
        flip //= 2
    spare = jnp.zeros(weight.shape[:2] + (DEEP - weight.shape[2] // 2,), weight.dtype)
    return jnp.concatenate(blocks[: count // 2] + [spare] + blocks[count // 2 :] + [spare], axis=2)


def body(hidden, mod_table, timestep, head_weight, conv_in, conv_mid, patch_weight, text_emb):
    parts = lax.axis_size("mp")
    groups = lax.axis_size("dp")
    tokens, depth = hidden.shape
    features = head_weight.shape[1]
    channels = features // 4
    width = conv_in.shape[2]
    n = PAIR_COLS
    pair_rows = tokens // (LT * n)
    cells = float(2 * pair_rows * LW)
    mp_index = lax.axis_index("mp")

    head_rows = head_weight.T
    taps = jnp.transpose(conv_mid, (1, 0, 2))
    rows = conv_mid.shape[0]
    far = groups // 2

    packed = pl.pallas_call(
        pack_kernel,
        in_specs=[HBM],
        out_specs=VMEM,
        out_shape=jax.ShapeDtypeStruct((9, rows, width), BF),
        scratch_shapes=[pltpu.VMEM((2, 9, rows, TILE), BF), pltpu.SemaphoreType.DMA((3, 4))],
        compiler_params=params(53),
        name="pack",
    )(taps)
    distant = exchange(packed, "dp", far)
    modulation, send = pl.pallas_call(
        functools.partial(head_kernel, parts),
        in_specs=[SMEM] + [HBM] * 3,
        out_specs=[VMEM] * 2,
        out_shape=[
            jax.ShapeDtypeStruct((2, depth), F32),
            jax.ShapeDtypeStruct((parts, 5 * n, 2 * features), BF),
        ],
        scratch_shapes=[
            pltpu.VMEM((tokens, depth), BF),
            pltpu.VMEM(mod_table.shape, BF),
            pltpu.VMEM((features, depth), BF),
            pltpu.SemaphoreType.DMA((3,)),
        ],
        compiler_params=params(56),
        name="head",
    )(timestep, hidden, mod_table, head_rows)
    send, conv_in = lax.optimization_barrier((send, conv_in))
    recv = lax.all_to_all(send, "mp", 0, 0, tiled=True)
    near_blocks, unit = spread(packed)
    recv, distant = lax.optimization_barrier((recv, distant))
    far_blocks, _ = spread(distant)
    blocks = len(near_blocks)
    info = jnp.reshape(mp_index, (1,)).astype(jnp.int32)
    taps_in = local_channels(jnp.transpose(conv_in[:, 9:], (1, 0, 2)), unit)
    pick = jnp.asarray(selection(channels))

    acc_shape = jax.ShapeDtypeStruct((24 * n, 2 * TILE), F32)
    views_shape = (LT, 8, 2 * n, 3 * DEEP)
    near_acc, far_views, slope, near_w, patch_w = pl.pallas_call(
        functools.partial(near_kernel, parts, blocks),
        in_specs=[SMEM, VMEM, VMEM, VMEM] + [HBM] * blocks,
        out_specs=[VMEM] * 5,
        out_shape=[
            acc_shape,
            jax.ShapeDtypeStruct(views_shape, BF),
            jax.ShapeDtypeStruct((16 * n, 2 * DEEP), F32),
            jax.ShapeDtypeStruct((9, width // 2, width), BF),
            jax.ShapeDtypeStruct((2, 16 * channels, 8 * DEEP), BF),
        ],
        scratch_shapes=[pltpu.VMEM(views_shape, BF), pltpu.SemaphoreType.DMA((blocks,))],
        cost_estimate=pl.CostEstimate(flops=4 * 10**9, bytes_accessed=10**7, transcendentals=10**6),
        compiler_params=params(20),
        name="near",
    )(info, recv, taps_in, pick, *near_blocks)
    sums, second_slope = pl.pallas_call(
        functools.partial(far_kernel, parts),
        in_specs=[SMEM] + [VMEM] * (2 + blocks),
        out_specs=[VMEM] * 2,
        out_shape=[
            jax.ShapeDtypeStruct((parts, 8, TILE), F32),
            jax.ShapeDtypeStruct((LT, 6, 2 * n, 2 * TILE), BF),
        ],
        scratch_shapes=[pltpu.VMEM(acc_shape.shape, F32)],
        compiler_params=params(16),
        name="far",
    )(info, near_acc, far_views, *far_blocks)
    all_sums = lax.all_to_all(sums, "mp", 0, 0, tiled=True)

    reward, contribution = pl.pallas_call(
        functools.partial(backward_kernel, parts, cells),
        in_specs=[SMEM] + [VMEM] * (8 + blocks),
        out_specs=[SMEM, VMEM],
        out_shape=[
            jax.ShapeDtypeStruct((1,), F32),
            jax.ShapeDtypeStruct((parts, 3 * n, 2 * features), BF),
        ],
        scratch_shapes=[pltpu.VMEM((LT, 6, 2 * n, 6 * TILE), BF), pltpu.VMEM((16 * n, 2 * DEEP), F32)],
        compiler_params=params(16),
        name="backward",
    )(info, all_sums, patch_weight, text_emb, second_slope, slope, pick, patch_w, near_w, *far_blocks)
    contributions = lax.all_to_all(contribution, "mp", 0, 0, tiled=True)

    token_grad, head_term = pl.pallas_call(
        functools.partial(token_kernel, parts),
        in_specs=[VMEM] * 3,
        out_specs=[VMEM, VMEM],
        out_shape=[
            jax.ShapeDtypeStruct((tokens, features), BF),
            jax.ShapeDtypeStruct((features, depth), BF),
        ],
        compiler_params=params(8),
        name="token",
    )(contributions, hidden, modulation)
    from_far = exchange(head_term, "dp", far)
    hidden_grad = pl.pallas_call(
        hidden_kernel,
        in_specs=[VMEM] * 3,
        out_specs=VMEM,
        out_shape=jax.ShapeDtypeStruct((tokens, depth), BF),
        compiler_params=params(8),
        name="hidden_grad",
    )(token_grad, head_rows, modulation)
    hidden_grad, from_far = lax.optimization_barrier((hidden_grad, from_far))
    head_grad = half_sum(head_term) + half_sum(from_far)
    return (reward, head_grad.T, hidden_grad)


def solution(mesh):
    in_specs = (
        P("dp", "mp"),
        P(None, None, "mp"),
        P("dp"),
        P("mp", None),
        P(),
        P("dp", None, None),
        P(),
        P("dp", None),
    )
    out_specs = (P("dp"), P("mp", None), P("dp", "mp"))
    return jax.shard_map(body, mesh=mesh, in_specs=in_specs, out_specs=out_specs, check_vma=False)
```
